32 devices in a mesh: scene: 8 (over z, y), lat: 4 (over x, core).
Axes of the slice: x: 2, y: 2, z: 4, core: 2. Of those that a mesh axis runs over, the one named last changes fastest.
Arguments:
- rays: bfloat16 [15360, 768], P('scene'), may hold values from -6 to 6
- latents: bfloat16 [24000, 768], P(('scene', 'lat')), may hold values from -6 to 6
- view_count: int32 [8], P('scene'), may hold values from 1 to 10, as said below
- view_mask: int32 [8, 10], P('scene'), may hold values from 0 to 1, as said below
- cotangent: bfloat16 [15360, 768], P('scene'), may hold values from -6 to 6
- w_query: bfloat16 [768, 768], P(('scene', 'lat')), may hold values from -0.21875 to 0.21875
- w_key: bfloat16 [768, 768], P(('scene', 'lat')), may hold values from -0.21875 to 0.21875
- w_value: bfloat16 [768, 768], P(('scene', 'lat')), may hold values from -0.21875 to 0.21875
- w_out: bfloat16 [768, 768], P(('scene', 'lat')), may hold values from -6 to 6
- w_up: bfloat16 [768, 1536], P(('scene', 'lat')), may hold values from -0.21875 to 0.21875
- w_down: bfloat16 [1536, 768], P(('scene', 'lat')), may hold values from -0.15625 to 0.15625
- first_gain: bfloat16 [768], P(('scene', 'lat')), may hold values from 0.25 to 1.75
- first_bias: bfloat16 [768], P(('scene', 'lat')), may hold values from -3 to 3
- second_gain: bfloat16 [768], P(('scene', 'lat')), may hold values from 0.25 to 1.75
- second_bias: bfloat16 [768], P(('scene', 'lat')), may hold values from -3 to 3
- out_bias: bfloat16 [768], P(('scene', 'lat')), may hold values from -3 to 3
- up_bias: bfloat16 [1536], P(('scene', 'lat')), may hold values from -3 to 3
- down_bias: bfloat16 [768], P(('scene', 'lat')), may hold values from -3 to 3
Outputs:
- layer_out: bfloat16 [15360, 768], P('scene')
- ray_grad: bfloat16 [15360, 768], P('scene')
- latent_grad: bfloat16 [24000, 768], P(('scene', 'lat'))
- query_weight_grad: float32 [768, 768], P(('scene', 'lat'))
- key_weight_grad: float32 [768, 768], P(('scene', 'lat'))
- value_weight_grad: float32 [768, 768], P(('scene', 'lat'))
- out_weight_grad: float32 [768, 768], P(('scene', 'lat'))
- up_weight_grad: float32 [768, 1536], P(('scene', 'lat'))
- down_weight_grad: float32 [1536, 768], P(('scene', 'lat'))
- first_gain_grad: float32 [768], P(('scene', 'lat'))
- first_bias_grad: float32 [768], P(('scene', 'lat'))
- second_gain_grad: float32 [768], P(('scene', 'lat'))
- second_bias_grad: float32 [768], P(('scene', 'lat'))
- out_bias_grad: float32 [768], P(('scene', 'lat'))
- up_bias_grad: float32 [1536], P(('scene', 'lat'))
- down_bias_grad: float32 [768], P(('scene', 'lat'))
The draws below stay inside these ranges and needn't reach their ends.
Inputs may be any that keep to these rules, and one draw needn't show every extreme that they name: `view_count`: one scene has all 10 views, and another has one. `view_mask`: view slot 0 is present in every scene; the scene with 10 views has every slot present.
All inputs are finite; a program needn't handle non-finite values.
Results may differ from the reference program's by a relative error of at most 0.025.
Values may be sent and summed in bfloat16 or wider, within the bound.
No kernel may reach another device: no remote copies, remote signals or barrier semaphores. Data moves between devices by JAX's collectives and lax.ppermute only.
A program may use at most 256 MiB of HBM per device.

```python
import jax
import jax.numpy as jnp
from jax import lax

D = 768
HEADS = 12
HEAD_DIM = 64
FF = 1536
RAYS = 1920
VIEWS = 10
VIEW_TOK = 300
SCENES = 8
LATENTS = 3000


def pick_scene(key):
    return jax.random.randint(jax.random.fold_in(key, 11), (), 0, SCENES)


def draw_view_count(key, part):
    chosen = pick_scene(key)
    key = jax.random.fold_in(key, 1)
    counted = jax.random.randint(key, (SCENES,), 1, VIEWS + 1)
    scene_ids = jnp.arange(SCENES)
    counted = jnp.where(scene_ids == (chosen + 1) % SCENES, 1, counted)
    counted = jnp.where(scene_ids == chosen, VIEWS, counted)
    return counted.astype(jnp.int32)


def draw_view_mask(key, part):
    chosen = pick_scene(key)
    key = jax.random.fold_in(key, 2)
    levels = jax.random.randint(key, (SCENES, VIEWS), 0, 4)
    present = (levels > 0) | (jnp.arange(VIEWS)[None, :] == 0) | (jnp.arange(SCENES)[:, None] == chosen)
    return present.astype(jnp.int32)


def with_spikes(values, own_key, source, target, blocks, factor):
    owner, partner = [(jnp.arange(values.shape[axis_at]) // (values.shape[axis_at] // blocks)).reshape([-1 if axis == axis_at else 1 for axis in range(values.ndim)]) for axis_at in (source, target)]
    chosen = jax.random.permutation(own_key, blocks)[partner]
    strong = (owner == chosen) | (owner == (partner + blocks // 2) % blocks)
    return jnp.where(strong, factor * values, values)


def block_scale(key, shape, cuts, smallest, top_value):
    def one(axis_at, parts):
        steps = jax.random.uniform(jax.random.fold_in(jax.random.fold_in(key, 6), axis_at), (parts,), jnp.float32, smallest / len(cuts), top_value / len(cuts))
        return jnp.repeat(jnp.exp(steps), shape[axis_at] // parts).reshape((-1,) + (1,) * (len(shape) - axis_at - 1))

    level = one(*cuts[0])
    for cut in cuts[1:]:
        level = level * one(*cut)
    return level


def bell_draw(stream_key, extent, width, limit, shards=(), held_as=jnp.bfloat16):
    array = width * jax.random.normal(stream_key, extent, jnp.float32)
    if shards:
        array = array * block_scale(stream_key, extent, shards, -0.22, 0.18)
    return jnp.clip(array, -limit, limit).astype(held_as)


def gaussian_with(stream_key, extent, scale, bound, shards, heavy, kind=jnp.bfloat16):
    values = scale * jax.random.normal(stream_key, extent, jnp.float32)
    if shards:
        values = values * block_scale(stream_key, extent, shards, -0.22, 0.18)
    return jnp.clip(with_spikes(values, jax.random.fold_in(stream_key, 3), *heavy), -bound, bound).astype(kind)


def setup_inputs(seed: int = 0) -> dict:
    splits = jax.random.split(jax.random.key(seed), 19)
    rays = gaussian_with(splits[0], (SCENES * RAYS, D), 1.0, 6.0, ((0, 8),), (0, 1, 8, 2.0))
    latents = bell_draw(splits[1], (SCENES * LATENTS, D), 1.0, 6.0, ((0, 32),))
    view_count = draw_view_count(jax.random.fold_in(splits[18], 71), 0)
    view_mask = draw_view_mask(jax.random.fold_in(splits[18], 71), 0)
    cotangent = bell_draw(splits[4], (SCENES * RAYS, D), 1.0, 6.0, ((0, 8),))
    w_query = bell_draw(splits[5], (D, D), D ** -0.5, 0.21875, ((0, 32),))
    w_key = bell_draw(splits[6], (D, D), D ** -0.5, 0.21875, ((0, 32),))
    w_value = bell_draw(splits[7], (D, D), D ** -0.5, 0.21875, ((0, 32),))
    w_out = bell_draw(splits[8], (D, D), (D // (2 * VIEW_TOK)) ** -0.5, 6.0, ((0, 32),))
    w_up = bell_draw(splits[9], (D, FF), D ** -0.5, 0.21875, ((0, 32),))
    w_down = bell_draw(splits[10], (FF, D), FF ** -0.5, 0.15625, ((0, 32),))
    first_gain = jnp.clip(1.0 + 0.15 * jax.random.normal(splits[11], (D,), jnp.float32), 0.25, 1.75).astype(jnp.bfloat16)
    first_bias = bell_draw(splits[12], (D,), 0.5, 3.0, ((0, 32),))
    second_gain = jnp.clip(1.0 + 0.15 * jax.random.normal(splits[13], (D,), jnp.float32), 0.25, 1.75).astype(jnp.bfloat16)
    second_bias = bell_draw(splits[14], (D,), 0.5, 3.0, ((0, 32),))
    out_bias = bell_draw(splits[15], (D,), 0.5, 3.0, ((0, 32),))
    up_bias = bell_draw(splits[16], (FF,), 0.5, 3.0, ((0, 32),))
    down_bias = bell_draw(splits[17], (D,), 0.5, 3.0, ((0, 32),))
    return {"rays": rays, "latents": latents, "view_count": view_count, "view_mask": view_mask, "cotangent": cotangent, "w_query": w_query, "w_key": w_key, "w_value": w_value, "w_out": w_out, "w_up": w_up, "w_down": w_down, "first_gain": first_gain, "first_bias": first_bias, "second_gain": second_gain, "second_bias": second_bias, "out_bias": out_bias, "up_bias": up_bias, "down_bias": down_bias}


@jax.custom_vjp
def low(v):
    return lax.optimization_barrier(v.astype(jnp.bfloat16)).astype(jnp.float32)

@jax.custom_vjp
def low_back(v):
    return v

def low_keep(v):
    return (low(v), None)

def low_pass(kept, grad):
    return (grad,)

def back_keep(v):
    return (v, None)

def back_low(kept, grad):
    return (low(grad),)
low.defvjp(low_keep, low_pass)
low_back.defvjp(back_keep, back_low)

def matmul(left_side, right_side):
    return jnp.dot(left_side, right_side, precision=lax.Precision.HIGHEST)

def layer_norm(values, gain_vec, offset):
    center = values - lax.optimization_barrier(jnp.mean(values, axis=-1, keepdims=True))
    spread = lax.optimization_barrier(jnp.mean(center * center, axis=-1, keepdims=True))
    return center * lax.rsqrt(spread + 1e-05) * gain_vec + offset

def scene_layer(params, ray_feats, lat_feats, live_keys):
    w_query, w_key, w_value, w_out, w_up, w_down, first_gain, first_bias, second_gain, second_bias, out_bias, up_bias, down_bias = params
    normed = low(layer_norm(ray_feats, first_gain, first_bias))
    queries = low(low_back(matmul(normed, w_query))).reshape(RAYS, HEADS, HEAD_DIM)
    keyset = low(low_back(matmul(lat_feats, w_key))).reshape(LATENTS, HEADS, HEAD_DIM)
    valset = low(low_back(matmul(lat_feats, w_value))).reshape(LATENTS, HEADS, HEAD_DIM)
    scores = low_back(jnp.einsum('rhd,khd->hrk', queries, keyset, precision=lax.Precision.HIGHEST) * 0.125)
    scores = jnp.where(live_keys[None, None, :], scores, -1e+30)
    highest = lax.optimization_barrier(jnp.max(scores, axis=-1, keepdims=True))
    weights_raw = jnp.exp(scores - highest)
    totals = lax.optimization_barrier(jnp.sum(weights_raw, axis=-1, keepdims=True))
    mixed_rows = jnp.einsum('hrk,khd->rhd', low(weights_raw), valset, precision=lax.Precision.HIGHEST)
    mixed_rows = mixed_rows / jnp.transpose(totals, (1, 0, 2))
    context = low(low_back(mixed_rows.reshape(RAYS, D)))
    middle = ray_feats + low_back(matmul(context, w_out) + out_bias)
    normed2 = low(layer_norm(middle, second_gain, second_bias))
    before = low_back(matmul(normed2, w_up) + up_bias)
    active = low(jax.nn.gelu(before, approximate=True))
    return middle + matmul(active, w_down) + down_bias

def reference(rays, latents, view_count, view_mask, cotangent, w_query, w_key, w_value, w_out, w_up, w_down, first_gain, first_bias, second_gain, second_bias, out_bias, up_bias, down_bias):
    view_of = jnp.arange(LATENTS, dtype=jnp.int32) // VIEW_TOK
    listed = jnp.take(view_mask, view_of, axis=1) > 0
    live_keys = listed & (view_of[None, :] < view_count[:, None])
    params = tuple((member.astype(jnp.float32) for member in (w_query, w_key, w_value, w_out, w_up, w_down, first_gain, first_bias, second_gain, second_bias, out_bias, up_bias, down_bias)))
    ray_feats = rays.astype(jnp.float32).reshape(SCENES, RAYS, D)
    lat_feats = latents.astype(jnp.float32).reshape(SCENES, LATENTS, D)
    checked = jax.checkpoint(scene_layer)

    def forward(params, ray_feats, lat_feats):
        return lax.map(lambda entries: checked(params, entries[0], entries[1], entries[2]), (ray_feats, lat_feats, live_keys))
    outputs, pullback = jax.vjp(forward, params, ray_feats, lat_feats)
    param_grads, ray_grads, lat_grads = pullback(cotangent.astype(jnp.float32).reshape(SCENES, RAYS, D))
    return (outputs.reshape(SCENES * RAYS, D).astype(jnp.bfloat16), ray_grads.reshape(SCENES * RAYS, D).astype(jnp.bfloat16), lat_grads.reshape(SCENES * LATENTS, D).astype(jnp.bfloat16), param_grads[0].astype(jnp.float32), param_grads[1].astype(jnp.float32), param_grads[2].astype(jnp.float32), param_grads[3].astype(jnp.float32), param_grads[4].astype(jnp.float32), param_grads[5].astype(jnp.float32), param_grads[6].astype(jnp.float32), param_grads[7].astype(jnp.float32), param_grads[8].astype(jnp.float32), param_grads[9].astype(jnp.float32), param_grads[10].astype(jnp.float32), param_grads[11].astype(jnp.float32), param_grads[12].astype(jnp.float32))
```

```python
import math
from functools import partial

import jax
import jax.numpy as jnp
from jax import lax
from jax.experimental import pallas as pl
from jax.experimental.pallas import tpu as pltpu
from jax.sharding import PartitionSpec as P

HEADS = 12
HEAD_DIM = 64
VIEWS = 10
VIEW_TOK = 300
LANES = 128
LATS = 4
OWN_HEADS = HEADS // LATS
OWN = OWN_HEADS * HEAD_DIM
DEAD = -1e30
LOG2E = math.log2(math.e)
Q_SCALE = 0.125 * LOG2E
ROOT = math.sqrt(2.0 / math.pi)
VMEM_BYTES = 56 * 2**20
BF = jnp.bfloat16
F32 = jnp.float32


def dot(left, right):
    return jnp.dot(left, right, preferred_element_type=F32)


def dot_rt(left, right):
    return lax.dot_general(left, right, (((1,), (1,)), ((), ())), preferred_element_type=F32)


def dot_lt(left, right):
    return lax.dot_general(left, right, (((0,), (0,)), ((), ())), preferred_element_type=F32)


def params(*semantics):
    return pltpu.CompilerParams(vmem_limit_bytes=VMEM_BYTES)


def shape(dims, dtype=BF):
    return jax.ShapeDtypeStruct(tuple(dims), dtype)


def norm_parts(values):
    center = values - jnp.mean(values, axis=-1, keepdims=True)
    spread = jnp.mean(center * center, axis=-1, keepdims=True)
    factor = lax.rsqrt(spread + 1e-05)
    return center * factor, factor


def norm_back(grad_out, normed, factor, gain_row):
    scaled = grad_out * gain_row
    return factor * (
        scaled
        - jnp.mean(scaled, axis=-1, keepdims=True)
        - normed * jnp.mean(scaled * normed, axis=-1, keepdims=True)
    )


def swap(values, axis, step):
    count = lax.axis_size(axis)
    return lax.ppermute(values, axis, [(i, i ^ step) for i in range(count)])


def stages(count):
    found, stride = [], count
    while stride > 1:
        group = 4 if stride % 4 == 0 else 2
        stride //= group
        found.append((stride, group))
    return found


def untangle(blocks, digit):
    count = blocks.shape[0]
    bit = 1
    while bit < count:
        paired = blocks.reshape((count // (2 * bit), 2, bit) + blocks.shape[1:])
        flipped = jnp.flip(paired, axis=1).reshape(blocks.shape)
        blocks = jnp.where((digit & bit) > 0, flipped, blocks)
        bit *= 2
    return blocks


def gather_scene(block):
    count = lax.axis_size("scene")
    me = lax.axis_index("scene")
    parts = block[None]
    for stride, group in stages(count):
        got = [parts] + [swap(parts, "scene", k * stride) for k in range(1, group)]
        digit = (me // stride) % group
        stacked = untangle(jnp.stack(got), digit)
        parts = jnp.swapaxes(stacked, 0, 1)
        parts = parts.reshape((-1,) + block.shape)
    return parts


def scatter_scene(blocks):
    count = lax.axis_size("scene")
    me = lax.axis_index("scene")
    held = blocks
    for stride, group in reversed(stages(count)):
        digit = (me // stride) % group
        view = held.reshape((-1, group) + blocks.shape[1:])
        total = lax.dynamic_index_in_dim(view, digit, 1, keepdims=False).astype(F32)
        for k in range(1, group):
            mine = lax.dynamic_index_in_dim(view, digit ^ k, 1, keepdims=False)
            total = total + swap(mine.astype(BF), "scene", k * stride).astype(F32)
        held = total.astype(BF)
    return total.reshape(blocks.shape[1:])


def pad_heads(weight):
    gap = jnp.zeros((weight.shape[0], LANES - HEAD_DIM), weight.dtype)
    pieces = []
    for h in range(OWN_HEADS):
        pieces += [weight[:, h * HEAD_DIM : (h + 1) * HEAD_DIM], gap]
    return jnp.concatenate(pieces, axis=1)


def query_kernel(where, rays, weight, gain, bias, lifted, query, query_t, wide):
    @pl.when(pl.program_id(0) == 0)
    def _():
        wide[...] = pad_heads(weight[...])

    normed, _ = norm_parts(rays[...].astype(F32))
    low = (normed * gain[...] + bias[...]).astype(BF)
    lifted[...] = low
    values = dot(low, wide[...]) * Q_SCALE
    lane = lax.broadcasted_iota(jnp.int32, (1, LANES), 1)
    for h in range(OWN_HEADS):
        one = values[:, h * LANES : (h + 1) * LANES]
        query[h] = jnp.where(lane == HEAD_DIM, 1.0, one).astype(BF)
        query_t[h, 0] = one.T[:HEAD_DIM].astype(BF)


def make_queries(where, rays, weight, gain, bias):
    count, width = rays.shape
    half = count // 2
    whole = lambda a: pl.BlockSpec(a.shape, lambda i, w: (0,) * a.ndim)
    return pl.pallas_call(
        query_kernel,
        grid_spec=pltpu.PrefetchScalarGridSpec(
            num_scalar_prefetch=1,
            grid=(2,),
            in_specs=[
                pl.BlockSpec((half, width), lambda i, w: (w[1] ^ i, 0)),
                whole(weight),
                whole(gain),
                whole(bias),
            ],
            out_specs=[
                pl.BlockSpec((half, width), lambda i, w: (i, 0)),
                pl.BlockSpec((OWN_HEADS, half, LANES), lambda i, w: (0, i, 0)),
                pl.BlockSpec((OWN_HEADS, 1, HEAD_DIM, half), lambda i, w: (0, i, 0, 0)),
            ],
            scratch_shapes=[pltpu.VMEM((width, OWN_HEADS * LANES), BF)],
        ),
        out_shape=[
            shape((count, width)),
            shape((OWN_HEADS, count, LANES)),
            shape((OWN_HEADS, 2, HEAD_DIM, half)),
        ],
        compiler_params=params(),
        name="queries",
    )(where, rays, weight, gain, bias)


def keyset_kernel(lat0, lat1, lat2, lat3, w_key, w_value, shut, key, key_t, val, val_t):
    wide_key, wide_value = pad_heads(w_key[...]), pad_heads(w_value[...])
    rows = lat0.shape[0]
    lane = lax.broadcasted_iota(jnp.int32, (1, LANES), 1)
    line = lax.broadcasted_iota(jnp.int32, (LANES, 1), 0)
    extra = (lane == HEAD_DIM) | (lane == HEAD_DIM + 1)
    for j, lat in enumerate((lat0, lat1, lat2, lat3)):
        at = pl.ds(j * rows, rows)
        keys = dot(lat[...], wide_key)
        vals = dot(lat[...], wide_value)
        for h in range(OWN_HEADS):
            one = keys[:, h * LANES : (h + 1) * LANES]
            key[h, at, :] = one.astype(BF)
            key_t[h, :, at] = jnp.where(line == HEAD_DIM, shut[j], one.T).astype(BF)
            one = jnp.where(extra, 1.0, vals[:, h * LANES : (h + 1) * LANES])
            val[h, at, :] = one.astype(BF)
            val_t[h, :, at] = one.T.astype(BF)


def make_keyset(lats, w_key, w_value, shut):
    total = LATS * lats[0].shape[0]
    tall, wide = shape((OWN_HEADS, total, LANES)), shape((OWN_HEADS, LANES, total))
    return pl.pallas_call(
        keyset_kernel,
        out_shape=[tall, wide, tall, wide],
        in_specs=[pl.BlockSpec(memory_space=pltpu.VMEM)] * 7,
        out_specs=[pl.BlockSpec(memory_space=pltpu.VMEM)] * 4,
        compiler_params=params(),
        name="keyset",
    )(*lats, w_key, w_value, shut)


def attend_kernel(sub, query, key_t, val, *rest):
    context, weights, inverse = rest[-3:]
    head = pl.program_id(0)
    rows = query.shape[1]

    def score(i):
        return dot(query[0, i * sub : (i + 1) * sub, :], key_t[0])

    scores = score(0)
    for i in range(rows // sub):
        later = score(i + 1) if i + 1 < rows // sub else None
        at = slice(i * sub, (i + 1) * sub)
        low = jnp.exp2(scores - jnp.max(scores, axis=1, keepdims=True)).astype(BF)
        weights[0, at, :] = low
        summed = dot(low, val[0])
        scale = 1.0 / summed[:, HEAD_DIM : HEAD_DIM + 1]
        mixed = (summed[:, :HEAD_DIM] * scale).astype(BF)
        inverse[0, at, :] = jnp.broadcast_to(scale, (sub, LANES))
        for h in range(OWN_HEADS):

            @pl.when(head == h)
            def _():
                context[at, h * HEAD_DIM : (h + 1) * HEAD_DIM] = mixed

        scores = later


def attend(half_index, query, key_t, val, held=None):
    _, count, _ = query.shape
    total = key_t.shape[2]
    half = count // 2
    sub = half // 6 if half % 96 == 0 else half
    block = lambda rows, cols: pl.BlockSpec((1, rows, cols), lambda h: (h, half_index, 0))
    every = lambda rows, cols: pl.BlockSpec((1, rows, cols), lambda h: (h, 0, 0))
    extra = [] if held is None else list(held)
    return pl.pallas_call(
        partial(attend_kernel, sub),
        grid=(OWN_HEADS,),
        in_specs=[block(half, LANES), every(LANES, total), every(total, LANES)]
        + [pl.BlockSpec(memory_space=pl.ANY)] * len(extra),
        out_specs=[
            pl.BlockSpec((half, OWN), lambda h: (0, 0)),
            block(half, total),
            block(half, LANES),
        ],
        out_shape=[
            shape((half, OWN)),
            shape((OWN_HEADS, count, total)),
            shape((OWN_HEADS, count, LANES), F32),
        ],
        input_output_aliases={3: 1, 4: 2} if extra else {},
        compiler_params=params(),
        name="attend",
    )(query, key_t, val, *extra)


def feed_kernel(
    where,
    rays,
    ctx0,
    ctx1,
    ctx2,
    ctx3,
    upstream,
    w_out,
    w_up,
    w_down,
    rows_in,
    up_shift,
    layer_out,
    d_middle,
    d_branch,
    d_own,
    d_sibling,
    lifted,
    d_before,
    active,
    sums,
    up_sums,
):
    step = pl.program_id(0)
    lat = where[0]
    out_shift, down_shift, gain, bias = (rows_in[i : i + 1, :] for i in range(4))
    middle = rays[...].astype(F32) + out_shift
    for j, ctx in enumerate((ctx0, ctx1, ctx2, ctx3)):
        at = pl.ds(pl.multiple_of((lat ^ j) * OWN, OWN), OWN)
        middle = middle + dot(ctx[...], w_out[at, :])
    normed, factor = norm_parts(middle)
    low = (normed * gain + bias).astype(BF)
    lifted[...] = low
    before = dot(low, w_up[...]) + up_shift[...]
    squared = before * before
    bent = jnp.tanh(ROOT * before * (1.0 + 0.044715 * squared))
    act = (0.5 * before * (1.0 + bent)).astype(BF)
    active[...] = act
    layer_out[...] = (middle + dot(act, w_down[...]) + down_shift).astype(BF)
    slope = 0.5 * (1.0 + bent) + (0.5 * ROOT) * before * (1.0 - bent * bent) * (
        1.0 + 3 * 0.044715 * squared
    )
    d_act = dot_rt(upstream[...], w_down[...])
    d_pre = (d_act * slope).astype(BF)
    d_before[...] = d_pre
    d_lifted = dot_rt(d_pre, w_up[...])
    up_wide = upstream[...].astype(F32)
    d_mid = up_wide + norm_back(d_lifted, normed, factor, gain)
    d_middle[...] = d_mid
    branch = d_mid.astype(BF)
    d_branch[...] = branch
    for j, target in enumerate((d_own, d_sibling)):
        at = pl.ds(pl.multiple_of((lat ^ j) * OWN, OWN), OWN)
        target[...] = dot_rt(branch, w_out[at, :]).astype(BF)
    column = lambda v: jnp.sum(v, axis=0, keepdims=True)
    pieces = (
        column(d_lifted * normed),
        column(d_lifted),
        column(branch.astype(F32)),
        column(up_wide),
    )
    up_piece = column(d_pre.astype(F32))

    @pl.when(step == 0)
    def _():
        sums[...] = jnp.zeros_like(sums)
        up_sums[...] = jnp.zeros_like(up_sums)

    for i, piece in enumerate(pieces):
        sums[i : i + 1, :] += piece
    up_sums[0:1, :] += up_piece


def feed(where, rays, ctxs, upstream, w_out, w_up, w_down, rows_in, up_shift):
    count, width = rays.shape
    hidden = w_up.shape[1]
    half = count // 2
    block = half // 4 if half % 64 == 0 else half
    steps = half // block
    whole = lambda a: pl.BlockSpec(a.shape, lambda i, w: (0,) * a.ndim)
    mine = pl.BlockSpec((block, width), lambda i, w: (w[1] * steps + i, 0))
    local = lambda cols: pl.BlockSpec((block, cols), lambda i, w: (i, 0))
    return pl.pallas_call(
        feed_kernel,
        grid_spec=pltpu.PrefetchScalarGridSpec(
            num_scalar_prefetch=1,
            grid=(steps,),
            in_specs=[mine]
            + [local(OWN)] * LATS
            + [mine, whole(w_out), whole(w_up), whole(w_down), whole(rows_in), whole(up_shift)],
            out_specs=[
                local(width),
                local(width),
                local(width),
                local(OWN),
                local(OWN),
                local(width),
                local(hidden),
                local(hidden),
                pl.BlockSpec((8, width), lambda i, w: (0, 0)),
                pl.BlockSpec((8, hidden), lambda i, w: (0, 0)),
            ],
        ),
        out_shape=[
            shape((half, width)),
            shape((half, width), F32),
            shape((half, width)),
            shape((half, OWN)),
            shape((half, OWN)),
            shape((half, width)),
            shape((half, hidden)),
            shape((half, hidden)),
            shape((8, width), F32),
            shape((8, hidden), F32),
        ],
        compiler_params=params(),
        name="feed",
    )(where, rays, *ctxs, upstream, w_out, w_up, w_down, rows_in, up_shift)


def split_columns(values, core, own, sibling):
    mid = values.shape[1] // 2
    low, high = values[:, :mid], values[:, mid:]
    own_part = jnp.where(core == 0, low, high)
    other = jnp.where(core == 0, high, low)
    own[...] = own_part.astype(own.dtype)
    sibling[...] = other.astype(sibling.dtype)


def feed_grads_kernel(
    where,
    ctx0,
    ctx1,
    ctx2,
    ctx3,
    d_branch,
    lifted,
    d_before,
    active,
    upstream,
    out_own,
    out_sib,
    up_own,
    up_sib,
    down_own,
    down_sib,
):
    lat, core = where[0], where[1]
    for j, ctx in enumerate((ctx0, ctx1, ctx2, ctx3)):
        at = pl.ds(pl.multiple_of((lat ^ j) * OWN, OWN), OWN)
        split_columns(dot_lt(ctx[...], d_branch[...]), core, out_own.at[at, :], out_sib.at[at, :])
    split_columns(dot_lt(lifted[...], d_before[...]), core, up_own, up_sib)
    split_columns(dot_lt(active[...], upstream[...]), core, down_own, down_sib)


def feed_grads(where, ctxs, d_branch, lifted, d_before, active, upstream):
    half, width = d_branch.shape
    hidden = active.shape[1]
    whole = lambda a: pl.BlockSpec(a.shape, lambda i, w: (0,) * a.ndim)
    columns = lambda a: pl.BlockSpec((half, a.shape[1] // 2), lambda i, w: (0, w[2]))
    outs = [(width, width // 4), (width, hidden // 4), (hidden, width // 4)]
    dims = [d for d in outs for _ in range(2)]
    return pl.pallas_call(
        feed_grads_kernel,
        grid_spec=pltpu.PrefetchScalarGridSpec(
            num_scalar_prefetch=1,
            grid=(1,),
            in_specs=[whole(c) for c in ctxs]
            + [
                columns(d_branch),
                whole(lifted),
                columns(d_before),
                whole(active),
                pl.BlockSpec((half, width // 2), lambda i, w: (w[1], w[2])),
            ],
            out_specs=[pl.BlockSpec(d, lambda i, w: (0, 0)) for d in dims],
        ),
        out_shape=[shape(d, BF) for d in dims],
        compiler_params=params(),
        name="feed_grads",
    )(where, *ctxs, d_branch, lifted, d_before, active, upstream)


def prepare_kernel(d_here, d_there, ctx_here, ctx_there, inverse, grad, grad_t):
    lane = lax.broadcasted_iota(jnp.int32, (1, LANES), 1)
    half = d_here.shape[0]
    gap = jnp.zeros((half, LANES - HEAD_DIM), F32)
    for i, (d_ctx, ctx) in enumerate(((d_here, ctx_here), (d_there, ctx_there))):
        at = slice(i * half, (i + 1) * half)
        upstream = d_ctx[...].astype(F32)
        product = upstream * ctx[...].astype(F32)
        for h in range(OWN_HEADS):
            cols = slice(h * HEAD_DIM, (h + 1) * HEAD_DIM)
            scale = inverse[h, at, :]
            delta = jnp.sum(product[:, cols], axis=1, keepdims=True) * scale
            high = delta.astype(BF).astype(F32)
            wide = jnp.concatenate([upstream[:, cols], gap], axis=1) * scale
            grad_t[h, i] = wide.T[:HEAD_DIM].astype(BF)
            wide = jnp.where(lane == HEAD_DIM, -high, wide)
            wide = jnp.where(lane == HEAD_DIM + 1, high - delta, wide)
            grad[h, at, :] = wide.astype(BF)


def prepare(d_here, d_there, ctx_here, ctx_there, inverse):
    half = d_here.shape[0]
    return pl.pallas_call(
        prepare_kernel,
        out_shape=[shape((OWN_HEADS, 2 * half, LANES)), shape((OWN_HEADS, 2, HEAD_DIM, half))],
        in_specs=[pl.BlockSpec(memory_space=pltpu.VMEM)] * 5,
        out_specs=[pl.BlockSpec(memory_space=pltpu.VMEM)] * 2,
        compiler_params=params(),
        name="prepare",
    )(d_here, d_there, ctx_here, ctx_there, inverse)


def back_kernel(sub, weights, grad, grad_t, query_t, key, val_t, d_query, d_key, d_val, sums):
    step, last = pl.program_id(1), pl.num_programs(1) - 1
    rows = weights.shape[1]
    found = []
    for i in range(rows // sub):
        at = slice(i * sub, (i + 1) * sub)
        d_weights = dot(grad[0, at, :], val_t[0])
        d_scores = (weights[0, at, :].astype(F32) * d_weights).astype(BF)
        d_query[0, at, :] = (dot(d_scores, key[0]) * 0.125).astype(BF)
        found.append(d_scores)
    d_scores = jnp.concatenate(found, axis=0) if len(found) > 1 else found[0]
    val_part = dot(grad_t[0, 0], weights[0])
    key_part = dot(query_t[0, 0], d_scores) * (1.0 / LOG2E)

    @pl.when(step == 0)
    def _():
        sums[0] = key_part
        sums[1] = val_part

    @pl.when(step == last)
    def _():
        d_key[0] = (sums[0] + key_part).astype(BF)
        d_val[0] = (sums[1] + val_part).astype(BF)


def attend_back(weights, grad, grad_t, query_t, key, val_t):
    _, count, total = weights.shape
    half = count // 2
    sub = half // 4 if half % 64 == 0 else half
    rows = lambda cols: pl.BlockSpec((1, half, cols), lambda h, b: (h, b, 0))
    turned = pl.BlockSpec((1, 1, HEAD_DIM, half), lambda h, b: (h, b, 0, 0))
    return pl.pallas_call(
        partial(back_kernel, sub),
        grid=(OWN_HEADS, 2),
        in_specs=[
            rows(total),
            rows(LANES),
            turned,
            turned,
            pl.BlockSpec((1, total, LANES), lambda h, b: (h, 0, 0)),
            pl.BlockSpec((1, LANES, total), lambda h, b: (h, 0, 0)),
        ],
        out_specs=[
            rows(LANES),
            pl.BlockSpec((1, HEAD_DIM, total), lambda h, b: (h, 0, 0)),
            pl.BlockSpec((1, HEAD_DIM, total), lambda h, b: (h, 0, 0)),
        ],
        out_shape=[
            shape((OWN_HEADS, count, LANES)),
            shape((OWN_HEADS, HEAD_DIM, total)),
            shape((OWN_HEADS, HEAD_DIM, total)),
        ],
        scratch_shapes=[pltpu.VMEM((2, HEAD_DIM, total), F32)],
        compiler_params=params(),
        name="attend_back",
    )(weights, grad, grad_t, query_t, key, val_t)


def first_grads_kernel(where, rays, dq0, dq1, dq2, dq3, w_query_t, gain, d_middle, ray_grad, sums):
    step = pl.program_id(0)
    lat = where[0]
    d_lifted = None
    for j, d_query in enumerate((dq0, dq1, dq2, dq3)):
        at = pl.ds(pl.multiple_of((lat ^ j) * OWN, OWN), OWN)
        part = dot(d_query[...], w_query_t[at, :])
        d_lifted = part if d_lifted is None else d_lifted + part
    normed, factor = norm_parts(rays[...].astype(F32))
    ray_grad[...] = (d_middle[...] + norm_back(d_lifted, normed, factor, gain[...])).astype(BF)

    @pl.when(step == 0)
    def _():
        sums[...] = jnp.zeros_like(sums)

    sums[0:1, :] += jnp.sum(d_lifted * normed, axis=0, keepdims=True)
    sums[1:2, :] += jnp.sum(d_lifted, axis=0, keepdims=True)


def first_grads(where, rays, d_queries, w_query_t, gain, d_middle):
    count, width = rays.shape
    half = count // 2
    block = half // 4 if half % 64 == 0 else half
    steps = half // block
    whole = lambda a: pl.BlockSpec(a.shape, lambda i, w: (0,) * a.ndim)
    local = lambda cols: pl.BlockSpec((block, cols), lambda i, w: (i, 0))
    return pl.pallas_call(
        first_grads_kernel,
        grid_spec=pltpu.PrefetchScalarGridSpec(
            num_scalar_prefetch=1,
            grid=(steps,),
            in_specs=[pl.BlockSpec((block, width), lambda i, w: (w[1] * steps + i, 0))]
            + [local(OWN)] * LATS
            + [whole(w_query_t), whole(gain), local(width)],
            out_specs=[local(width), pl.BlockSpec((8, width), lambda i, w: (0, 0))],
        ),
        out_shape=[shape((half, width)), shape((8, width), F32)],
        compiler_params=params(),
        name="first_grads",
    )(where, rays, *d_queries, w_query_t, gain, d_middle)


def projection_grads_kernel(lifted, d_here, d_there, lat0, lat1, lat2, lat3, d_key, d_val, out):
    half = d_here.shape[0]
    out[0] = dot_lt(d_here[...], lifted[:half]).T.astype(BF)
    out[0] += dot_lt(d_there[...], lifted[half:]).T.astype(BF)
    rows = lat0.shape[0]
    for i, grads in enumerate((d_key, d_val)):
        total = None
        for j, lat in enumerate((lat0, lat1, lat2, lat3)):
            part = dot(grads[:, j * rows : (j + 1) * rows], lat[...])
            total = part if total is None else total + part
        out[1 + i] = total.T.astype(BF)


def projection_grads(lifted, d_here, d_there, lats, d_key, d_val):
    return pl.pallas_call(
        projection_grads_kernel,
        out_shape=shape((3, lifted.shape[1], OWN)),
        in_specs=[pl.BlockSpec(memory_space=pltpu.VMEM)] * 9,
        out_specs=pl.BlockSpec(memory_space=pltpu.VMEM),
        compiler_params=params(),
        name="projection_grads",
    )(lifted, d_here, d_there, *lats, d_key, d_val)


def latent_kernel(where, got0, got1, got2, got3, w_key_t, w_value_t, out):
    lat = where[0]
    total = None
    for j, got in enumerate((got0, got1, got2, got3)):
        at = pl.ds(pl.multiple_of((lat ^ j) * OWN, OWN), OWN)
        for i, weight in enumerate((w_key_t, w_value_t)):
            part = dot_lt(got[i], weight[at, :])
            total = part if total is None else total + part
    out[...] = total[: out.shape[0]].astype(BF)


def latent_grads(where, got, w_key_t, w_value_t, rows):
    return pl.pallas_call(
        latent_kernel,
        out_shape=shape((rows, w_key_t.shape[1])),
        in_specs=[pl.BlockSpec(memory_space=pltpu.SMEM)]
        + [pl.BlockSpec(memory_space=pltpu.VMEM)] * 6,
        out_specs=pl.BlockSpec(memory_space=pltpu.VMEM),
        compiler_params=params(),
        name="latent_grads",
    )(where, *got, w_key_t, w_value_t)


def both_halves(core, here, there):
    first = jnp.where(core == 0, here, there)
    second = jnp.where(core == 0, there, here)
    return jnp.concatenate([first, second], axis=0)


def body(
    rays,
    latents,
    view_count,
    view_mask,
    cotangent,
    w_query,
    w_key,
    w_value,
    w_out,
    w_up,
    w_down,
    first_gain,
    first_bias,
    second_gain,
    second_bias,
    out_bias,
    up_bias,
    down_bias,
):
    scenes = lax.axis_size("scene")
    lat = lax.axis_index("lat")
    core, side = lat % 2, lat // 2
    where = jnp.stack([lat, core, side]).astype(jnp.int32)
    count, width = rays.shape
    hidden = w_up.shape[1]
    half = count // 2
    lat_rows = latents.shape[0]
    lat_pad = -(-lat_rows // LANES) * LANES
    shard = w_query.shape[0]

    packed = jnp.concatenate([w_out, w_up[:, :width], w_up[:, width:], w_down], axis=0)
    feed_weights = lax.all_gather(packed, ("scene", "lat"), axis=0, tiled=False)

    own_lat = jnp.pad(latents, ((0, lat_pad - lat_rows), (0, 0)))
    far_lat = swap(own_lat, "lat", 2)
    lats = [own_lat, swap(own_lat, "lat", 1), far_lat, swap(far_lat, "lat", 1)]

    vectors = [first_gain, first_bias, second_gain, second_bias, out_bias, down_bias, up_bias]
    flat = jnp.concatenate(vectors)
    flat = jnp.pad(flat, (0, OWN - flat.shape[0]))
    trio = jnp.stack([w_query, w_key, w_value]).reshape(3, shard, LATS, OWN)
    message_rows = -(-(3 * shard + 1) // 16) * 16
    trio = jnp.transpose(trio, (2, 0, 1, 3)).reshape(LATS, 3 * shard, OWN)
    message = jnp.concatenate(
        [
            trio,
            jnp.broadcast_to(flat, (LATS, 1, OWN)),
            jnp.zeros((LATS, message_rows - 3 * shard - 1, OWN), BF),
        ],
        axis=1,
    )
    pieces = [
        lax.dynamic_index_in_dim(message, lat ^ k, 0, keepdims=False) for k in range(LATS)
    ]
    pieces = [pieces[0]] + [swap(pieces[k], "lat", k) for k in range(1, LATS)]
    pieces = untangle(jnp.stack(pieces), lat)
    gathered = gather_scene(pieces)
    trio = gathered[:, :, : 3 * shard].reshape(scenes, LATS, 3, shard, OWN)
    trio = jnp.transpose(trio, (2, 0, 1, 3, 4)).reshape(3, width, OWN)
    vec = gathered[:, :, 3 * shard, : 8 * shard].astype(F32).reshape(scenes * LATS, 8, shard)
    vec = jnp.transpose(vec, (1, 0, 2)).reshape(8, width)[:6]
    up_shift = gathered[:, :, 3 * shard, 6 * shard : 8 * shard].astype(F32).reshape(1, hidden)
    turned = jnp.transpose(trio, (0, 2, 1))
    turned = lax.all_gather(turned, "lat", axis=1, tiled=True)

    spot = jnp.arange(lat_pad, dtype=jnp.int32)
    block_of = lat ^ jnp.arange(LATS, dtype=jnp.int32)
    view_of = (block_of[:, None] * lat_rows + spot[None, :]) // VIEW_TOK
    matches = view_of[..., None] == jnp.arange(VIEWS, dtype=jnp.int32)
    listed = jnp.sum(jnp.where(matches, view_mask[0], 0), axis=-1) > 0
    live = listed & (view_of < view_count[0]) & (spot < lat_rows)[None, :]
    shut = jnp.where(live, 0.0, DEAD).astype(F32).reshape(LATS, 1, lat_pad)

    lifted1, query, query_t = make_queries(where, rays, trio[0], vec[0:1], vec[1:2])
    key, key_t, val, val_t = make_keyset(lats, trio[1], trio[2], shut)

    there_ctx, weights, inverse = attend(1, query, key_t, val)
    here_ctx, weights, inverse = attend(0, query, key_t, val, (weights, inverse))
    ctxs = [
        here_ctx,
        swap(there_ctx, "lat", 1),
        swap(here_ctx, "lat", 2),
        swap(there_ctx, "lat", 3),
    ]

    full_out = feed_weights[:, :shard].reshape(width, width)
    full_up = jnp.concatenate(
        [
            feed_weights[:, shard : 2 * shard].reshape(width, width),
            feed_weights[:, 2 * shard : 3 * shard].reshape(width, width),
        ],
        axis=1,
    )
    full_down = feed_weights[:, 3 * shard :].reshape(hidden, width)
    rows_in = jnp.stack([vec[4], vec[5], vec[2], vec[3]])
    (
        out_half,
        d_middle,
        d_branch,
        d_own,
        d_sibling,
        lifted2,
        d_before,
        active,
        feed_sums,
        up_sums,
    ) = feed(
        where, rays, ctxs, cotangent, full_out, full_up, full_down, rows_in, up_shift
    )
    d_there = swap(d_sibling, "lat", 1)
    layer_out = both_halves(core, out_half, swap(out_half, "lat", 1))

    out_own, out_sib, up_own, up_sib, down_own, down_sib = feed_grads(
        where, ctxs, d_branch, lifted2, d_before, active, cotangent
    )

    def by_scene(out_part, up_part, down_part):
        parts = [
            out_part.reshape(scenes, -1, OWN),
            up_part.reshape(scenes, -1, 2, OWN).swapaxes(1, 2).reshape(scenes, -1, OWN),
            down_part.reshape(scenes, -1, OWN),
        ]
        return jnp.concatenate(parts, axis=1)

    feed_part = by_scene(out_own, up_own, down_own)
    feed_other = swap(by_scene(out_sib, up_sib, down_sib), "lat", 1)
    feed_part = (feed_part.astype(F32) + feed_other.astype(F32)).astype(BF)
    feed_part = scatter_scene(feed_part)

    grad, grad_t = prepare(d_own, d_there, here_ctx, there_ctx, inverse)
    d_query, d_key, d_val = attend_back(weights, grad, grad_t, query_t, key, val_t)
    d_query = d_query[:, :, :HEAD_DIM].swapaxes(0, 1).reshape(count, OWN)
    dq_here, dq_there = d_query[:half], d_query[half:]
    d_queries = [
        dq_here,
        swap(dq_there, "lat", 1),
        swap(dq_here, "lat", 2),
        swap(dq_there, "lat", 3),
    ]
    ray_half, first_sums = first_grads(where, rays, d_queries, turned[0], vec[0:1], d_middle)
    ray_grad = both_halves(core, ray_half, swap(ray_half, "lat", 1))

    d_key = d_key.reshape(OWN, -1)
    d_val = d_val.reshape(OWN, -1)
    pair = jnp.stack([d_key, d_val]).reshape(2, OWN, LATS, lat_pad)
    got = [pair[:, :, 0]] + [swap(pair[:, :, k], "lat", k) for k in range(1, LATS)]
    latent_grad = latent_grads(where, got, turned[1], turned[2], lat_rows)

    trio_grads = projection_grads(lifted1, dq_here, dq_there, lats, d_key, d_val)
    trio_grads = trio_grads.reshape(3, scenes, LATS * shard, OWN).swapaxes(0, 1)
    trio_grads = trio_grads.reshape(scenes, 3 * LATS * shard, OWN)
    vec_grads = [first_sums[0], first_sums[1], feed_sums[0], feed_sums[1], feed_sums[2], feed_sums[3]]
    vec_grads = [v.reshape(scenes, LATS, shard) for v in vec_grads]
    vec_grads.append(up_sums[0].reshape(scenes, LATS, 2 * shard))
    vec_grads = jnp.concatenate(vec_grads, axis=2)
    vec_grads = jnp.pad(vec_grads, ((0, 0), (0, 0), (0, OWN - 8 * shard)))
    late = scatter_scene(jnp.concatenate([trio_grads, vec_grads.astype(BF)], axis=1))

    block = LATS * shard
    mats = [late[i * block : (i + 1) * block].reshape(LATS, shard, OWN) for i in range(3)]
    mats += [feed_part[i * block : (i + 1) * block].reshape(LATS, shard, OWN) for i in range(3)]
    mats.append(feed_part[3 * block :].reshape(LATS, 2 * shard, OWN))
    mats.append(late[3 * block : 3 * block + LATS].reshape(LATS, 1, OWN))
    final = jnp.concatenate(mats, axis=1)
    sent = [lax.dynamic_index_in_dim(final, lat ^ k, 0, keepdims=False) for k in range(LATS)]
    near = [sent[0]] + [swap(sent[k].astype(BF), "lat", k).astype(F32) for k in range(1, LATS)]
    vec_own = near[0][8 * shard] + near[1][8 * shard]
    cols = untangle(jnp.stack(near), lat)
    joined = jnp.transpose(cols[:, : 8 * shard], (1, 0, 2))

    def columns(first, rows):
        return joined[first : first + rows].reshape(rows, width)

    up_pair = cols[:, 4 * shard : 6 * shard].reshape(LATS, 2, shard, OWN)
    up_grad = jnp.transpose(up_pair, (2, 0, 1, 3)).reshape(shard, hidden)
    piece = lambda i: vec_own[i * shard : (i + 1) * shard]
    return (
        layer_out,
        ray_grad,
        latent_grad,
        columns(0, shard),
        columns(shard, shard),
        columns(2 * shard, shard),
        columns(3 * shard, shard),
        up_grad,
        columns(6 * shard, 2 * shard),
        piece(0),
        piece(1),
        piece(2),
        piece(3),
        piece(4),
        vec_own[6 * shard : 8 * shard],
        piece(5),
    )


def solution(mesh):
    rows = P(("scene", "lat"), None)
    line = P(("scene", "lat"))
    scene = P("scene", None)
    in_specs = (scene, rows, P("scene"), scene, scene) + (rows,) * 6 + (line,) * 7
    out_specs = (scene, scene, rows) + (rows,) * 6 + (line,) * 7
    return jax.shard_map(body, mesh=mesh, in_specs=in_specs, out_specs=out_specs, check_vma=False)
```

```python
import math
from functools import partial

import jax
import jax.numpy as jnp
from jax import lax
from jax.experimental import pallas as pl
from jax.experimental.pallas import tpu as pltpu
from jax.sharding import PartitionSpec as P

HEADS = 12
HEAD_DIM = 64
VIEWS = 10
VIEW_TOK = 300
LANES = 128
LATS = 4
OWN_HEADS = HEADS // LATS
OWN = OWN_HEADS * HEAD_DIM
DEAD = -1e30
LOG2E = math.log2(math.e)
Q_SCALE = 0.125 * LOG2E
ROOT = math.sqrt(2.0 / math.pi)
VMEM_BYTES = 56 * 2**20
BF = jnp.bfloat16
F32 = jnp.float32


def dot(left, right):
    return jnp.dot(left, right, preferred_element_type=F32)


def dot_rt(left, right):
    return lax.dot_general(left, right, (((1,), (1,)), ((), ())), preferred_element_type=F32)


def dot_lt(left, right):
    return lax.dot_general(left, right, (((0,), (0,)), ((), ())), preferred_element_type=F32)


def params():
    return pltpu.CompilerParams(vmem_limit_bytes=VMEM_BYTES)


def cost(micros):
    return pl.CostEstimate(
        flops=int(micros * 1e9), bytes_accessed=int(micros * 3.3e6), transcendentals=0
    )


def vmem(count):
    return [pl.BlockSpec(memory_space=pltpu.VMEM)] * count


ANY = pl.BlockSpec(memory_space=pl.ANY)
SMEM = pl.BlockSpec(memory_space=pltpu.SMEM)


def shape(dims, dtype=BF):
    return jax.ShapeDtypeStruct(tuple(dims), dtype)


def norm_parts(values):
    center = values - jnp.mean(values, axis=-1, keepdims=True)
    spread = jnp.mean(center * center, axis=-1, keepdims=True)
    factor = lax.rsqrt(spread + 1e-05)
    return center * factor, factor


def norm_back(grad_out, normed, factor, gain_row):
    scaled = grad_out * gain_row
    return factor * (
        scaled
        - jnp.mean(scaled, axis=-1, keepdims=True)
        - normed * jnp.mean(scaled * normed, axis=-1, keepdims=True)
    )


def swap(values, axis, step):
    count = lax.axis_size(axis)
    return lax.ppermute(values, axis, [(i, i ^ step) for i in range(count)])


def stages(count):
    found, stride = [], count
    while stride > 1:
        group = 4 if stride % 4 == 0 else 2
        stride //= group
        found.append((stride, group))
    return found


def gather_scene(parts):
    steps = [0]
    got = [parts]
    passed = []
    for stride, group in stages(lax.axis_size("scene")):
        parts = got[0] if len(got) == 1 else jnp.concatenate(got)
        got = [parts] + [swap(parts, "scene", k * stride) for k in range(1, group)]
        steps = [step ^ (k * stride) for k in range(group) for step in steps]
        passed = passed or got[1:]
    return got, steps, passed


def in_order(stacked, steps, me):
    places = [steps.index(i) for i in range(len(steps))]
    order = jnp.take(jnp.array(places, jnp.int32), jnp.arange(len(steps)) ^ me)
    return jnp.take(stacked, order, axis=0)


def scatter_scene(blocks):
    count = lax.axis_size("scene")
    me = lax.axis_index("scene")
    held = blocks
    for stride, group in reversed(stages(count)):
        digit = (me // stride) % group
        view = held.reshape((-1, group) + blocks.shape[1:])
        total = lax.dynamic_index_in_dim(view, digit, 1, keepdims=False).astype(F32)
        for k in range(1, group):
            mine = lax.dynamic_index_in_dim(view, digit ^ k, 1, keepdims=False)
            total = total + swap(mine.astype(BF), "scene", k * stride).astype(F32)
        held = total.astype(BF)
    return total.reshape(blocks.shape[1:])


def fold(rows):
    half = rows.shape[0] // 2
    return jnp.concatenate([rows[:half], rows[half:]], axis=1)


def unfold(rows):
    half = rows.shape[1] // 2
    return jnp.concatenate([rows[:, :half], rows[:, half:]], axis=0)


def choose(index, options):
    picked = options[0]
    for i in range(1, len(options)):
        picked = jnp.where(index == i, options[i], picked)
    return picked


def pack_kernel(where, w_query, w_key, w_value, vector, *out):
    shard = w_query.shape[0]
    values = [w[...].astype(F32) for w in (w_query, w_key, w_value)]
    tail = jnp.broadcast_to(vector[...].astype(F32), (8, OWN))
    for k in range(LATS):
        target = where[0] ^ k
        for m, value in enumerate(values):
            cols = [value[:, p * OWN : (p + 1) * OWN] for p in range(LATS)]
            values_k = choose(target, cols)
            if m == 0:
                rows = [values_k]
            else:
                rows.append(values_k)
        out[k][...] = fold(jnp.concatenate(rows + [tail], axis=0)).astype(BF)


def pack(where, w_query, w_key, w_value, vector):
    rows = 3 * w_query.shape[0] + 8
    return pl.pallas_call(
        pack_kernel,
        out_shape=[shape((rows // 2, 2 * OWN))] * LATS,
        in_specs=[SMEM] + vmem(4),
        out_specs=vmem(LATS),
        compiler_params=params(),
        cost_estimate=cost(2),
        name="pack",
    )(where, w_query, w_key, w_value, vector)


def unpack_kernel(steps, where, *refs):
    *chunks, trio, turned, rows_out, up_out, held, lines = refs
    lat, scene = where[0], where[3]
    shard = held.shape[1] // (len(steps) * LATS)
    entry = 0
    for chunk in chunks:
        for p in range(chunk.shape[0]):
            values = unfold(chunk[p].astype(F32))
            source = (scene ^ steps[entry // LATS]) * LATS + (lat ^ (entry % LATS))
            at = pl.ds(pl.multiple_of(source * shard, 8), shard)
            for m in range(3):
                held[m, at, :] = values[m * shard : (m + 1) * shard]
            lines[pl.ds(source, 1), :] = values[3 * shard : 3 * shard + 1]
            entry += 1
    for m in range(3):
        low = held[m].astype(BF)
        trio[m] = low
        turned[m] = held[m].T.astype(BF)
    sources = lines.shape[0]
    low = lines[...].astype(BF)
    for target, size, first in ((rows_out, shard, 0), (up_out, 2 * shard, 6)):
        wide = target.shape[1]
        col = lax.broadcasted_iota(jnp.int32, (1, wide), 1).astype(F32)
        owner = jnp.floor((col + 0.5) * (1.0 / size))
        spot = col - owner * size
        row = lax.broadcasted_iota(jnp.int32, (OWN, 1), 0).astype(F32)
        line = lax.broadcasted_iota(jnp.int32, (sources, 1), 0).astype(F32)
        for v in range(6 if first == 0 else 1):
            hot = jnp.where(row == spot + (first + v) * shard, 1.0, 0.0).astype(BF)
            spread = jnp.where(line == owner, dot(low, hot), 0.0)
            target[v : v + 1, :] = jnp.sum(spread, axis=0, keepdims=True)


def unpack(where, chunks, steps, shard):
    sources = len(steps) * LATS
    width = sources * shard
    return pl.pallas_call(
        partial(unpack_kernel, steps),
        out_shape=[
            shape((3, width, OWN)),
            shape((3, OWN, width)),
            shape((8, width), F32),
            shape((1, 2 * width), F32),
        ],
        in_specs=[SMEM] + vmem(len(chunks)),
        out_specs=vmem(4),
        scratch_shapes=[pltpu.VMEM((3, width, OWN), F32), pltpu.VMEM((sources, OWN), F32)],
        compiler_params=params(),
        cost_estimate=cost(3),
        name="unpack",
    )(where, *chunks)


def attention_weights(where, w_query, w_key, w_value, vectors):
    shard, width = w_query.shape
    flat = jnp.concatenate(vectors)
    flat = jnp.pad(flat, (0, OWN - flat.shape[0])).reshape(1, OWN)
    if shard % 8 == 0:
        pieces = pack(where, w_query, w_key, w_value, flat)
        pieces = [pieces[0]] + [swap(pieces[k], "lat", k) for k in range(1, LATS)]
        chunks, steps, passed = gather_scene(jnp.stack(pieces))
        return unpack(where, chunks, steps, shard), pieces[2:], passed
    lat, scene = lax.axis_index("lat"), lax.axis_index("scene")
    scenes = lax.axis_size("scene")
    trio = jnp.stack([w_query, w_key, w_value]).reshape(3, shard, LATS, OWN)
    trio = jnp.transpose(trio, (2, 0, 1, 3)).reshape(LATS, 3 * shard, OWN)
    message = jnp.concatenate([trio, jnp.broadcast_to(flat, (LATS, 1, OWN))], axis=1)
    pieces = [lax.dynamic_index_in_dim(message, lat ^ k, 0, keepdims=False) for k in range(LATS)]
    pieces = [pieces[0]] + [swap(pieces[k], "lat", k) for k in range(1, LATS)]
    pieces = in_order(jnp.stack(pieces), list(range(LATS)), lat)
    chunks, steps, passed = gather_scene(pieces[None])
    gathered = in_order(jnp.concatenate(chunks), steps, scene)
    trio = gathered[:, :, : 3 * shard].reshape(scenes, LATS, 3, shard, OWN)
    trio = jnp.transpose(trio, (2, 0, 1, 3, 4)).reshape(3, width, OWN)
    lines = gathered[:, :, 3 * shard, : 8 * shard].astype(F32).reshape(scenes * LATS, 8, shard)
    rows = jnp.transpose(lines, (1, 0, 2)).reshape(8, width)
    up = lines[:, 6:].reshape(1, 2 * width)
    return (trio, jnp.transpose(trio, (0, 2, 1)), rows, up), [], []


def pad_kernel(latents, *refs):
    out = refs[-1]
    rows = latents.shape[0]
    out[:rows, :] = latents[...]
    out[rows:, :] = jnp.zeros((out.shape[0] - rows, out.shape[1]), out.dtype)


def pad_latents(latents, rows, after):
    return pl.pallas_call(
        pad_kernel,
        out_shape=shape((rows, latents.shape[1])),
        in_specs=vmem(1) + [ANY] * len(after),
        out_specs=pl.BlockSpec(memory_space=pltpu.VMEM),
        compiler_params=params(),
        cost_estimate=cost(2),
        name="pad_latents",
    )(latents, *after)


def pack_feed_kernel(w_out, w_up, w_down, *refs):
    out = refs[-1]
    shard, width = w_out.shape
    out[: 2 * shard, :] = w_down[...]
    out[2 * shard : 3 * shard, :] = w_out[...]
    out[3 * shard : 4 * shard, :] = w_up[:, :width]
    out[4 * shard :, :] = w_up[:, width:]


def pack_feed(w_out, w_up, w_down, after):
    shard, width = w_out.shape
    return pl.pallas_call(
        pack_feed_kernel,
        out_shape=shape((5 * shard, width)),
        in_specs=vmem(3) + [ANY] * len(after),
        out_specs=pl.BlockSpec(memory_space=pltpu.VMEM),
        compiler_params=params(),
        cost_estimate=cost(2),
        name="pack_feed",
    )(w_out, w_up, w_down, *after)


def assemble_kernel(steps, where, *refs):
    chunks, (w_out, w_up, w_down, held) = refs[:LATS], refs[LATS:]
    lat, scene = where[0], where[3]
    shard = held.shape[1] // 5
    width = w_out.shape[1]
    for j, chunk in enumerate(chunks):
        for p, step in enumerate(steps):
            held[(scene ^ step) * LATS + (lat ^ j)] = chunk[p]
    w_down[...] = held[:, : 2 * shard, :].reshape(w_down.shape)
    w_out[...] = held[:, 2 * shard : 3 * shard, :].reshape(w_out.shape)
    w_up[:, :width] = held[:, 3 * shard : 4 * shard, :].reshape(width, width)
    w_up[:, width:] = held[:, 4 * shard :, :].reshape(width, width)


def assemble(where, chunks, steps):
    _, rows, width = chunks[0].shape
    sources = len(steps) * LATS
    return pl.pallas_call(
        partial(assemble_kernel, steps),
        out_shape=[shape((width, width)), shape((width, 2 * width)), shape((2 * width, width))],
        in_specs=[SMEM] + vmem(LATS),
        out_specs=vmem(3),
        scratch_shapes=[pltpu.VMEM((sources, rows, width), BF)],
        compiler_params=params(),
        cost_estimate=cost(6),
        name="assemble",
    )(where, *chunks)


def feed_weights(where, w_out, w_up, w_down, after):
    shard, width = w_out.shape
    if shard % 8 == 0:
        chunks, steps, _ = gather_scene(pack_feed(w_out, w_up, w_down, after)[None])
        mine = jnp.concatenate(chunks)
        far = swap(mine, "lat", 2)
        chunks = [mine, swap(mine, "lat", 1), far, swap(far, "lat", 1)]
        return assemble(where, chunks, steps)
    packed = jnp.concatenate([w_out, w_up[:, :width], w_up[:, width:], w_down], axis=0)
    held = lax.all_gather(packed, ("scene", "lat"), axis=0, tiled=False)
    parts = [held[:, n * shard : (n + 1) * shard].reshape(width, width) for n in range(3)]
    up = jnp.concatenate(parts[1:], axis=1)
    return parts[0], up, held[:, 3 * shard :].reshape(2 * width, width)


def pad_heads(weight):
    gap = jnp.zeros((weight.shape[0], LANES - HEAD_DIM), weight.dtype)
    pieces = []
    for h in range(OWN_HEADS):
        pieces += [weight[:, h * HEAD_DIM : (h + 1) * HEAD_DIM], gap]
    return jnp.concatenate(pieces, axis=1)


def query_kernel(where, rays, weight, rows_in, normed_low, query, query_t, wide):
    @pl.when(pl.program_id(0) == 0)
    def _():
        wide[...] = pad_heads(weight[0])

    normed, _ = norm_parts(rays[...].astype(F32))
    normed_low[...] = normed.astype(BF)
    low = (normed * rows_in[0:1, :] + rows_in[1:2, :]).astype(BF)
    values = dot(low, wide[...]) * Q_SCALE
    lane = lax.broadcasted_iota(jnp.int32, (1, LANES), 1)
    for h in range(OWN_HEADS):
        one = values[:, h * LANES : (h + 1) * LANES]
        query[h] = jnp.where(lane == HEAD_DIM, 1.0, one).astype(BF)
        query_t[h, 0] = one.T[:HEAD_DIM].astype(BF)


def make_queries(where, rays, trio, rows_in):
    count, width = rays.shape
    block = count // 4
    whole = lambda a: pl.BlockSpec(a.shape, lambda i, w: (0,) * a.ndim)
    return pl.pallas_call(
        query_kernel,
        grid_spec=pltpu.PrefetchScalarGridSpec(
            num_scalar_prefetch=1,
            grid=(4,),
            in_specs=[
                pl.BlockSpec((block, width), lambda i, w: (i ^ (2 * w[1]), 0)),
                pl.BlockSpec((1,) + trio.shape[1:], lambda i, w: (0, 0, 0)),
                whole(rows_in),
            ],
            out_specs=[
                pl.BlockSpec((block, width), lambda i, w: (i, 0)),
                pl.BlockSpec((OWN_HEADS, block, LANES), lambda i, w: (0, i, 0)),
                pl.BlockSpec((OWN_HEADS, 1, HEAD_DIM, block), lambda i, w: (0, i, 0, 0)),
            ],
            scratch_shapes=[pltpu.VMEM((width, OWN_HEADS * LANES), BF)],
        ),
        out_shape=[
            shape((count, width)),
            shape((OWN_HEADS, count, LANES)),
            shape((OWN_HEADS, 4, HEAD_DIM, block)),
        ],
        compiler_params=params(),
        cost_estimate=cost(6),
        name="queries",
    )(where, rays, trio, rows_in)


def keyset_kernel(lat0, lat1, lat2, lat3, trio, shut, key, key_t, val, val_t, wide, here):
    step = pl.program_id(0)

    @pl.when(step == 0)
    def _():
        wide[0] = pad_heads(trio[1])
        wide[1] = pad_heads(trio[2])

    for j, lat in enumerate((lat0, lat1, lat2, lat3)):

        @pl.when(step == j)
        def _():
            here[...] = lat[...]

    lane = lax.broadcasted_iota(jnp.int32, (1, LANES), 1)
    line = lax.broadcasted_iota(jnp.int32, (LANES, 1), 0)
    extra = (lane == HEAD_DIM) | (lane == HEAD_DIM + 1)
    keys = dot(here[...], wide[0])
    vals = dot(here[...], wide[1])
    for h in range(OWN_HEADS):
        one = keys[:, h * LANES : (h + 1) * LANES]
        key[h] = one.astype(BF)
        key_t[h] = jnp.where(line == HEAD_DIM, shut[0], one.T).astype(BF)
        one = jnp.where(extra, 1.0, vals[:, h * LANES : (h + 1) * LANES])
        val_t[h] = one.T.astype(BF)
    narrow = dot(here[...], trio[2])
    lane = lax.broadcasted_iota(jnp.int32, (1, 2 * LANES), 1)
    narrow = jnp.concatenate(
        [narrow, jnp.ones((narrow.shape[0], 2 * LANES - OWN), F32)], axis=1
    )
    for h in range(OWN_HEADS):
        first = h * HEAD_DIM
        mine = ((lane >= first) & (lane < first + HEAD_DIM)) | (lane == OWN)
        val[h] = jnp.where(mine, narrow, 0.0).astype(BF)


def make_keyset(lats, trio, shut):
    rows, width = lats[0].shape
    total = LATS * rows
    tall, long = shape((OWN_HEADS, total, LANES)), shape((OWN_HEADS, LANES, total))
    broad = shape((OWN_HEADS, total, 2 * LANES))
    whole = lambda a: pl.BlockSpec(a.shape, lambda i: (0,) * a.ndim)
    down = pl.BlockSpec((OWN_HEADS, rows, LANES), lambda i: (0, i, 0))
    flat = pl.BlockSpec((OWN_HEADS, rows, 2 * LANES), lambda i: (0, i, 0))
    over = pl.BlockSpec((OWN_HEADS, LANES, rows), lambda i: (0, 0, i))
    return pl.pallas_call(
        keyset_kernel,
        grid=(LATS,),
        out_shape=[tall, long, broad, long],
        in_specs=[whole(lat) for lat in lats]
        + [whole(trio), pl.BlockSpec((1, 1, rows), lambda i: (i, 0, 0))],
        out_specs=[down, over, flat, over],
        scratch_shapes=[
            pltpu.VMEM((2, width, OWN_HEADS * LANES), BF),
            pltpu.VMEM((rows, width), BF),
        ],
        compiler_params=params(),
        cost_estimate=cost(8),
        name="keyset",
    )(*lats, trio, shut)


def attend_kernel(sub, query, key_t, val, *rest):
    context, weights, inverse, mixed = rest[-4:]
    head, part = pl.program_id(0), pl.program_id(1)
    rows = query.shape[1]

    @pl.when(head == 0)
    def _():
        mixed[part] = jnp.zeros(mixed.shape[1:], F32)

    def score(i):
        return dot(query[0, i * sub : (i + 1) * sub, :], key_t[0])

    scores = score(0)
    for i in range(rows // sub):
        later = score(i + 1) if i + 1 < rows // sub else None
        at = slice(i * sub, (i + 1) * sub)
        low = jnp.exp2(scores - jnp.max(scores, axis=1, keepdims=True)).astype(BF)
        weights[0, at, :] = low
        summed = dot(low, val[0])
        scale = 1.0 / summed[:, OWN : OWN + 1]
        mixed[part, at, :] += summed * scale
        inverse[0, at, :] = jnp.broadcast_to(scale, (sub, LANES))
        scores = later

    for p in range(2):

        @pl.when((head == OWN_HEADS - 1) & (part == p))
        def _():
            context[:, p * OWN : (p + 1) * OWN] = mixed[p, :, :OWN].astype(BF)


def attend(half_index, query, key_t, val, held=None):
    _, count, _ = query.shape
    total = key_t.shape[2]
    half = count // 2
    block = half // 2
    sub = block // 3 if block % 48 == 0 else block
    rows = lambda cols: pl.BlockSpec((1, block, cols), lambda h, b: (h, 2 * half_index + b, 0))
    every = lambda rows, cols: pl.BlockSpec((1, rows, cols), lambda h, b: (h, 0, 0))
    extra = [] if held is None else list(held)
    return pl.pallas_call(
        partial(attend_kernel, sub),
        grid=(OWN_HEADS, 2),
        in_specs=[rows(LANES), every(LANES, total), every(total, 2 * LANES)] + [ANY] * len(extra),
        out_specs=[
            pl.BlockSpec((block, 2 * OWN), lambda h, b: (0, 0)),
            rows(total),
            rows(LANES),
        ],
        out_shape=[
            shape((block, 2 * OWN)),
            shape((OWN_HEADS, count, total)),
            shape((OWN_HEADS, count, LANES), F32),
        ],
        scratch_shapes=[pltpu.VMEM((2, block, 2 * LANES), F32)],
        input_output_aliases={3: 1, 4: 2} if extra else {},
        compiler_params=params(),
        cost_estimate=cost(16),
        name="attend",
    )(query, key_t, val, *extra)


def turn_kernel(trio, *refs):
    out = refs[-1]
    for m in range(3):
        out[m] = trio[m].astype(F32).T.astype(BF)


def turn(trio, after):
    _, width, cols = trio.shape
    return pl.pallas_call(
        turn_kernel,
        out_shape=shape((3, cols, width)),
        in_specs=vmem(1) + [ANY] * len(after),
        out_specs=pl.BlockSpec(memory_space=pltpu.VMEM),
        compiler_params=params(),
        cost_estimate=cost(2),
        name="turn",
    )(trio, *after)


def prepare_kernel(d_ctx, ctx, inverse, *refs):
    grad, grad_t = refs[-2:]
    lane = lax.broadcasted_iota(jnp.int32, (1, LANES), 1)
    block = d_ctx.shape[0]
    gap = jnp.zeros((block, LANES - HEAD_DIM), F32)
    for p in range(2):
        at = slice(p * block, (p + 1) * block)
        upstream = d_ctx[:, p * OWN : (p + 1) * OWN].astype(F32)
        product = upstream * ctx[:, p * OWN : (p + 1) * OWN].astype(F32)
        for h in range(OWN_HEADS):
            cols = slice(h * HEAD_DIM, (h + 1) * HEAD_DIM)
            scale = inverse[h, at, :]
            delta = jnp.sum(product[:, cols], axis=1, keepdims=True) * scale
            high = delta.astype(BF).astype(F32)
            wide = jnp.concatenate([upstream[:, cols], gap], axis=1) * scale
            grad_t[h, p] = wide.T[:HEAD_DIM].astype(BF)
            wide = jnp.where(lane == HEAD_DIM, -high, wide)
            wide = jnp.where(lane == HEAD_DIM + 1, high - delta, wide)
            grad[h, at, :] = wide.astype(BF)


def prepare(half_index, d_ctx, ctx, inverse, held=None):
    _, count, _ = inverse.shape
    half = count // 2
    extra = [] if held is None else list(held)
    whole = lambda a: pl.BlockSpec(a.shape, lambda i: (0, 0))
    rows = pl.BlockSpec((OWN_HEADS, half, LANES), lambda i: (0, half_index, 0))
    return pl.pallas_call(
        prepare_kernel,
        grid=(1,),
        out_shape=[
            shape((OWN_HEADS, count, LANES)),
            shape((OWN_HEADS, 4, HEAD_DIM, half // 2)),
        ],
        in_specs=[whole(d_ctx), whole(ctx), rows] + [ANY] * len(extra),
        out_specs=[
            rows,
            pl.BlockSpec((OWN_HEADS, 2, HEAD_DIM, half // 2), lambda i: (0, half_index, 0, 0)),
        ],
        input_output_aliases={3: 0, 4: 1} if extra else {},
        compiler_params=params(),
        cost_estimate=cost(3),
        name="prepare",
    )(d_ctx, ctx, inverse, *extra)


def back_kernel(sub, lat_rows, apart, weights, grad, grad_t, query_t, key, val_t, *refs):
    *out, sums, d_query = refs[-2 - LATS * (2 if apart else 1) :]
    pair_out, query_out = out[:LATS], out[-LATS:]
    query_at = 0 if apart else 2 * lat_rows
    step = pl.program_id(0)
    rows = weights.shape[1]
    start = pl.multiple_of((step % 2) * rows, rows)
    val_part = dot(grad_t[0, 0], weights[0])
    found = []
    for i in range(rows // sub):
        at = slice(i * sub, (i + 1) * sub)
        d_weights = dot(grad[0, at], val_t[0])
        d_scores = (weights[0, at, :].astype(F32) * d_weights).astype(BF)
        d_query[pl.ds(start + i * sub, sub), :] = dot(d_scores, key[0]) * 0.125
        found.append(d_scores)
    d_scores = jnp.concatenate(found, axis=0) if len(found) > 1 else found[0]
    key_part = dot(query_t[0, 0], d_scores) * (1.0 / LOG2E)

    @pl.when(step == 0)
    def _():
        sums[0] = key_part
        sums[1] = val_part

    @pl.when(step > 0)
    def _():
        sums[0] += key_part
        sums[1] += val_part

    @pl.when(step == 3)
    def _():
        for i in range(2):
            total = sums[i].astype(BF)
            for j in range(LATS):
                pair_out[j][:, i * lat_rows : (i + 1) * lat_rows] = total[
                    :, j * lat_rows : (j + 1) * lat_rows
                ]

    for last in (1, 3):

        @pl.when(step == last)
        def _():
            turned = d_query[...].T[:HEAD_DIM].astype(BF)
            for j in (last // 2, last // 2 + 2):
                query_out[j][:, query_at : query_at + 2 * rows] = turned


def attend_back(head, apart, weights, grad, grad_t, query_t, key, val_t, after):
    _, count, total = weights.shape
    rows = count // 4
    sub = rows // 2 if rows % 32 == 0 else rows
    lat_rows = total // LATS
    pad = lambda n: -(-n // LANES) * LANES
    if apart:
        widths = [2 * lat_rows] * LATS + [pad(2 * rows)] * LATS
    else:
        widths = [pad(2 * lat_rows + 2 * rows)] * LATS
    of_head = lambda cols: pl.BlockSpec((1, rows, cols), lambda b: (head, b, 0))
    turned = pl.BlockSpec((1, 1, HEAD_DIM, rows), lambda b: (head, b, 0, 0))
    return pl.pallas_call(
        partial(back_kernel, sub, lat_rows, apart),
        grid=(4,),
        in_specs=[
            of_head(total),
            of_head(LANES),
            turned,
            turned,
            pl.BlockSpec((1, total, LANES), lambda b: (head, 0, 0)),
            pl.BlockSpec((1, LANES, total), lambda b: (head, 0, 0)),
        ]
        + [ANY] * len(after),
        out_specs=[pl.BlockSpec((HEAD_DIM, w), lambda b: (0, 0)) for w in widths],
        out_shape=[shape((HEAD_DIM, w)) for w in widths],
        scratch_shapes=[
            pltpu.VMEM((2, HEAD_DIM, total), F32),
            pltpu.VMEM((2 * rows, LANES), F32),
        ],
        compiler_params=params(),
        cost_estimate=cost(13),
        name=f"attend_back_{head}",
    )(weights, grad, grad_t, query_t, key, val_t, *after)


def quarter_halves(values, core):
    mid = values.shape[1] // 2
    low, high = values[:, :mid], values[:, mid:]
    return jnp.where(core == 0, low, high), jnp.where(core == 0, high, low)


def feed_kernel(
    fine,
    where,
    rays,
    ctx0,
    ctx1,
    ctx2,
    ctx3,
    upstream,
    w_out,
    w_up,
    w_down,
    rows_in,
    up_shift,
    layer_out,
    d_middle,
    d_own,
    d_sibling,
    *refs,
):
    outs, (acc_out, acc_up, acc_down, sums, up_sums, halves) = refs[:-6], refs[-6:]
    step, last = pl.program_id(0), pl.num_programs(0) - 1
    lat, core, side = where[0], where[1], where[2]
    width = rays.shape[1]
    hidden = w_up.shape[1]

    @pl.when(step == 0)
    def _():
        for ref in (acc_out, acc_up, acc_down, sums, up_sums):
            ref[...] = jnp.zeros_like(ref)

    gain, bias = rows_in[2:3, :], rows_in[3:4, :]
    middle = rays[...].astype(F32) + rows_in[4:5, :]
    upper = step < (last + 1) // 2
    ctxs = [
        jnp.where(upper, ctx[:, :OWN], ctx[:, OWN:]) for ctx in (ctx0, ctx1, ctx2, ctx3)
    ]
    spots = [pl.ds(pl.multiple_of((lat ^ j) * OWN, OWN), OWN) for j in range(LATS)]
    for ctx, at in zip(ctxs, spots):
        middle = middle + dot(ctx, w_out[at, :])
    normed, factor = norm_parts(middle)
    low = (normed * gain + bias).astype(BF)
    before = dot(low, w_up[...]) + up_shift[...]
    squared = before * before
    bent = jnp.tanh(ROOT * before * (1.0 + 0.044715 * squared))
    act = (0.5 * before * (1.0 + bent)).astype(BF)
    layer_out[...] = (middle + dot(act, w_down[...]) + rows_in[5:6, :]).astype(BF)
    slope = 0.5 * (1.0 + bent) + (0.5 * ROOT) * before * (1.0 - bent * bent) * (
        1.0 + 3 * 0.044715 * squared
    )
    d_pre = (dot_rt(upstream[...], w_down[...]) * slope).astype(BF)
    d_lifted = dot_rt(d_pre, w_up[...])
    up_wide = upstream[...].astype(F32)
    d_mid = up_wide + norm_back(d_lifted, normed, factor, gain)
    d_middle[...] = d_mid
    branch = d_mid.astype(BF)
    block = rays.shape[0]
    place = pl.ds(pl.multiple_of((step % ((last + 1) // 2)) * block, 16), block)
    for target, at in zip((d_own, d_sibling), spots):
        part = dot_rt(branch, w_out[at, :]).astype(BF)

        @pl.when(upper)
        def _():
            target[place, :OWN] = part

        @pl.when(jnp.logical_not(upper))
        def _():
            target[place, OWN:] = part

    column = lambda v: jnp.sum(v, axis=0, keepdims=True)
    sums[0:1, :] += column(d_lifted * normed)
    sums[1:2, :] += column(d_lifted)
    sums[2:3, :] += column(branch.astype(F32))
    sums[3:4, :] += column(up_wide)
    up_sums[0:1, :] += column(d_pre.astype(F32))

    wide, narrow = hidden // 2, width // 2
    halves[:, :hidden] = d_pre
    halves[:, hidden:] = branch
    pre_half = halves[:, pl.ds(pl.multiple_of(side * wide, LANES), wide)]
    branch_half = halves[:, pl.ds(pl.multiple_of(hidden + side * narrow, LANES), narrow)]
    up_half = upstream[:, pl.ds(pl.multiple_of(side * narrow, LANES), narrow)]
    for ctx, at in zip(ctxs, spots):
        acc_out[at, :] += dot_lt(ctx, branch_half)
    acc_up[...] += dot_lt(low, pre_half)
    acc_down[...] += dot_lt(act, up_half)

    @pl.when(step == last)
    def _():
        if not fine:
            for i, acc in enumerate((acc_out, acc_up, acc_down)):
                own, sibling = quarter_halves(acc[...], core)
                outs[2 * i][...] = own.astype(BF)
                outs[2 * i + 1][...] = sibling.astype(BF)
            outs[6][...] = sums[...]
            outs[7][...] = up_sums[...]
            return
        own_msg, sib_msg = outs
        scenes = own_msg.shape[0]
        block = width // scenes
        for i, acc in enumerate((acc_out, acc_up, acc_down)):
            for msg, part in zip((own_msg, sib_msg), quarter_halves(acc[...], core)):
                part = part.astype(BF)
                for s in range(scenes):
                    if i == 0:
                        msg[s, :block, :OWN] = part[s * block : (s + 1) * block]
                    elif i == 1:
                        msg[s, block : 2 * block, :] = part[s * block : (s + 1) * block]
                    else:
                        rows = part[2 * s * block : 2 * (s + 1) * block]
                        msg[s, 2 * block : 3 * block, :] = fold(rows)
        lines = line_up(sums, up_sums, scenes * LATS)
        for s in range(scenes):
            mine = lines[s * LATS : (s + 1) * LATS]
            mine = jnp.concatenate([mine, jnp.zeros((block - LATS, OWN), F32)], axis=0)
            own_msg[s, :block, OWN:] = mine.astype(BF)
            sib_msg[s, :block, OWN:] = jnp.zeros((block, OWN), BF)


def line_up(sums, up_sums, sources):
    total = None
    for ref, size, first, count in (
        (sums, sums.shape[1] // sources, 2, 4),
        (up_sums, up_sums.shape[1] // sources, 6, 1),
    ):
        wide = ref.shape[1]
        col = lax.broadcasted_iota(jnp.int32, (1, wide), 1).astype(F32)
        owner = jnp.floor((col + 0.5) * (1.0 / size))
        spot = (col - owner * size)
        row = lax.broadcasted_iota(jnp.int32, (OWN, 1), 0).astype(F32)
        line = lax.broadcasted_iota(jnp.int32, (sources, 1), 0).astype(F32)
        shard = sums.shape[1] // sources
        for v in range(count):
            hot = jnp.where(row == spot + (first + v) * shard, 1.0, 0.0).astype(BF)
            mine = jnp.where(line == owner, ref[v : v + 1, :], 0.0).astype(BF)
            part = dot_rt(mine, hot)
            total = part if total is None else total + part
    return total


def feed(where, rays, ctxs, upstream, weights, rows_in, up_shift, scenes, fine):
    count, width = rays.shape
    hidden = up_shift.shape[1]
    half = count // 2
    steps = 4
    block = half // steps
    whole = lambda a: pl.BlockSpec(a.shape, lambda i, w: (0,) * a.ndim)
    mine = pl.BlockSpec((block, width), lambda i, w: (w[1] * steps + i, 0))
    local = lambda cols: pl.BlockSpec((block, cols), lambda i, w: (i, 0))
    if fine:
        msg = (scenes, 3 * (width // scenes), 2 * OWN)
        dims = [(msg, BF)] * 2
    else:
        mats = [(width, width // 4), (width, hidden // 4), (hidden, width // 4)]
        dims = [(d, BF) for d in mats for _ in range(2)] + [((8, width), F32), ((8, hidden), F32)]
    folded = pl.BlockSpec((half // 2, 2 * OWN), lambda i, w: (0, 0))
    return pl.pallas_call(
        partial(feed_kernel, fine),
        grid_spec=pltpu.PrefetchScalarGridSpec(
            num_scalar_prefetch=1,
            grid=(steps,),
            in_specs=[mine]
            + [pl.BlockSpec((block, 2 * OWN), lambda i, w: (i % (steps // 2), 0))] * LATS
            + [mine]
            + [whole(w) for w in weights]
            + [whole(rows_in), whole(up_shift)],
            out_specs=[local(width), local(width), folded, folded]
            + [pl.BlockSpec(d, partial(lambda n, i, w: (0,) * n, len(d))) for d, _ in dims],
            scratch_shapes=[
                pltpu.VMEM((width, width // 2), F32),
                pltpu.VMEM((width, hidden // 2), F32),
                pltpu.VMEM((hidden, width // 2), F32),
                pltpu.VMEM((8, width), F32),
                pltpu.VMEM((8, hidden), F32),
                pltpu.VMEM((block, hidden + width), BF),
            ],
        ),
        out_shape=[
            shape((half, width)),
            shape((half, width), F32),
            shape((half // 2, 2 * OWN)),
            shape((half // 2, 2 * OWN)),
        ]
        + [shape(d, t) for d, t in dims],
        compiler_params=params(),
        cost_estimate=cost(28),
        name="feed",
    )(where, rays, *ctxs, upstream, *weights, rows_in, up_shift)


def add_kernel(where, own, got, send, keep):
    row = where[4]
    for z in range(send.shape[0]):
        at = 2 * z + (1 - row)
        send[z] = (own[at].astype(F32) + got[at].astype(F32)).astype(BF)
        at = 2 * z + row
        keep[z] = (own[at].astype(F32) + got[at].astype(F32)).astype(BF)


def add_pair(where, own, got):
    scenes = own.shape[0]
    dims = (scenes // 2,) + own.shape[1:]
    return pl.pallas_call(
        add_kernel,
        out_shape=[shape(dims)] * 2,
        in_specs=[SMEM] + vmem(2),
        out_specs=vmem(2),
        compiler_params=params(),
        cost_estimate=cost(3),
        name="add_pair",
    )(where, own, got)


def spread_kernel(where, keep, got, *out):
    for k in range(4):
        at = where[5] ^ k
        out[k][...] = (keep[at].astype(F32) + got[at].astype(F32)).astype(BF)


def add_spread(where, keep, got):
    return pl.pallas_call(
        spread_kernel,
        out_shape=[shape(keep.shape[1:])] * 4,
        in_specs=[SMEM] + vmem(2),
        out_specs=vmem(4),
        compiler_params=params(),
        cost_estimate=cost(2),
        name="add_spread",
    )(where, keep, got)


def regroup_kernel(shard, where, *refs):
    late, feed_part, out, held = refs[:4], refs[4:8], refs[8:12], refs[12]
    block = LATS * shard
    first = sum(unfold(r[...].astype(F32)) for r in late)
    feed_sum = sum(r[...].astype(F32) for r in feed_part)
    left, right = feed_sum[:, :OWN], feed_sum[:, OWN:]
    held[: 3 * block] = first[: 3 * block]
    held[3 * block : 6 * block] = left
    held[6 * block :] = right[block:]
    for k in range(LATS):
        target = where[0] ^ k

        def part(base):
            return held[pl.ds(pl.multiple_of(base * block + target * shard, 8), shard), :]

        rows = [part(n) for n in (0, 1, 2, 3, 4, 6)]
        two = target % 2
        for n in range(2):
            at = (2 * two + n) * shard
            low = held[pl.ds(pl.multiple_of(5 * block + at, 8), shard), :]
            high = held[pl.ds(pl.multiple_of(7 * block + at, 8), shard), :]
            rows.append(jnp.where(target < 2, low, high))
        rows.append(first[3 * block : 3 * block + 8, :])
        line = choose(target, [right[p : p + 1] for p in range(LATS)])
        rows.append(jnp.broadcast_to(line, (24, OWN)))
        out[k][...] = fold(jnp.concatenate(rows, axis=0)).astype(BF)


def regroup(where, late, feed_part, shard):
    rows = 8 * shard + 32
    return pl.pallas_call(
        partial(regroup_kernel, shard),
        out_shape=[shape((rows // 2, 2 * OWN))] * LATS,
        in_specs=[SMEM] + vmem(8),
        out_specs=vmem(LATS),
        scratch_shapes=[pltpu.VMEM((8 * LATS * shard, OWN), F32)],
        compiler_params=params(),
        cost_estimate=cost(2),
        name="regroup",
    )(where, *late, *feed_part)


def settle_kernel(shard, where, got0, got1, got2, got3, w_query, gain, bias, *out):
    lat = where[0]
    mats, firsts, lines = out[:6], out[6:8], out[8]
    got = [unfold(g[...].astype(F32)) for g in (got0, got1, got2, got3)]
    at = 8 * shard + 8
    lines[...] = got[0][at : at + 8] + got[1][at : at + 8]
    whole = jnp.concatenate([choose(lat ^ p, got) for p in range(LATS)], axis=1)
    part = lambda n, count=1: whole[n * shard : (n + count) * shard]
    sums = whole[8 * shard : 8 * shard + 1] + whole[8 * shard + 1 : 8 * shard + 2]
    weight = w_query[...].astype(F32)
    mats[0][...] = part(0) * gain[...] + bias[...] * sums
    mats[1][...] = part(1)
    mats[2][...] = part(2)
    mats[3][...] = part(3)
    cols = [part(n)[:, p * OWN : (p + 1) * OWN] for p in range(LATS) for n in (4, 5)]
    mats[4][...] = jnp.concatenate(cols, axis=1)
    mats[5][...] = part(6, 2)
    firsts[0][...] = jnp.sum(part(0) * weight, axis=1, keepdims=True)
    firsts[1][...] = jnp.sum(weight * sums, axis=1, keepdims=True)


def settle(where, got, w_query, gain, bias):
    shard, width = w_query.shape
    flat = shape((shard, width), F32)
    tall = shape((2 * shard, width), F32)
    wide = shape((shard, 2 * width), F32)
    return pl.pallas_call(
        partial(settle_kernel, shard),
        out_shape=[flat] * 4
        + [wide, tall, shape((shard, 1), F32), shape((shard, 1), F32), shape((8, OWN), F32)],
        in_specs=[SMEM] + vmem(7),
        out_specs=vmem(9),
        compiler_params=params(),
        cost_estimate=cost(2),
        name="settle",
    )(where, *got, w_query, gain, bias)


def projection_grads_kernel(fine, lat_rows, where, normed_low, *refs):
    lats, msgs, out = refs[:4], refs[4:16], refs[16:]
    half = normed_low.shape[0] // 2
    width = normed_low.shape[1]
    msg = lambda h, j: msgs[h * LATS + j]
    d_query = [
        jnp.concatenate(
            [msg(h, j)[:, 2 * lat_rows : 2 * lat_rows + half] for h in range(OWN_HEADS)], axis=0
        )
        for j in range(2)
    ]
    total = dot(d_query[0], normed_low[:half]) + dot(d_query[1], normed_low[half:])
    sums = sum(jnp.sum(d.astype(F32), axis=1, keepdims=True) for d in d_query)
    high = sums.astype(BF).astype(F32)
    lane = lax.broadcasted_iota(jnp.int32, (1, LANES), 1)
    sums = jnp.where(lane == 0, high, jnp.where(lane == 1, sums - high, 0.0)).T[:32]
    parts = [total]
    pair = None
    for j in range(LATS):
        left = jnp.concatenate(
            [msg(h, j)[:, i * lat_rows : (i + 1) * lat_rows] for i in range(2) for h in range(OWN_HEADS)],
            axis=0,
        )
        part = dot(left, lats[j][...])
        pair = part if pair is None else pair + part
    parts += [pair[:OWN], pair[OWN:]]
    parts = [part.T for part in parts]
    if not fine:
        for i, part in enumerate(parts):
            out[0][i] = part.astype(BF)
        out[1][...] = sums
        return
    send, keep = out
    scenes = 2 * send.shape[0]
    block = width // scenes
    for s in range(scenes):
        rows = [part[s * block : (s + 1) * block] for part in parts]
        value = fold(jnp.concatenate(rows + [sums], axis=0)).astype(BF)
        mine = where[4] == s % 2

        @pl.when(mine)
        def _():
            keep[s // 2] = value

        @pl.when(jnp.logical_not(mine))
        def _():
            send[s // 2] = value


def projection_grads(where, normed_low, lats, msgs, scenes, fine):
    width = normed_low.shape[1]
    if fine:
        outs = [shape((scenes // 2, 3 * (width // scenes) // 2 + 16, 2 * OWN))] * 2
    else:
        outs = [shape((3, width, OWN)), shape((32, OWN), F32)]
    return pl.pallas_call(
        partial(projection_grads_kernel, fine, lats[0].shape[0]),
        out_shape=outs,
        in_specs=[SMEM] + vmem(17),
        out_specs=vmem(2),
        compiler_params=params(),
        cost_estimate=cost(7),
        name="projection_grads",
    )(where, normed_low, *lats, *msgs)


def first_grads_kernel(lat_rows, where, rays, rows_in, d_middle, *refs):
    turned, msgs, ray_grad, d_query = refs[:4], refs[4:16], refs[16], refs[17]
    half = rays.shape[0]
    for h in range(OWN_HEADS):
        for j in range(LATS):
            first = j * OWN + h * HEAD_DIM
            at = slice(first, first + HEAD_DIM)
            d_query[at, :] = msgs[h * LATS + j][:, 2 * lat_rows : 2 * lat_rows + half]
    weight = jnp.concatenate([t[0] for t in turned], axis=0)
    for first in range(0, half, 256):
        at = slice(first, min(first + 256, half))
        d_lifted = dot_lt(d_query[:, at], weight)
        normed, factor = norm_parts(rays[at, :].astype(F32))
        back = norm_back(d_lifted, normed, factor, rows_in[0:1, :])
        ray_grad[at, :] = (d_middle[at, :] + back).astype(BF)


def first_grads(where, rays, turned, rows_in, d_middle, msgs, lat_rows):
    count, width = rays.shape
    half = count // 2
    whole = lambda a: pl.BlockSpec(a.shape, lambda i, w: (0,) * a.ndim)
    return pl.pallas_call(
        partial(first_grads_kernel, lat_rows),
        grid_spec=pltpu.PrefetchScalarGridSpec(
            num_scalar_prefetch=1,
            grid=(1,),
            in_specs=[
                pl.BlockSpec((half, width), lambda i, w: (w[1], 0)),
                whole(rows_in),
                whole(d_middle),
            ]
            + [pl.BlockSpec((1, OWN, width), lambda i, w: (0, 0, 0))] * LATS
            + [whole(m) for m in msgs],
            out_specs=pl.BlockSpec((half, width), lambda i, w: (0, 0)),
            scratch_shapes=[pltpu.VMEM((width, half), BF)],
        ),
        out_shape=shape((half, width)),
        compiler_params=params(),
        cost_estimate=cost(6),
        name="first_grads",
    )(where, rays, rows_in, d_middle, *turned, *msgs)


def latent_kernel(*refs):
    turned, msgs, out, held = refs[:4], refs[4:16], refs[16], refs[17]
    lat_rows = held.shape[2]
    width = out.shape[1]
    total = None
    for i in range(2):
        for h in range(OWN_HEADS):
            for j in range(LATS):
                first = j * OWN + h * HEAD_DIM
                at = slice(first, first + HEAD_DIM)
                held[i, at, :] = msgs[h * LATS + j][:, i * lat_rows : (i + 1) * lat_rows]
        part = dot_lt(held[i], jnp.concatenate([t[1 + i] for t in turned], axis=0))
        total = part if total is None else total + part
    out[...] = total[: out.shape[0]].astype(BF)


def latent_grads(turned, msgs, rows, lat_rows):
    width = turned[0].shape[2]
    return pl.pallas_call(
        latent_kernel,
        out_shape=shape((rows, width)),
        in_specs=vmem(16),
        out_specs=pl.BlockSpec(memory_space=pltpu.VMEM),
        scratch_shapes=[pltpu.VMEM((2, width, lat_rows), BF)],
        compiler_params=params(),
        cost_estimate=cost(6),
        name="latent_grads",
    )(*turned, *msgs)


def both_halves(core, here, there):
    first = jnp.where(core == 0, here, there)
    second = jnp.where(core == 0, there, here)
    return jnp.concatenate([first, second], axis=0)


def body(
    rays,
    latents,
    view_count,
    view_mask,
    cotangent,
    w_query,
    w_key,
    w_value,
    w_out,
    w_up,
    w_down,
    first_gain,
    first_bias,
    second_gain,
    second_bias,
    out_bias,
    up_bias,
    down_bias,
):
    scenes = lax.axis_size("scene")
    lat, scene = lax.axis_index("lat"), lax.axis_index("scene")
    core, side = lat % 2, lat // 2
    where = jnp.stack([lat, core, side, scene, scene % 2, scene // 2]).astype(jnp.int32)
    count, width = rays.shape
    hidden = w_up.shape[1]
    lat_rows = latents.shape[0]
    lat_pad = -(-lat_rows // LANES) * LANES
    shard = w_query.shape[0]
    fine = shard % 8 == 0 and scenes == 8

    vectors = [first_gain, first_bias, second_gain, second_bias, out_bias, down_bias, up_bias]
    (trio, _, rows_in, up_shift), first_passed, passed = attention_weights(
        where, w_query, w_key, w_value, vectors
    )

    own_lat = pad_latents(latents, lat_pad, first_passed)
    far_lat = swap(own_lat, "lat", 2)
    lats = [own_lat, swap(own_lat, "lat", 1), far_lat, swap(far_lat, "lat", 1)]

    weights_in = feed_weights(where, w_out, w_up, w_down, passed)

    spot = jnp.arange(lat_pad, dtype=jnp.int32)
    block_of = lat ^ jnp.arange(LATS, dtype=jnp.int32)
    view_of = (block_of[:, None] * lat_rows + spot[None, :]) // VIEW_TOK
    matches = view_of[..., None] == jnp.arange(VIEWS, dtype=jnp.int32)
    listed = jnp.sum(jnp.where(matches, view_mask[0], 0), axis=-1) > 0
    live = listed & (view_of < view_count[0]) & (spot < lat_rows)[None, :]
    shut = jnp.where(live, 0.0, DEAD).astype(F32).reshape(LATS, 1, lat_pad)

    normed_low, query, query_t = make_queries(where, rays, trio, rows_in)
    key, key_t, val, val_t = make_keyset(lats, trio, shut)

    there_ctx, weights, inverse = attend(1, query, key_t, val)
    here_ctx, weights, inverse = attend(0, query, key_t, val, (weights, inverse))
    ctxs = [
        here_ctx,
        swap(there_ctx, "lat", 1),
        swap(here_ctx, "lat", 2),
        swap(there_ctx, "lat", 3),
    ]

    turned = turn(trio, [ctxs[1]])
    far_turned = swap(turned, "lat", 2)
    turned = [turned, swap(turned, "lat", 1), far_turned, swap(far_turned, "lat", 1)]
    out_half, d_middle, d_own, d_sibling, *feed_out = feed(
        where, rays, ctxs, cotangent, weights_in, rows_in, up_shift, scenes, fine
    )
    d_there = swap(d_sibling, "lat", 1)
    layer_out = both_halves(core, out_half, swap(out_half, "lat", 1))

    if fine:
        own_msg, sib_msg = feed_out
        send, keep = add_pair(where, own_msg, swap(sib_msg, "lat", 1))
        feed_blocks = add_spread(where, keep, swap(send, "scene", 1))
        feed_part = [feed_blocks[0]] + [swap(feed_blocks[k], "scene", 2 * k) for k in range(1, 4)]

    ready = prepare(0, d_own, here_ctx, inverse)
    ready = prepare(1, d_there, there_ctx, inverse, ready)
    waits = [[], [send], [feed_blocks[0]]] if fine else [[]] * OWN_HEADS
    back, got = [], []
    for h in range(OWN_HEADS):
        after = waits[h] + (back[-1:] if back else [])
        mine = attend_back(h, False, weights, *ready, query_t, key, val_t, after)
        back += mine
        got += [mine[0]] + [swap(mine[k], "lat", k) for k in range(1, LATS)]
    grads = projection_grads(where, normed_low, lats, back, scenes, fine)
    ray_half = first_grads(where, rays, turned, rows_in, d_middle, got, lat_pad)
    ray_grad = both_halves(core, ray_half, swap(ray_half, "lat", 1))
    latent_grad = latent_grads(turned, got, lat_rows, lat_pad)

    first = [v.reshape(shard, 1).astype(F32) for v in (first_gain, first_bias)]
    if fine:
        send, keep = grads
        late = add_spread(where, keep, swap(send, "scene", 1))
        late = [late[0]] + [swap(late[k], "scene", 2 * k) for k in range(1, 4)]
        final = regroup(where, late, feed_part, shard)
        final = [final[0]] + [swap(final[k], "lat", k) for k in range(1, LATS)]
    else:
        final = plain_final(feed_out, grads, scenes, shard)
    *mats, gain_grad, bias_grad, lines = settle(where, final, w_query, *first)
    piece = lambda i, n=1: lines[0, i * shard : (i + n) * shard]
    return (
        layer_out,
        ray_grad,
        latent_grad,
        mats[0],
        mats[1],
        mats[2],
        mats[3],
        mats[4],
        mats[5],
        gain_grad.reshape(shard),
        bias_grad.reshape(shard),
        piece(2),
        piece(3),
        piece(4),
        piece(6, 2),
        piece(5),
    )


def plain_final(feed_out, grads, scenes, shard):
    lat = lax.axis_index("lat")
    out_own, out_sib, up_own, up_sib, down_own, down_sib, sums, up_sums = feed_out
    trio, query_sums = grads

    def by_scene(out_part, up_part, down_part):
        parts = [
            out_part.reshape(scenes, -1, OWN),
            up_part.reshape(scenes, -1, 2, OWN).swapaxes(1, 2).reshape(scenes, -1, OWN),
            down_part.reshape(scenes, -1, OWN),
        ]
        return jnp.concatenate(parts, axis=1).astype(F32)

    feed_part = by_scene(out_own, up_own, down_own)
    feed_part = feed_part + swap(by_scene(out_sib, up_sib, down_sib), "lat", 1)
    feed_part = scatter_scene(feed_part)
    block = LATS * shard
    trio = trio.reshape(3, scenes, block, OWN).swapaxes(0, 1).reshape(scenes, 3 * block, OWN)
    lines = [v.reshape(scenes, LATS, shard) for v in sums[:4]]
    lines = [jnp.zeros_like(lines[0])] * 2 + lines + [up_sums[0].reshape(scenes, LATS, 2 * shard)]
    lines = jnp.concatenate(lines, axis=2)
    lines = jnp.pad(lines, ((0, 0), (0, 0), (0, OWN - 8 * shard)))
    cols = jnp.broadcast_to(query_sums[:2], (scenes, 2, OWN))
    late = scatter_scene(jnp.concatenate([trio.astype(F32), cols, lines], axis=1))
    mats = [late[i * block : (i + 1) * block].reshape(LATS, shard, OWN) for i in range(3)]
    mats += [feed_part[i * block : (i + 1) * block].reshape(LATS, shard, OWN) for i in range(3)]
    mats.append(feed_part[3 * block :].reshape(LATS, 2 * shard, OWN))
    cols = jnp.pad(late[3 * block : 3 * block + 2], ((0, 6), (0, 0)))
    mats.append(jnp.broadcast_to(cols, (LATS, 8, OWN)))
    lines = late[3 * block + 2 :].reshape(LATS, 1, OWN)
    mats.append(jnp.broadcast_to(lines, (LATS, 24, OWN)))
    final = jnp.concatenate(mats, axis=1).astype(BF)
    half = final.shape[1] // 2
    final = jnp.concatenate([final[:, :half], final[:, half:]], axis=2)
    sent = [lax.dynamic_index_in_dim(final, lat ^ k, 0, keepdims=False) for k in range(LATS)]
    return [sent[0]] + [swap(sent[k], "lat", k) for k in range(1, LATS)]


def solution(mesh):
    rows = P(("scene", "lat"), None)
    line = P(("scene", "lat"))
    scene = P("scene", None)
    in_specs = (scene, rows, P("scene"), scene, scene) + (rows,) * 6 + (line,) * 7
    out_specs = (scene, scene, rows) + (rows,) * 6 + (line,) * 7
    return jax.shard_map(body, mesh=mesh, in_specs=in_specs, out_specs=out_specs, check_vma=False)
```

```python
import math
from functools import partial

import jax
import jax.numpy as jnp
from jax import lax
from jax.experimental import pallas as pl
from jax.experimental.pallas import tpu as pltpu
from jax.sharding import PartitionSpec as P

HEADS = 12
HEAD_DIM = 64
VIEWS = 10
VIEW_TOK = 300
LANES = 128
LATS = 4
OWN_HEADS = HEADS // LATS
OWN = OWN_HEADS * HEAD_DIM
DEAD = -1e30
LOG2E = math.log2(math.e)
Q_SCALE = 0.125 * LOG2E
ROOT = math.sqrt(2.0 / math.pi)
SCALE = 1.0
VMEM_BYTES = 63 * 2**20
BF = jnp.bfloat16
F32 = jnp.float32


def dot(left, right):
    return jnp.dot(left, right, preferred_element_type=F32)


def dot_rt(left, right):
    return lax.dot_general(left, right, (((1,), (1,)), ((), ())), preferred_element_type=F32)


def dot_lt(left, right):
    return lax.dot_general(left, right, (((0,), (0,)), ((), ())), preferred_element_type=F32)


def params():
    return pltpu.CompilerParams(vmem_limit_bytes=VMEM_BYTES)


def cost(micros):
    return pl.CostEstimate(
        flops=int(micros * SCALE * 1e9), bytes_accessed=int(micros * SCALE * 3.3e6), transcendentals=0
    )


def vmem(count):
    return [pl.BlockSpec(memory_space=pltpu.VMEM)] * count


ANY = pl.BlockSpec(memory_space=pl.ANY)
SMEM = pl.BlockSpec(memory_space=pltpu.SMEM)


def shape(dims, dtype=BF):
    return jax.ShapeDtypeStruct(tuple(dims), dtype)


def norm_parts(values):
    center = values - jnp.mean(values, axis=-1, keepdims=True)
    spread = jnp.mean(center * center, axis=-1, keepdims=True)
    factor = lax.rsqrt(spread + 1e-05)
    return center * factor, factor


def norm_back(grad_out, normed, factor, gain_row):
    scaled = grad_out * gain_row
    return factor * (
        scaled
        - jnp.mean(scaled, axis=-1, keepdims=True)
        - normed * jnp.mean(scaled * normed, axis=-1, keepdims=True)
    )


def swap(values, axis, step):
    count = lax.axis_size(axis)
    return lax.ppermute(values, axis, [(i, i ^ step) for i in range(count)])


def stages(count):
    found, stride = [], count
    while stride > 1:
        group = 4 if stride % 4 == 0 else 2
        stride //= group
        found.append((stride, group))
    return found


def collect_kernel(count, *refs):
    out, rows = refs[-1], 0
    for ref in refs[:count]:
        out[rows : rows + ref.shape[0]] = ref[...]
        rows += ref.shape[0]


def collect(values, after):
    rows = sum(v.shape[0] for v in values)
    return pl.pallas_call(
        partial(collect_kernel, len(values)),
        out_shape=shape((rows,) + values[0].shape[1:]),
        in_specs=vmem(len(values)) + [ANY] * len(after),
        out_specs=pl.BlockSpec(memory_space=pltpu.VMEM),
        compiler_params=params(),
        cost_estimate=cost(0.3),
        name="collect",
    )(*values, *after)


def gather_scene(parts, after=()):
    steps = [0]
    got = [parts]
    passed = []
    for stride, group in stages(lax.axis_size("scene")):
        if len(got) == 1:
            parts = got[0]
        else:
            parts = collect(got, after) if after else jnp.concatenate(got)
        got = [parts] + [swap(parts, "scene", k * stride) for k in range(1, group)]
        steps = [step ^ (k * stride) for k in range(group) for step in steps]
        passed = [parts]
    return got, steps, passed


def in_order(stacked, steps, me):
    places = [steps.index(i) for i in range(len(steps))]
    order = jnp.take(jnp.array(places, jnp.int32), jnp.arange(len(steps)) ^ me)
    return jnp.take(stacked, order, axis=0)


def scatter_scene(blocks):
    count = lax.axis_size("scene")
    me = lax.axis_index("scene")
    held = blocks
    for stride, group in reversed(stages(count)):
        digit = (me // stride) % group
        view = held.reshape((-1, group) + blocks.shape[1:])
        total = lax.dynamic_index_in_dim(view, digit, 1, keepdims=False).astype(F32)
        for k in range(1, group):
            mine = lax.dynamic_index_in_dim(view, digit ^ k, 1, keepdims=False)
            total = total + swap(mine.astype(BF), "scene", k * stride).astype(F32)
        held = total.astype(BF)
    return total.reshape(blocks.shape[1:])


def fold(rows):
    half = rows.shape[0] // 2
    return jnp.concatenate([rows[:half], rows[half:]], axis=1)


def unfold(rows):
    half = rows.shape[1] // 2
    return jnp.concatenate([rows[:, :half], rows[:, half:]], axis=0)


def choose(index, options):
    picked = options[0]
    for i in range(1, len(options)):
        picked = jnp.where(index == i, options[i], picked)
    return picked


def pack_kernel(where, w_query, w_key, w_value, *refs):
    vectors, out = refs[:-LATS], refs[-LATS:]
    values = [w[...].astype(F32) for w in (w_query, w_key, w_value)]
    line = [v[...].astype(F32).reshape(1, v.shape[0]) for v in vectors]
    line = jnp.concatenate(line, axis=1)
    line = jnp.concatenate([line, jnp.zeros((1, OWN - line.shape[1]), F32)], axis=1) if (
        line.shape[1] < OWN
    ) else line
    tail = jnp.broadcast_to(line, (8, OWN))
    for k in range(LATS):
        target = where[0] ^ k
        rows = []
        for value in values:
            cols = [value[:, p * OWN : (p + 1) * OWN] for p in range(LATS)]
            rows.append(choose(target, cols))
        out[k][...] = fold(jnp.concatenate(rows + [tail], axis=0)).astype(BF)


def pack(where, w_query, w_key, w_value, vectors):
    rows = 3 * w_query.shape[0] + 8
    return pl.pallas_call(
        pack_kernel,
        out_shape=[shape((rows // 2, 2 * OWN))] * LATS,
        in_specs=[SMEM] + vmem(3 + len(vectors)),
        out_specs=vmem(LATS),
        compiler_params=params(),
        cost_estimate=cost(0.5),
        name="pack",
    )(where, w_query, w_key, w_value, *vectors)


def unpack_kernel(steps, where, *refs):
    *chunks, trio, turned, rows_out, up_out, held, lines = refs
    lat, scene = where[0], where[3]
    shard = held.shape[1] // (len(steps) * LATS)
    entry = 0
    for chunk in chunks:
        for p in range(chunk.shape[0]):
            values = unfold(chunk[p].astype(F32))
            source = (scene ^ steps[entry // LATS]) * LATS + (lat ^ (entry % LATS))
            at = pl.ds(pl.multiple_of(source * shard, 8), shard)
            for m in range(3):
                held[m, at, :] = values[m * shard : (m + 1) * shard]
            lines[pl.ds(source, 1), :] = values[3 * shard : 3 * shard + 1]
            entry += 1
    for m in range(3):
        low = held[m].astype(BF)
        trio[m] = low
        turned[m] = held[m].T.astype(BF)
    sources = lines.shape[0]
    low = lines[...].astype(BF)
    for target, size, first in ((rows_out, shard, 0), (up_out, 2 * shard, 6)):
        wide = target.shape[1]
        col = lax.broadcasted_iota(jnp.int32, (1, wide), 1).astype(F32)
        owner = jnp.floor((col + 0.5) * (1.0 / size))
        spot = col - owner * size
        row = lax.broadcasted_iota(jnp.int32, (OWN, 1), 0).astype(F32)
        line = lax.broadcasted_iota(jnp.int32, (sources, 1), 0).astype(F32)
        for v in range(6 if first == 0 else 1):
            hot = jnp.where(row == spot + (first + v) * shard, 1.0, 0.0).astype(BF)
            spread = jnp.where(line == owner, dot(low, hot), 0.0)
            target[v : v + 1, :] = jnp.sum(spread, axis=0, keepdims=True)


def unpack(where, chunks, steps, shard):
    sources = len(steps) * LATS
    width = sources * shard
    return pl.pallas_call(
        partial(unpack_kernel, steps),
        out_shape=[
            shape((3, width, OWN)),
            shape((3, OWN, width)),
            shape((8, width), F32),
            shape((1, 2 * width), F32),
        ],
        in_specs=[SMEM] + vmem(len(chunks)),
        out_specs=vmem(4),
        scratch_shapes=[pltpu.VMEM((3, width, OWN), F32), pltpu.VMEM((sources, OWN), F32)],
        compiler_params=params(),
        cost_estimate=cost(0.5),
        name="unpack",
    )(where, *chunks)


def attention_weights(where, w_query, w_key, w_value, vectors, latents, lat_pad):
    shard, width = w_query.shape
    if shard % 8 == 0:
        pieces = pack(where, w_query, w_key, w_value, vectors)
        pieces = [pieces[0]] + [swap(pieces[k], "lat", k) for k in range(1, LATS)]
        own_lat = pad_latents(latents, lat_pad, pieces[2:])
        stacked = collect([p[None] for p in pieces], ())
        chunks, steps, passed = gather_scene(stacked, [own_lat])
        return unpack(where, chunks, steps, shard), own_lat, [stacked] + passed
    flat = jnp.concatenate(vectors)
    flat = jnp.pad(flat, (0, OWN - flat.shape[0])).reshape(1, OWN)
    lat, scene = lax.axis_index("lat"), lax.axis_index("scene")
    scenes = lax.axis_size("scene")
    trio = jnp.stack([w_query, w_key, w_value]).reshape(3, shard, LATS, OWN)
    trio = jnp.transpose(trio, (2, 0, 1, 3)).reshape(LATS, 3 * shard, OWN)
    message = jnp.concatenate([trio, jnp.broadcast_to(flat, (LATS, 1, OWN))], axis=1)
    pieces = [lax.dynamic_index_in_dim(message, lat ^ k, 0, keepdims=False) for k in range(LATS)]
    pieces = [pieces[0]] + [swap(pieces[k], "lat", k) for k in range(1, LATS)]
    pieces = in_order(jnp.stack(pieces), list(range(LATS)), lat)
    chunks, steps, passed = gather_scene(pieces[None])
    gathered = in_order(jnp.concatenate(chunks), steps, scene)
    trio = gathered[:, :, : 3 * shard].reshape(scenes, LATS, 3, shard, OWN)
    trio = jnp.transpose(trio, (2, 0, 1, 3, 4)).reshape(3, width, OWN)
    lines = gathered[:, :, 3 * shard, : 8 * shard].astype(F32).reshape(scenes * LATS, 8, shard)
    rows = jnp.transpose(lines, (1, 0, 2)).reshape(8, width)
    up = lines[:, 6:].reshape(1, 2 * width)
    own_lat = pad_latents(latents, lat_pad, [])
    return (trio, jnp.transpose(trio, (0, 2, 1)), rows, up), own_lat, []


def gate_kernel(*refs):
    pass


def gate(values, after):
    one = not isinstance(values, list)
    values = [values] if one else values
    out = pl.pallas_call(
        gate_kernel,
        out_shape=[shape(v.shape, v.dtype) for v in values],
        in_specs=[ANY] * (len(values) + len(after)),
        out_specs=[ANY] * len(values),
        input_output_aliases={i: i for i in range(len(values))},
        compiler_params=params(),
        cost_estimate=cost(0.2),
        name="gate",
    )(*values, *after)
    return out[0] if one else list(out)


def pad_kernel(latents, *refs):
    out = refs[-1]
    rows = latents.shape[0]
    out[:rows, :] = latents[...]
    out[rows:, :] = jnp.zeros((out.shape[0] - rows, out.shape[1]), out.dtype)


def pad_latents(latents, rows, after):
    return pl.pallas_call(
        pad_kernel,
        out_shape=shape((rows, latents.shape[1])),
        in_specs=vmem(1) + [ANY] * len(after),
        out_specs=pl.BlockSpec(memory_space=pltpu.VMEM),
        compiler_params=params(),
        cost_estimate=cost(0.5),
        name="pad_latents",
    )(latents, *after)


def pack_feed_kernel(w_out, w_up, w_down, *refs):
    out = refs[-1]
    shard, width = w_out.shape
    out[: 2 * shard, :] = w_down[...]
    out[2 * shard : 3 * shard, :] = w_out[...]
    out[3 * shard : 4 * shard, :] = w_up[:, :width]
    out[4 * shard :, :] = w_up[:, width:]


def pack_feed(w_out, w_up, w_down, after):
    shard, width = w_out.shape
    return pl.pallas_call(
        pack_feed_kernel,
        out_shape=shape((5 * shard, width)),
        in_specs=vmem(3) + [ANY] * len(after),
        out_specs=pl.BlockSpec(memory_space=pltpu.VMEM),
        compiler_params=params(),
        cost_estimate=cost(0.3),
        name="pack_feed",
    )(w_out, w_up, w_down, *after)


def feed_weights(w_out, w_up, w_down, after):
    if w_out.shape[0] % 8 == 0:
        packed = gate(pack_feed(w_out, w_up, w_down, after[:1]), after[1:])
        return lax.all_gather(packed, ("scene", "lat"), axis=0, tiled=False)
    width = w_out.shape[1]
    packed = jnp.concatenate([w_down, w_out, w_up[:, :width], w_up[:, width:]], axis=0)
    held = lax.all_gather(packed, ("scene", "lat"), axis=0, tiled=False)
    shard = w_out.shape[0]
    parts = [held[:, : 2 * shard].reshape(2 * width, width)]
    parts += [held[:, n * shard : (n + 1) * shard].reshape(width, width) for n in range(2, 5)]
    return jnp.concatenate(parts, axis=0)


def widen(weight):
    gap = jnp.zeros((weight.shape[0], 2 * LANES - OWN), weight.dtype)
    return jnp.concatenate([weight, gap], axis=1)


def own_lanes(head, axis):
    spot = lax.broadcasted_iota(jnp.int32, (1, LANES) if axis == 1 else (LANES, 1), axis)
    first = (head % 2) * HEAD_DIM
    return (spot >= first) & (spot < first + HEAD_DIM), spot, HEAD_DIM - first


def lane_block(values, head):
    return values[:, (head // 2) * LANES : (head // 2 + 1) * LANES]


def query_kernel(where, rays, weight, rows_in, normed_low, query, wide):
    @pl.when(pl.program_id(0) == 0)
    def _():
        wide[...] = widen(weight[0])

    normed, _ = norm_parts(rays[...].astype(F32))
    normed_low[...] = normed.astype(BF)
    low = (normed * rows_in[0:1, :] + rows_in[1:2, :]).astype(BF)
    values = dot(low, wide[...]) * Q_SCALE
    for h in range(OWN_HEADS):
        own, lane, spare = own_lanes(h, 1)
        one = jnp.where(lane == spare, 1.0, 0.0)
        query[h] = jnp.where(own, lane_block(values, h), one).astype(BF)


def make_queries(where, rays, trio, rows_in):
    count, width = rays.shape
    block = count // 4
    whole = lambda a: pl.BlockSpec(a.shape, lambda i, w: (0,) * a.ndim)
    return pl.pallas_call(
        query_kernel,
        grid_spec=pltpu.PrefetchScalarGridSpec(
            num_scalar_prefetch=1,
            grid=(4,),
            in_specs=[
                pl.BlockSpec((block, width), lambda i, w: (i ^ (2 * w[1]), 0)),
                pl.BlockSpec((1,) + trio.shape[1:], lambda i, w: (0, 0, 0)),
                whole(rows_in),
            ],
            out_specs=[
                pl.BlockSpec((block, width), lambda i, w: (i, 0)),
                pl.BlockSpec((OWN_HEADS, block, LANES), lambda i, w: (0, i, 0)),
            ],
            scratch_shapes=[pltpu.VMEM((width, 2 * LANES), BF)],
        ),
        out_shape=[
            shape((count, width)),
            shape((OWN_HEADS, count, LANES)),
        ],
        compiler_params=params(),
        cost_estimate=cost(2),
        name="queries",
    )(where, rays, trio, rows_in)


def keyset_kernel(lat_a, lat_b, trio, shut, *refs):
    key, key_t, val, val_t, wide, here = refs[-6:]
    step = pl.program_id(0)

    @pl.when(step == 0)
    def _():
        wide[0] = widen(trio[1])
        wide[1] = widen(trio[2])

    for j, lat in enumerate((lat_a, lat_b)):

        @pl.when(step == j)
        def _():
            here[...] = lat[...]

    keys = dot(here[...], wide[0])
    vals = dot(here[...], wide[1])
    blocks = lambda v: [v[:, i * LANES : (i + 1) * LANES].T for i in range(2)]
    keys_t, vals_t = blocks(keys), blocks(vals)
    for h in range(OWN_HEADS):
        own, _, _ = own_lanes(h, 1)
        own_line, line, spare = own_lanes(h, 0)
        key[h] = jnp.where(own, lane_block(keys, h), 0.0).astype(BF)
        val[h] = jnp.where(own, lane_block(vals, h), 1.0).astype(BF)
        mask = jnp.where(line == spare, shut[0], 0.0)
        key_t[h] = jnp.where(own_line, keys_t[h // 2], mask).astype(BF)
        val_t[h] = jnp.where(own_line, vals_t[h // 2], 1.0).astype(BF)


def make_keyset(pair, lats, trio, shut, held=None):
    rows, width = lats[0].shape
    total = LATS * rows
    tall, long = shape((OWN_HEADS, total, LANES)), shape((OWN_HEADS, LANES, total))
    whole = lambda a: pl.BlockSpec(a.shape, lambda i: (0,) * a.ndim)
    down = pl.BlockSpec((OWN_HEADS, rows, LANES), lambda i: (0, 2 * pair + i, 0))
    over = pl.BlockSpec((OWN_HEADS, LANES, rows), lambda i: (0, 0, 2 * pair + i))
    extra = [] if held is None else list(held)
    return pl.pallas_call(
        keyset_kernel,
        grid=(2,),
        out_shape=[tall, long, tall, long],
        in_specs=[whole(lat) for lat in lats]
        + [whole(trio), pl.BlockSpec((1, 1, rows), lambda i: (2 * pair + i, 0, 0))]
        + [ANY] * len(extra),
        out_specs=[down, over, down, over],
        scratch_shapes=[pltpu.VMEM((2, width, 2 * LANES), BF), pltpu.VMEM((rows, width), BF)],
        input_output_aliases={4 + i: i for i in range(len(extra))},
        compiler_params=params(),
        cost_estimate=cost(5),
        name="keyset",
    )(*lats, trio, shut, *extra)


def attend_kernel(sub, query, key_t, val, *rest):
    context, native, weights, inverse, mixed = rest[-5:]
    head, part = pl.program_id(0), pl.program_id(1)
    rows = query.shape[1]
    own, _, _ = own_lanes(head, 1)
    spot = part * 2 + head // 2

    def score(i):
        return dot(query[0, i * sub : (i + 1) * sub, :], key_t[0])

    scores = score(0)
    for i in range(rows // sub):
        later = score(i + 1) if i + 1 < rows // sub else None
        at = slice(i * sub, (i + 1) * sub)
        low = jnp.exp2(scores - jnp.max(scores, axis=1, keepdims=True)).astype(BF)
        weights[0, at, :] = low
        summed = dot(low, val[0])
        scale = 1.0 / jnp.where(own, pltpu.roll(summed, HEAD_DIM, 1), summed)
        held = jnp.where(head == 1, mixed[spot, at, :], 0.0)
        mixed[spot, at, :] = jnp.where(own, summed * scale, held)
        inverse[0, at, :] = scale
        scores = later

    for p in range(2):

        @pl.when((head == OWN_HEADS - 1) & (part == p))
        def _():
            both = jnp.concatenate([mixed[2 * p], mixed[2 * p + 1]], axis=1).astype(BF)
            native[p * rows : (p + 1) * rows, :] = both
            context[:, p * OWN : (p + 1) * OWN] = both[:, :OWN]


def attend(half_index, query, key_t, val, held=None, after=()):
    _, count, _ = query.shape
    total = key_t.shape[2]
    half = count // 2
    block = half // 2
    sub = block // 3 if block % 48 == 0 else block
    rows = lambda cols: pl.BlockSpec((1, block, cols), lambda h, b: (h, 2 * half_index + b, 0))
    every = lambda rows, cols: pl.BlockSpec((1, rows, cols), lambda h, b: (h, 0, 0))
    extra = ([] if held is None else list(held)) + list(after)
    return pl.pallas_call(
        partial(attend_kernel, sub),
        grid=(OWN_HEADS, 2),
        in_specs=[rows(LANES), every(LANES, total), every(total, LANES)] + [ANY] * len(extra),
        out_specs=[
            pl.BlockSpec((block, 2 * OWN), lambda h, b: (0, 0)),
            pl.BlockSpec((half, 2 * LANES), lambda h, b: (0, 0)),
            rows(total),
            rows(LANES),
        ],
        out_shape=[
            shape((block, 2 * OWN)),
            shape((half, 2 * LANES)),
            shape((OWN_HEADS, count, total)),
            shape((OWN_HEADS, count, LANES), F32),
        ],
        scratch_shapes=[pltpu.VMEM((4, block, LANES), F32)],
        input_output_aliases={} if held is None else {3: 2, 4: 3},
        compiler_params=params(),
        cost_estimate=cost(16),
        name="attend",
    )(query, key_t, val, *extra)


def back_kernel(sub, lat_rows, head, fine, weights, inverse, *refs):
    d_here, d_there, ctx_here, ctx_there, query, key, val_t = refs[:7]
    refs = refs[7:]
    lats, normed_low, earlier, where, refs = refs[:LATS], refs[LATS], refs[5], refs[6], refs[7:]
    messages = LATS
    *out, sums, d_query, lat_here, normed_here, sem = refs[-(messages + 7) :] if (
        fine and head > 0
    ) else refs[-(messages + 6) :]
    grads_out = out[messages:]
    pair_out, query_out = out[:LATS], out[messages - LATS : messages]
    query_at = 2 * lat_rows
    step = pl.program_id(0)
    rows = weights.shape[1]
    half = 2 * rows
    start = pl.multiple_of((step % 2) * rows, rows)
    loads = [
        pltpu.make_async_copy(lat, lat_here.at[pl.ds(j * lat_rows, lat_rows)], sem.at[j])
        for j, lat in enumerate(lats)
    ]
    loads.append(pltpu.make_async_copy(normed_low, normed_here, sem.at[LATS]))

    @pl.when(step == 0)
    def _():
        for load in loads:
            load.start()

    own, lane, spare = own_lanes(head, 1)
    far = step >= 2
    upstream = jnp.where(far, d_there[...], d_here[...]).astype(F32)
    ctx = jnp.where(far, ctx_there[...], ctx_here[...]).astype(F32)
    scale = inverse[0]
    delta = jnp.sum(jnp.where(own, upstream * ctx, 0.0), axis=1, keepdims=True) * scale
    high = delta.astype(BF).astype(F32)
    rest = jnp.where(lane == spare + 1, high - delta, 0.0)
    rest = jnp.where(lane == spare, -high, rest)
    grad = jnp.where(own, upstream * scale, rest).astype(BF)
    val_part = dot_lt(grad, weights[0])
    found = []
    for i in range(rows // sub):
        at = slice(i * sub, (i + 1) * sub)
        d_weights = dot(grad[at], val_t[0])
        d_scores = (weights[0, at, :].astype(F32) * d_weights).astype(BF)
        d_query[pl.ds(start + i * sub, sub), :] = dot(d_scores, key[0]) * 0.125
        found.append(d_scores)
    d_scores = jnp.concatenate(found, axis=0) if len(found) > 1 else found[0]
    key_part = dot_lt(query[0], d_scores) * (1.0 / LOG2E)

    @pl.when(step == 0)
    def _():
        sums[0] = key_part
        sums[1] = val_part

    @pl.when(step > 0)
    def _():
        sums[0] += key_part
        sums[1] += val_part

    first = (head % 2) * HEAD_DIM

    @pl.when(step == 3)
    def _():
        for i in range(2):
            total = sums[i, first : first + HEAD_DIM].astype(BF)
            for j in range(LATS):
                pair_out[j][:, i * lat_rows : (i + 1) * lat_rows] = total[
                    :, j * lat_rows : (j + 1) * lat_rows
                ]

    for last in (1, 3):

        @pl.when(step == last)
        def _():
            turned = d_query[...].T[first : first + HEAD_DIM].astype(BF)
            for j in (last // 2, last // 2 + 2):
                query_out[j][:, query_at : query_at + half] = turned

    @pl.when(step == 3)
    def _():
        for load in loads:
            load.wait()
        turned = [query_out[b][:, query_at : query_at + half] for b in range(2)]
        part = dot(turned[0], normed_here[:half]) + dot(turned[1], normed_here[half:])
        both = [sums[i, first : first + HEAD_DIM] for i in range(2)]
        both = dot(jnp.concatenate(both, axis=0).astype(BF), lat_here[...])
        parts = [part, both[:HEAD_DIM], both[HEAD_DIM:]]
        col = sum(jnp.sum(t.astype(F32), axis=1, keepdims=True) for t in turned)
        high = col.astype(BF).astype(F32)
        col = jnp.where(lane == 0, high, jnp.where(lane == 1, col - high, 0.0)).T[:16]
        parts = [p.T for p in parts] + [col]
        if head == 0 or not fine:
            grads_out[0][...] = jnp.concatenate(parts, axis=0)
            return
        send, keep = grads_out
        scenes = 2 * send.shape[0]
        width = normed_here.shape[1]
        block = width // scenes
        if head == 1:
            parts = [
                jnp.concatenate([earlier[i * width : i * width + p.shape[0]], p], axis=1)
                for i, p in enumerate(parts)
            ]
        for s in range(scenes):
            mine = [p[s * block : (s + 1) * block] for p in parts[:3]] + parts[3:]
            if head == 2:
                mine = fold(jnp.concatenate(mine + [jnp.zeros((16, HEAD_DIM), F32)], axis=0))
            else:
                mine = jnp.concatenate(mine, axis=0)
            mine = mine.astype(BF)
            kept = where[4] == s % 2

            @pl.when(kept)
            def _():
                keep[s // 2] = mine

            @pl.when(jnp.logical_not(kept))
            def _():
                send[s // 2] = mine


def attend_back(head, fine, weights, inverse, d_ctxs, ctxs, query, key, val_t, lats, normed_low, earlier, where, after):
    _, count, total = weights.shape
    rows = count // 4
    sub = rows // 2 if rows % 32 == 0 else rows
    lat_rows = total // LATS
    width = normed_low.shape[1]
    pad = lambda n: -(-n // LANES) * LANES
    outs = [shape((HEAD_DIM, pad(2 * lat_rows + 2 * rows)))] * LATS
    if head == 0 or not fine:
        outs.append(shape((3 * width + 16, HEAD_DIM), F32))
    else:
        block = 3 * (width // 8)
        dims = (4, block + 16, LANES) if head == 1 else (4, block // 2 + 16, LANES)
        outs += [shape(dims)] * 2
    of_head = lambda cols: pl.BlockSpec((1, rows, cols), lambda b: (head, b, 0))
    here = pl.BlockSpec((rows, LANES), lambda b: (jnp.minimum(b, 1), head // 2))
    there = pl.BlockSpec((rows, LANES), lambda b: (jnp.maximum(b, 2) - 2, head // 2))
    whole = lambda a: pl.BlockSpec(a.shape, lambda b: (0,) * len(a.shape))
    early = whole(earlier) if head == 1 and fine else ANY
    return pl.pallas_call(
        partial(back_kernel, sub, lat_rows, head, fine),
        grid=(4,),
        in_specs=[
            of_head(total),
            of_head(LANES),
            here,
            there,
            here,
            there,
            of_head(LANES),
            pl.BlockSpec((1, total, LANES), lambda b: (head, 0, 0)),
            pl.BlockSpec((1, LANES, total), lambda b: (head, 0, 0)),
        ]
        + [ANY] * (LATS + 1)
        + [early, SMEM]
        + [ANY] * len(after),
        out_specs=[whole(o) for o in outs],
        out_shape=outs,
        scratch_shapes=[
            pltpu.VMEM((2, LANES, total), F32),
            pltpu.VMEM((2 * rows, LANES), F32),
            pltpu.VMEM((total, width), BF),
            pltpu.VMEM((count, width), BF),
            pltpu.SemaphoreType.DMA((LATS + 1,)),
        ],
        compiler_params=params(),
        cost_estimate=cost(14),
        name=f"attend_back_{head}",
    )(weights, inverse, *d_ctxs, *ctxs, query, key, val_t, *lats, normed_low, earlier, where, *after)


def quarter_halves(values, core):
    mid = values.shape[1] // 2
    low, high = values[:, :mid], values[:, mid:]
    return jnp.where(core == 0, low, high), jnp.where(core == 0, high, low)


def feed_kernel(fine, where, *refs):
    ins, rows_in, up_shift = refs[:7], refs[7], refs[8]
    layer_out, layer_half, d_middle, d_own, d_sibling = refs[9:14]
    grads_out = refs[14:-16]
    held, rays, ctxs, upstream, w_out, w_up, w_down, low_out, low_mid, own, sibling = refs[-16:-5]
    halves, active, lifted, sem_in, sem_out = refs[-5:]
    lat, core, side = where[0], where[1], where[2]
    half, width = rays.shape
    hidden = w_up.shape[1]
    block = half // 4
    mine = pl.ds(pl.multiple_of(core * half, half), half)
    sources = [ins[6], ins[0].at[mine]] + list(ins[1:5]) + [ins[5].at[mine]]
    targets = [held, rays] + [ctxs.at[j] for j in range(LATS)] + [upstream]
    loads = [
        pltpu.make_async_copy(a, b, sem_in.at[n]) for n, (a, b) in enumerate(zip(sources, targets))
    ]
    stores = []

    def store(source, target):
        stores.append(pltpu.make_async_copy(source, target, sem_out.at[len(stores)]))
        stores[-1].start()

    for load in loads:
        load.start()
    for load in loads[:6]:
        load.wait()
    if held.ndim == 3:
        shard = held.shape[1] // 5
        piece = lambda n, count=1: held[:, n * shard : (n + count) * shard, :]
    else:
        piece = lambda n, count=1: held[n * width : (n + count) * width, :]
    w_out[...] = piece(2).reshape(width, width)
    w_up[:, :width] = piece(3).reshape(width, width)
    w_up[:, width:] = piece(4).reshape(width, width)
    w_down[...] = piece(0, 2).reshape(hidden, width)
    gain, bias = rows_in[2:3, :], rows_in[3:4, :]
    spots = [pl.ds(pl.multiple_of((lat ^ j) * OWN, OWN), OWN) for j in range(LATS)]

    def ctx_rows(j, i):
        at = slice((i % 2) * block, (i % 2 + 1) * block)
        return ctxs[j, at, (i // 2) * OWN : (i // 2 + 1) * OWN]

    begun = []
    for i in range(4):
        at = slice(i * block, (i + 1) * block)
        middle = rays[at, :].astype(F32) + rows_in[4:5, :]
        for j in range(LATS):
            middle = middle + dot(ctx_rows(j, i), w_out[spots[j], :])
        normed, factor = norm_parts(middle)
        lifted[at, :] = (normed * gain + bias).astype(BF)
        begun.append((middle, normed, factor))
    for load in loads[6:]:
        load.wait()
    column = lambda v: jnp.sum(v, axis=0, keepdims=True)
    sums, up_sums = [0.0] * 4, 0.0
    for i in range(4):
        at = slice(i * block, (i + 1) * block)
        middle, normed, factor = begun[i]
        before = dot(lifted[at, :], w_up[...]) + up_shift[...]
        squared = before * before
        bent = jnp.tanh(before * (ROOT + (ROOT * 0.044715) * squared))
        scaled = 0.5 * before
        act = (scaled + scaled * bent).astype(BF)
        active[at, :] = act
        slope = 0.5 + 0.5 * bent + scaled * (1.0 - bent * bent) * (
            ROOT + (3 * 0.044715 * ROOT) * squared
        )
        d_pre = (dot_rt(upstream[at, :], w_down[...]) * slope).astype(BF)
        halves[at, :hidden] = d_pre
        low_out[at, :] = (middle + dot(act, w_down[...]) + rows_in[5:6, :]).astype(BF)
        d_lifted = dot_rt(d_pre, w_up[...])
        up_wide = upstream[at, :].astype(F32)
        d_mid = up_wide + norm_back(d_lifted, normed, factor, gain)
        branch = d_mid.astype(BF)
        low_mid[at, :] = branch
        halves[at, hidden:] = branch
        gap = jnp.zeros((block, 2 * LANES - OWN), F32)
        for target, spot in zip((own, sibling), spots):
            part = dot_rt(branch, w_out[spot, :])
            target[at, :] = jnp.concatenate([part, gap], axis=1).astype(BF)
        pieces = (d_lifted * normed, d_lifted, branch.astype(F32), up_wide)
        sums = [total + column(piece) for total, piece in zip(sums, pieces)]
        up_sums = up_sums + column(d_pre.astype(F32))
    store(sibling, d_sibling)
    store(own, d_own)
    store(low_out, layer_half)
    store(low_out, layer_out.at[mine])
    store(low_mid, d_middle)

    wide, narrow = hidden // 2, width // 2
    pre_half = halves[:, pl.ds(pl.multiple_of(side * wide, LANES), wide)]
    branch_half = halves[:, pl.ds(pl.multiple_of(hidden + side * narrow, LANES), narrow)]
    up_half = upstream[:, pl.ds(pl.multiple_of(side * narrow, LANES), narrow)]
    up_grad = dot_lt(lifted[...], pre_half)
    down_grad = dot_lt(active[...], up_half)
    if fine:
        messages = grads_out[2:]
        scenes = messages[0].shape[0]
        shard = width // (scenes * LATS)

        def parities(values, rows):
            parts = [values[n * rows : (n + 1) * rows] for n in range(LATS)]
            even = jnp.concatenate([parts[0], parts[2]], axis=0)
            odd = jnp.concatenate([parts[1], parts[3]], axis=0)
            first, second = jnp.where(core == 0, even, odd), jnp.where(core == 0, odd, even)
            return zip(messages, (first.astype(BF), second.astype(BF)))

        for s in range(scenes):
            rows = LATS * shard
            for message, part in parities(up_grad[s * rows : (s + 1) * rows], shard):
                message[s, 2 * shard : 4 * shard, :] = part[:, :narrow]
                message[s, 4 * shard : 6 * shard, :] = part[:, narrow:]
            rows = 2 * LATS * shard
            for message, part in parities(down_grad[s * rows : (s + 1) * rows], 2 * shard):
                message[s, 6 * shard : 10 * shard, :] = part
        for j in range(LATS):
            ctx = jnp.concatenate([ctxs[j, :, :OWN], ctxs[j, :, OWN:]], axis=0)
            values = dot_lt(ctx, branch_half)
            rows = LATS * shard
            for q in range(OWN // rows):
                place = (lat ^ j) * (OWN // rows) + q
                for message, part in parities(values[q * rows : (q + 1) * rows], shard):
                    message[place, : 2 * shard, :] = part
        lines = line_up(sums, up_sums, scenes * LATS)
        for s in range(scenes):
            line = lines[s * LATS : (s + 1) * LATS]
            even = jnp.concatenate([line[0:1], line[2:3]], axis=0)
            odd = jnp.concatenate([line[1:2], line[3:4]], axis=0)
            for n, message in enumerate(messages):
                rows = jnp.where(core == n, even, odd)
                rows = jnp.concatenate([rows, jnp.zeros((14, OWN), F32)], axis=0)
                rows = jnp.concatenate([rows, jnp.zeros_like(rows)], axis=1)
                message[s, 10 * shard :, :] = rows.astype(BF)
        for message, target in zip(messages, grads_out):
            store(message, target)
    else:
        for i, part in ((1, up_grad), (2, down_grad)):
            first, second = quarter_halves(part, core)
            grads_out[2 * i][...] = first.astype(BF)
            grads_out[2 * i + 1][...] = second.astype(BF)
        for j in range(LATS):
            ctx = jnp.concatenate([ctxs[j, :, :OWN], ctxs[j, :, OWN:]], axis=0)
            first, second = quarter_halves(dot_lt(ctx, branch_half), core)
            grads_out[0][spots[j], :] = first.astype(BF)
            grads_out[1][spots[j], :] = second.astype(BF)
        grads_out[6][...] = jnp.concatenate(sums + [jnp.zeros((4, width), F32)], axis=0)
        grads_out[7][...] = jnp.broadcast_to(up_sums, (8, hidden))
    for copy in stores:
        copy.wait()


def line_up(sums, up_sums, sources):
    total = None
    shard = sums[0].shape[1] // sources
    for rows, size, first in ((sums, shard, 2), ([up_sums], 2 * shard, 6)):
        wide = rows[0].shape[1]
        col = lax.broadcasted_iota(jnp.int32, (1, wide), 1).astype(F32)
        owner = jnp.floor((col + 0.5) * (1.0 / size))
        spot = (col - owner * size)
        row = lax.broadcasted_iota(jnp.int32, (OWN, 1), 0).astype(F32)
        line = lax.broadcasted_iota(jnp.int32, (sources, 1), 0).astype(F32)
        for v, values in enumerate(rows):
            hot = jnp.where(row == spot + (first + v) * shard, 1.0, 0.0).astype(BF)
            mine = jnp.where(line == owner, values, 0.0).astype(BF)
            part = dot_rt(mine, hot)
            total = part if total is None else total + part
    return total


def feed(where, rays, ctxs, upstream, weights, rows_in, up_shift, scenes, fine):
    count, width = rays.shape
    hidden = up_shift.shape[1]
    half = count // 2
    mats = [(width, width // 4), (width, hidden // 4), (hidden, width // 4)]
    if fine:
        message = (scenes, 10 * (width // (scenes * LATS)) + 16, width // 2)
        grads = [shape(message)] * 2
        spec, held = ANY, [pltpu.VMEM(message, BF)] * 2
    else:
        grads = [shape(d) for d in mats for _ in range(2)]
        grads += [shape((8, width), F32), shape((8, hidden), F32)]
        spec, held = pl.BlockSpec(memory_space=pltpu.VMEM), []
    return pl.pallas_call(
        partial(feed_kernel, fine),
        out_shape=[
            shape((count, width)),
            shape((half, width)),
            shape((half, width)),
            shape((half, 2 * LANES)),
            shape((half, 2 * LANES)),
        ]
        + grads,
        in_specs=[SMEM] + [ANY] * 7 + vmem(2),
        out_specs=[ANY] * 5 + [spec] * len(grads),
        scratch_shapes=held
        + [
            pltpu.VMEM(weights.shape, BF),
            pltpu.VMEM((half, width), BF),
            pltpu.VMEM((LATS, half // 2, 2 * OWN), BF),
            pltpu.VMEM((half, width), BF),
            pltpu.VMEM((width, width), BF),
            pltpu.VMEM((width, hidden), BF),
            pltpu.VMEM((hidden, width), BF),
            pltpu.VMEM((half, width), BF),
            pltpu.VMEM((half, width), BF),
            pltpu.VMEM((half, 2 * LANES), BF),
            pltpu.VMEM((half, 2 * LANES), BF),
            pltpu.VMEM((half, hidden + width), BF),
            pltpu.VMEM((half, hidden), BF),
            pltpu.VMEM((half, width), BF),
            pltpu.SemaphoreType.DMA((7,)),
            pltpu.SemaphoreType.DMA((8,)),
        ],
        compiler_params=params(),
        cost_estimate=cost(26),
        name="feed",
    )(where, rays, *ctxs, upstream, weights, rows_in, up_shift)


def halve_kernel(bit, where, own, got, send, keep):
    count = send.shape[0]
    mine = where[4] if count == 4 else where[6]
    low = (1 << bit) - 1
    for n in range(count):
        first = ((n & ~low) << 1) | (n & low)
        for target, side in ((send, 1 - mine), (keep, mine)):
            at = first + (side << bit)
            target[n] = (own[at].astype(F32) + got[at].astype(F32)).astype(BF)


def halve(where, bit, own, got):
    count, rows, cols = own.shape
    half = shape((count // 2, rows, cols))
    return pl.pallas_call(
        partial(halve_kernel, bit),
        out_shape=[half, half],
        in_specs=[SMEM] + vmem(2),
        out_specs=vmem(2),
        compiler_params=params(),
        cost_estimate=cost(3),
        name="halve",
    )(where, own, got)


def spread_kernel(count, where, *refs):
    pairs, feed_keep, feed_got, out = refs[: 2 * count], refs[-8], refs[-7], refs[-6:]
    for k in range(4):
        at = where[5] ^ k
        parts = [
            pairs[2 * n][at].astype(F32) + pairs[2 * n + 1][at].astype(F32) for n in range(count)
        ]
        out[k][...] = jnp.concatenate(parts, axis=0).astype(BF)
    mine = where[5] % 2
    for target, at in ((out[4], 1 - mine), (out[5], mine)):
        target[...] = (feed_keep[at].astype(F32) + feed_got[at].astype(F32)).astype(BF)


def add_spread(where, pairs, feed_keep, feed_got):
    rows = sum(keep.shape[1] for keep, _ in pairs)
    last = shape(feed_keep.shape[1:])
    return pl.pallas_call(
        partial(spread_kernel, len(pairs)),
        out_shape=[shape((rows, pairs[0][0].shape[2]))] * 4 + [last] * 2,
        in_specs=[SMEM] + vmem(2 * len(pairs) + 2),
        out_specs=vmem(6),
        compiler_params=params(),
        cost_estimate=cost(2),
        name="add_spread",
    )(where, *[a for pair in pairs for a in pair], feed_keep, feed_got)


def regroup_kernel(shard, where, *refs):
    trio, out, held = refs[:4], refs[6:10], refs[10]
    side = where[2]
    block = LATS * shard
    total = sum(r[...].astype(F32) for r in trio)
    pair, third = total[: 3 * block + 16], unfold(total[3 * block + 16 :])
    held[...] = jnp.concatenate([pair, third[: 3 * block + 16]], axis=1)
    feed_sum = refs[4][...].astype(F32) + refs[5][...].astype(F32)
    places = [[], []]
    for q in range(2):
        for first, rows in ((0, shard), (2 * shard, shard), (4 * shard, shard), (6 * shard, 2 * shard)):
            places[q].append(feed_sum[first + q * rows : first + (q + 1) * rows])
        line = feed_sum[10 * shard + q : 10 * shard + q + 1]
        places[q].append(jnp.broadcast_to(line, (8, line.shape[1])))
    places = [jnp.concatenate(p, axis=0) for p in places]
    for k in range(LATS):
        rows = []
        for n in range(3):
            at = n * block + (where[0] ^ k) * shard
            rows.append(held[pl.ds(pl.multiple_of(at, 8), shard), :])
        rows.append(held[3 * block : 3 * block + 8, :])
        rows.append(jnp.zeros((16, OWN), F32))
        value = fold(jnp.concatenate(rows, axis=0))
        if k % 2 == 0:
            mine = jnp.where(side == (k // 2), places[0], places[1])
            value = jnp.concatenate([value, mine], axis=0)
        out[k][...] = value.astype(BF)


def regroup(where, trio, feed_keep, feed_got, shard):
    small = (3 * shard + 24) // 2
    large = small + 5 * shard + 8
    return pl.pallas_call(
        partial(regroup_kernel, shard),
        out_shape=[shape((rows, 2 * OWN)) for rows in (large, small, large, small)],
        in_specs=[SMEM] + vmem(6),
        out_specs=vmem(LATS),
        scratch_shapes=[pltpu.VMEM((3 * LATS * shard + 16, OWN), F32)],
        compiler_params=params(),
        cost_estimate=cost(2),
        name="regroup",
    )(where, *trio, feed_keep, feed_got)


def settle_kernel(shard, where, got0, got1, got2, got3, w_query, gain, bias, *out):
    lat, side = where[0], where[2]
    mats, firsts, rest = out[-13:-7], out[-7:-5], out[-5:]
    got = [g[...].astype(F32) for g in (got0, got1, got2, got3)]
    small = got[1].shape[0]
    here, there = got[0][small:], got[2][small:]
    left, right = jnp.where(side == 0, here, there), jnp.where(side == 0, there, here)
    both = lambda a, b: jnp.concatenate([left[a:b], right[a:b]], axis=1)
    got = [unfold(g[:small]) for g in got]
    whole = jnp.concatenate([choose(lat ^ p, got) for p in range(LATS)], axis=1)
    part = lambda n: whole[n * shard : (n + 1) * shard]
    sums = whole[3 * shard : 3 * shard + 1] + whole[3 * shard + 1 : 3 * shard + 2]
    weight = w_query[...].astype(F32)
    mats[0][...] = part(0) * gain[...] + bias[...] * sums
    mats[1][...] = part(1)
    mats[2][...] = part(2)
    mats[3][...] = both(0, shard)
    cols = [half[n * shard : (n + 1) * shard] for half in (left, right) for n in (1, 2)]
    mats[4][...] = jnp.concatenate(cols, axis=1)
    mats[5][...] = both(3 * shard, 5 * shard)
    firsts[0][...] = jnp.sum((part(0) * weight).T, axis=0)
    firsts[1][...] = jnp.sum((weight * sums).T, axis=0)
    line = here[5 * shard : 5 * shard + 1]
    for target, (first, count) in zip(rest, ((2, 1), (3, 1), (4, 1), (6, 2), (5, 1))):
        target[...] = line[:, first * shard : (first + count) * shard].reshape(count * shard)


def settle(where, got, w_query, gain, bias, after):
    shard, width = w_query.shape
    flat = shape((shard, width), F32)
    tall = shape((2 * shard, width), F32)
    wide = shape((shard, 2 * width), F32)
    return pl.pallas_call(
        partial(settle_kernel, shard),
        out_shape=[flat] * 4
        + [wide, tall]
        + [shape((n * shard,), F32) for n in (1, 1, 1, 1, 1, 2, 1)],
        in_specs=[SMEM] + vmem(7) + [ANY] * len(after),
        out_specs=vmem(13),
        compiler_params=params(),
        cost_estimate=cost(2),
        name="settle",
    )(where, *got, w_query, gain, bias, *after)


def first_grads_kernel(where, rays, rows_in, d_middle, *refs):
    turned, pieces, (ray_grad, ray_half, d_query, turned_query) = refs[0], refs[1:25], refs[-4:]
    block = rays.shape[0]
    step = pl.program_id(0)

    @pl.when(step == 0)
    def _():
        half = d_query.shape[0]
        for h in range(OWN_HEADS):
            for j in range(LATS):
                entry = 2 * (h * LATS + j)
                part = jnp.concatenate([pieces[entry][...], pieces[entry + 1][...]], axis=1)
                first = (where[0] ^ j) * OWN + h * HEAD_DIM
                at = pl.ds(pl.multiple_of(first, HEAD_DIM), HEAD_DIM)
                turned_query[at, :] = part[:, :half]
        d_query[...] = turned_query[...].T

    at = pl.ds(pl.multiple_of(step * block, 16), block)
    d_lifted = dot(d_query[at, :], turned[...].reshape(rays.shape[1], rays.shape[1]))
    normed, factor = norm_parts(rays[...].astype(F32))
    back = norm_back(d_lifted, normed, factor, rows_in[0:1, :])
    low = (d_middle[...].astype(F32) + back).astype(BF)
    ray_grad[...] = low
    ray_half[...] = low


def first_grads(where, rays, turned, rows_in, d_middle, msgs, lat_rows, after):
    count, width = rays.shape
    half = count // 2
    steps = 2
    block = half // steps
    whole = lambda a: pl.BlockSpec(a.shape, lambda i, w: (0,) * a.ndim)
    pieces, specs = [], []
    for m in (m for group in msgs for m in group):
        tail = (m.shape[1] - 2 * lat_rows) // 2
        for n in range(2):
            pieces.append(m)
            at = 2 * lat_rows // tail + n
            specs.append(pl.BlockSpec((HEAD_DIM, tail), partial(lambda at, i, w: (0, at), at)))
    return pl.pallas_call(
        first_grads_kernel,
        grid_spec=pltpu.PrefetchScalarGridSpec(
            num_scalar_prefetch=1,
            grid=(steps,),
            in_specs=[
                pl.BlockSpec((block, width), lambda i, w: (w[1] * steps + i, 0)),
                whole(rows_in),
                pl.BlockSpec((block, width), lambda i, w: (i, 0)),
            ]
            + [pl.BlockSpec((LATS, 1, OWN, width), lambda i, w: (0, 0, 0, 0))]
            + specs
            + [ANY] * len(after),
            out_specs=[
                pl.BlockSpec((block, width), lambda i, w: (w[1] * steps + i, 0)),
                pl.BlockSpec((block, width), lambda i, w: (i, 0)),
            ],
            scratch_shapes=[pltpu.VMEM((half, width), BF), pltpu.VMEM((width, half), BF)],
        ),
        out_shape=[shape((count, width)), shape((half, width))],
        compiler_params=params(),
        cost_estimate=cost(6),
        name="first_grads",
    )(where, rays, rows_in, d_middle, turned, *pieces, *after)


def latent_kernel(where, turned, *refs):
    msgs, out, held = refs[:12], refs[-2], refs[-1]
    lat_rows = held.shape[2]
    width = out.shape[1]
    total = None
    for i in range(2):
        for h in range(OWN_HEADS):
            for j in range(LATS):
                first = (where[0] ^ j) * OWN + h * HEAD_DIM
                at = pl.ds(pl.multiple_of(first, HEAD_DIM), HEAD_DIM)
                held[i, at, :] = msgs[h * LATS + j][:, i * lat_rows : (i + 1) * lat_rows]
        part = dot_lt(held[i], turned[:, 1 + i].reshape(width, width))
        total = part if total is None else total + part
    out[...] = total[: out.shape[0]].astype(BF)


def latent_grads(where, turned, msgs, rows, lat_rows, after):
    width = turned.shape[3]
    pair = pl.BlockSpec((HEAD_DIM, 2 * lat_rows), lambda i, w: (0, 0))
    return pl.pallas_call(
        latent_kernel,
        grid_spec=pltpu.PrefetchScalarGridSpec(
            num_scalar_prefetch=1,
            grid=(1,),
            in_specs=[pl.BlockSpec(turned.shape, lambda i, w: (0, 0, 0, 0))]
            + [pair] * 12
            + [ANY] * len(after),
            out_specs=pl.BlockSpec((rows, width), lambda i, w: (0, 0)),
            scratch_shapes=[pltpu.VMEM((2, width, lat_rows), BF)],
        ),
        out_shape=shape((rows, width)),
        compiler_params=params(),
        cost_estimate=cost(6),
        name="latent_grads",
    )(where, turned, *msgs, *after)


def join(where, full, there):
    first = (1 - where[1]) * there.shape[0]
    return lax.dynamic_update_slice(full, there, (first, jnp.int32(0)))


def body(
    rays,
    latents,
    view_count,
    view_mask,
    cotangent,
    w_query,
    w_key,
    w_value,
    w_out,
    w_up,
    w_down,
    first_gain,
    first_bias,
    second_gain,
    second_bias,
    out_bias,
    up_bias,
    down_bias,
):
    scenes = lax.axis_size("scene")
    lat, scene = lax.axis_index("lat"), lax.axis_index("scene")
    core, side = lat % 2, lat // 2
    where = jnp.stack([lat, core, side, scene, scene % 2, scene // 2, scene // 4])
    where = where.astype(jnp.int32)
    count, width = rays.shape
    hidden = w_up.shape[1]
    lat_rows = latents.shape[0]
    lat_pad = -(-lat_rows // LANES) * LANES
    shard = w_query.shape[0]
    fine = shard % 8 == 0 and scenes == 8

    vectors = [first_gain, first_bias, second_gain, second_bias, out_bias, down_bias, up_bias]
    (trio, turned, rows_in, up_shift), own_lat, passed = attention_weights(
        where, w_query, w_key, w_value, vectors, latents, lat_pad
    )

    near_lat, far_lat = swap(own_lat, "lat", 1), swap(own_lat, "lat", 2)

    weights_in = feed_weights(w_out, w_up, w_down, passed)

    spot = jnp.arange(lat_pad, dtype=jnp.int32)
    block_of = lat ^ jnp.arange(LATS, dtype=jnp.int32)
    view_of = (block_of[:, None] * lat_rows + spot[None, :]) // VIEW_TOK
    matches = view_of[..., None] == jnp.arange(VIEWS, dtype=jnp.int32)
    listed = jnp.sum(jnp.where(matches, view_mask[0], 0), axis=-1) > 0
    live = listed & (view_of < view_count[0]) & (spot < lat_rows)[None, :]
    shut = jnp.where(live, 0.0, DEAD).astype(F32).reshape(LATS, 1, lat_pad)

    normed_low, query = make_queries(where, rays, trio, rows_in)
    far_lat = gate(far_lat, [query])
    lats = [own_lat, near_lat, far_lat, swap(far_lat, "lat", 1)]
    keyset = make_keyset(0, lats[:2], trio, shut)
    key, key_t, val, val_t = make_keyset(1, lats[2:], trio, shut, keyset)

    there_ctx, there_wide, weights, inverse = attend(1, query, key_t, val)
    near, far = swap(there_ctx, "lat", 1), swap(there_ctx, "lat", 3)
    here_ctx, here_wide, weights, inverse = attend(0, query, key_t, val, (weights, inverse))
    here_ctx = gate(here_ctx, [near, far])
    ctxs = [here_ctx, near, swap(here_ctx, "lat", 2), far]

    turned = lax.all_gather(gate(turned, ctxs[2:]), "lat", axis=0, tiled=False)
    layer_out, out_half, d_middle, d_own, d_sibling, *feed_out = feed(
        where, rays, ctxs, cotangent, weights_in, rows_in, up_shift, scenes, fine
    )
    d_there = swap(d_sibling, "lat", 1)
    out_there = swap(out_half, "lat", 1)
    layer_out = join(where, layer_out, out_there)

    if fine:
        own_msg, sib_msg = feed_out
        feed_send, feed_keep = halve(where, 0, own_msg, swap(sib_msg, "lat", 1))
        feed_got = swap(feed_send, "scene", 1)

    got, grads, after = [], [], []
    for h in range(OWN_HEADS):
        if h == 1:
            after = after + [out_there] + ([feed_send] if fine else [])
        elif h == 2:
            after = after + got[0][1:]
            if fine:
                feed_keep = gate(feed_keep, after)
                feed_send, feed_keep = halve(where, 1, feed_keep, feed_got)
                feed_got = swap(feed_send, "scene", 4)
                after = after + [feed_send]
        out = attend_back(
            h,
            fine,
            weights,
            inverse,
            (d_own, d_there),
            (here_wide, there_wide),
            query,
            key,
            val_t,
            lats,
            normed_low,
            grads[0] if grads else where,
            where,
            after,
        )
        if h == 2:
            out = gate(list(out), got[1][1:] + ([pair_got, feed_got] if fine else []))
        after = [out[0]]
        grads += out[LATS:]
        if h == 1 and fine:
            pair_got = swap(grads[1], "scene", 1)
        got.append([out[0]] + [swap(out[k], "lat", k) for k in range(1, LATS)])
    after = []
    if fine:
        pairs = [(grads[2], pair_got), (grads[4], swap(grads[3], "scene", 1))]
        *late, feed_send, feed_keep = add_spread(where, pairs, feed_keep, feed_got)
        after = [late[0]]
        feed_got = swap(feed_send, "scene", 2)
        late = [late[0]] + [swap(late[k], "scene", 2 * k) for k in range(1, 4)]
    ray_grad, ray_half = first_grads(where, rays, turned, rows_in, d_middle, got, lat_pad, after)
    if fine:
        ray_half = gate(ray_half, late[1:] + [feed_got])
    ray_grad = join(where, ray_grad, swap(ray_half, "lat", 1))
    if fine:
        final = regroup(where, late, feed_keep, feed_got, shard)
        after = [final[0]]
    latent_grad = latent_grads(
        where, turned, [m for g in got for m in g], lat_rows, lat_pad, after
    )
    first = [v.reshape(shard, 1).astype(F32) for v in (first_gain, first_bias)]
    if fine:
        final = [final[0]] + [swap(final[k], "lat", k) for k in range(1, LATS)]
        small = settle(where, final, w_query, *first, [latent_grad])
    else:
        joined = jnp.concatenate(grads, axis=1)
        grads = joined[: 3 * width].reshape(3, width, OWN), joined[3 * width :]
        small = plain_final(feed_out, grads, scenes, shard, w_query, *first)
    return (layer_out, ray_grad, latent_grad, *small)


def plain_final(feed_out, grads, scenes, shard, w_query, gain, bias):
    lat = lax.axis_index("lat")
    out_own, out_sib, up_own, up_sib, down_own, down_sib, sums, up_sums = feed_out
    trio, query_sums = grads

    def by_scene(out_part, up_part, down_part):
        parts = [
            out_part.reshape(scenes, -1, OWN),
            up_part.reshape(scenes, -1, 2, OWN).swapaxes(1, 2).reshape(scenes, -1, OWN),
            down_part.reshape(scenes, -1, OWN),
        ]
        return jnp.concatenate(parts, axis=1).astype(F32)

    feed_part = by_scene(out_own, up_own, down_own)
    feed_part = feed_part + swap(by_scene(out_sib, up_sib, down_sib), "lat", 1)
    feed_part = scatter_scene(feed_part)
    block = LATS * shard
    trio = trio.reshape(3, scenes, block, OWN).swapaxes(0, 1).reshape(scenes, 3 * block, OWN)
    lines = [v.reshape(scenes, LATS, shard) for v in sums[:4]]
    lines = [jnp.zeros_like(lines[0])] * 2 + lines + [up_sums[0].reshape(scenes, LATS, 2 * shard)]
    lines = jnp.concatenate(lines, axis=2)
    lines = jnp.pad(lines, ((0, 0), (0, 0), (0, OWN - 8 * shard)))
    cols = jnp.broadcast_to(query_sums[:2], (scenes, 2, OWN))
    late = scatter_scene(jnp.concatenate([trio.astype(F32), cols, lines], axis=1))
    mats = [late[i * block : (i + 1) * block].reshape(LATS, shard, OWN) for i in range(3)]
    mats += [feed_part[i * block : (i + 1) * block].reshape(LATS, shard, OWN) for i in range(3)]
    mats.append(feed_part[3 * block :].reshape(LATS, 2 * shard, OWN))
    mats.append(jnp.broadcast_to(late[3 * block : 3 * block + 2], (LATS, 2, OWN)))
    mats.append(late[3 * block + 2 :].reshape(LATS, 1, OWN))
    final = jnp.concatenate(mats, axis=1).astype(BF)
    sent = [lax.dynamic_index_in_dim(final, lat ^ k, 0, keepdims=False) for k in range(LATS)]
    got = [sent[0]] + [swap(sent[k], "lat", k) for k in range(1, LATS)]
    got = [g.astype(F32) for g in got]
    line = got[0][-1] + got[1][-1]
    cols = in_order(jnp.stack(got), list(range(LATS)), lat)
    joined = jnp.transpose(cols, (1, 0, 2)).reshape(cols.shape[1], -1)
    part = lambda n, count=1: joined[n * shard : (n + count) * shard]
    up = cols[:, 4 * shard : 6 * shard].reshape(LATS, 2, shard, OWN)
    up = jnp.transpose(up, (2, 0, 1, 3)).reshape(shard, -1)
    sums = joined[8 * shard : 8 * shard + 1] + joined[8 * shard + 1 : 8 * shard + 2]
    weight = w_query.astype(F32)
    piece = lambda i, n=1: line[i * shard : (i + n) * shard]
    return (
        part(0) * gain + bias * sums,
        part(1),
        part(2),
        part(3),
        up,
        part(6, 2),
        jnp.sum(part(0) * weight, axis=1),
        jnp.sum(weight * sums, axis=1),
        piece(2),
        piece(3),
        piece(4),
        piece(6, 2),
        piece(5),
    )


def solution(mesh):
    rows = P(("scene", "lat"), None)
    line = P(("scene", "lat"))
    scene = P("scene", None)
    in_specs = (scene, rows, P("scene"), scene, scene) + (rows,) * 6 + (line,) * 7
    out_specs = (scene, scene, rows) + (rows,) * 6 + (line,) * 7
    return jax.shard_map(body, mesh=mesh, in_specs=in_specs, out_specs=out_specs, check_vma=False)
```

```python
import math
from functools import partial

import jax
import jax.numpy as jnp
from jax import lax
from jax.experimental import pallas as pl
from jax.experimental.pallas import tpu as pltpu
from jax.sharding import PartitionSpec as P

HEADS = 12
HEAD_DIM = 64
VIEWS = 10
VIEW_TOK = 300
LANES = 128
LATS = 4
OWN_HEADS = HEADS // LATS
OWN = OWN_HEADS * HEAD_DIM
DEAD = -1e30
LOG2E = math.log2(math.e)
Q_SCALE = 0.125 * LOG2E
ROOT = math.sqrt(2.0 / math.pi)
SCALE = 1.0
VMEM_BYTES = 63 * 2**20
BF = jnp.bfloat16
F32 = jnp.float32


def dot(left, right):
    return jnp.dot(left, right, preferred_element_type=F32)


def dot_rt(left, right):
    return lax.dot_general(left, right, (((1,), (1,)), ((), ())), preferred_element_type=F32)


def dot_lt(left, right):
    return lax.dot_general(left, right, (((0,), (0,)), ((), ())), preferred_element_type=F32)


def params():
    return pltpu.CompilerParams(vmem_limit_bytes=VMEM_BYTES)


def cost(micros):
    return pl.CostEstimate(
        flops=int(micros * SCALE * 1e9), bytes_accessed=int(micros * SCALE * 3.3e6), transcendentals=0
    )


def vmem(count):
    return [pl.BlockSpec(memory_space=pltpu.VMEM)] * count


ANY = pl.BlockSpec(memory_space=pl.ANY)
SMEM = pl.BlockSpec(memory_space=pltpu.SMEM)


def shape(dims, dtype=BF):
    return jax.ShapeDtypeStruct(tuple(dims), dtype)


def norm_parts(values):
    center = values - jnp.mean(values, axis=-1, keepdims=True)
    spread = jnp.mean(center * center, axis=-1, keepdims=True)
    factor = lax.rsqrt(spread + 1e-05)
    return center * factor, factor


def norm_back(grad_out, normed, factor, gain_row):
    scaled = grad_out * gain_row
    return factor * (
        scaled
        - jnp.mean(scaled, axis=-1, keepdims=True)
        - normed * jnp.mean(scaled * normed, axis=-1, keepdims=True)
    )


def swap(values, axis, step):
    count = lax.axis_size(axis)
    return lax.ppermute(values, axis, [(i, i ^ step) for i in range(count)])


def stages(count):
    found, stride = [], count
    while stride > 1:
        group = 4 if stride % 4 == 0 else 2
        stride //= group
        found.append((stride, group))
    return found


def collect_kernel(count, *refs):
    out, rows = refs[-1], 0
    for ref in refs[:count]:
        out[rows : rows + ref.shape[0]] = ref[...]
        rows += ref.shape[0]


def collect(values, after):
    rows = sum(v.shape[0] for v in values)
    return pl.pallas_call(
        partial(collect_kernel, len(values)),
        out_shape=shape((rows,) + values[0].shape[1:]),
        in_specs=vmem(len(values)) + [ANY] * len(after),
        out_specs=pl.BlockSpec(memory_space=pltpu.VMEM),
        compiler_params=params(),
        cost_estimate=cost(0.3),
        name="collect",
    )(*values, *after)


def gather_scene(parts, after=()):
    steps = [0]
    got = [parts]
    passed = []
    for stride, group in stages(lax.axis_size("scene")):
        if len(got) == 1:
            parts = got[0]
        else:
            parts = collect(got, after) if after else jnp.concatenate(got)
        got = [parts] + [swap(parts, "scene", k * stride) for k in range(1, group)]
        steps = [step ^ (k * stride) for k in range(group) for step in steps]
        passed = [parts]
    return got, steps, passed


def in_order(stacked, steps, me):
    places = [steps.index(i) for i in range(len(steps))]
    order = jnp.take(jnp.array(places, jnp.int32), jnp.arange(len(steps)) ^ me)
    return jnp.take(stacked, order, axis=0)


def scatter_scene(blocks):
    count = lax.axis_size("scene")
    me = lax.axis_index("scene")
    held = blocks
    for stride, group in reversed(stages(count)):
        digit = (me // stride) % group
        view = held.reshape((-1, group) + blocks.shape[1:])
        total = lax.dynamic_index_in_dim(view, digit, 1, keepdims=False).astype(F32)
        for k in range(1, group):
            mine = lax.dynamic_index_in_dim(view, digit ^ k, 1, keepdims=False)
            total = total + swap(mine.astype(BF), "scene", k * stride).astype(F32)
        held = total.astype(BF)
    return total.reshape(blocks.shape[1:])


def fold(rows):
    half = rows.shape[0] // 2
    return jnp.concatenate([rows[:half], rows[half:]], axis=1)


def unfold(rows):
    half = rows.shape[1] // 2
    return jnp.concatenate([rows[:, :half], rows[:, half:]], axis=0)


def choose(index, options):
    picked = options[0]
    for i in range(1, len(options)):
        picked = jnp.where(index == i, options[i], picked)
    return picked


def pack_kernel(where, w_query, w_key, w_value, *refs):
    vectors, out = refs[:-LATS], refs[-LATS:]
    values = [w[...].astype(F32) for w in (w_query, w_key, w_value)]
    line = [v[...].astype(F32).reshape(1, v.shape[0]) for v in vectors]
    line = jnp.concatenate(line, axis=1)
    line = jnp.concatenate([line, jnp.zeros((1, OWN - line.shape[1]), F32)], axis=1) if (
        line.shape[1] < OWN
    ) else line
    tail = jnp.broadcast_to(line, (8, OWN))
    for k in range(LATS):
        target = where[0] ^ k
        rows = []
        for value in values:
            cols = [value[:, p * OWN : (p + 1) * OWN] for p in range(LATS)]
            rows.append(choose(target, cols))
        out[k][...] = fold(jnp.concatenate(rows + [tail], axis=0)).astype(BF)


def pack(where, w_query, w_key, w_value, vectors):
    rows = 3 * w_query.shape[0] + 8
    return pl.pallas_call(
        pack_kernel,
        out_shape=[shape((rows // 2, 2 * OWN))] * LATS,
        in_specs=[SMEM] + vmem(3 + len(vectors)),
        out_specs=vmem(LATS),
        compiler_params=params(),
        cost_estimate=cost(0.5),
        name="pack",
    )(where, w_query, w_key, w_value, *vectors)


def unpack_kernel(steps, where, *refs):
    *chunks, trio, turned, rows_out, up_out, held, lines = refs
    lat, scene = where[0], where[3]
    shard = held.shape[1] // (len(steps) * LATS)
    entry = 0
    for chunk in chunks:
        for p in range(chunk.shape[0]):
            values = unfold(chunk[p].astype(F32))
            source = (scene ^ steps[entry // LATS]) * LATS + (lat ^ (entry % LATS))
            at = pl.ds(pl.multiple_of(source * shard, 8), shard)
            for m in range(3):
                held[m, at, :] = values[m * shard : (m + 1) * shard]
            lines[pl.ds(source, 1), :] = values[3 * shard : 3 * shard + 1]
            entry += 1
    for m in range(3):
        low = held[m].astype(BF)
        trio[m] = low
        turned[m] = held[m].T.astype(BF)
    sources = lines.shape[0]
    low = lines[...].astype(BF)
    for target, size, first in ((rows_out, shard, 0), (up_out, 2 * shard, 6)):
        wide = target.shape[1]
        col = lax.broadcasted_iota(jnp.int32, (1, wide), 1).astype(F32)
        owner = jnp.floor((col + 0.5) * (1.0 / size))
        spot = col - owner * size
        row = lax.broadcasted_iota(jnp.int32, (OWN, 1), 0).astype(F32)
        line = lax.broadcasted_iota(jnp.int32, (sources, 1), 0).astype(F32)
        for v in range(6 if first == 0 else 1):
            hot = jnp.where(row == spot + (first + v) * shard, 1.0, 0.0).astype(BF)
            spread = jnp.where(line == owner, dot(low, hot), 0.0)
            target[v : v + 1, :] = jnp.sum(spread, axis=0, keepdims=True)


def unpack(where, chunks, steps, shard):
    sources = len(steps) * LATS
    width = sources * shard
    return pl.pallas_call(
        partial(unpack_kernel, steps),
        out_shape=[
            shape((3, width, OWN)),
            shape((3, OWN, width)),
            shape((8, width), F32),
            shape((1, 2 * width), F32),
        ],
        in_specs=[SMEM] + vmem(len(chunks)),
        out_specs=vmem(4),
        scratch_shapes=[pltpu.VMEM((3, width, OWN), F32), pltpu.VMEM((sources, OWN), F32)],
        compiler_params=params(),
        cost_estimate=cost(0.5),
        name="unpack",
    )(where, *chunks)


def attention_weights(where, w_query, w_key, w_value, vectors, latents, lat_pad, early):
    shard, width = w_query.shape
    if shard % 8 == 0:
        pieces = pack(where, w_query, w_key, w_value, vectors)
        pieces = [pieces[0]] + [swap(pieces[k], "lat", k) for k in range(1, LATS)]
        own_lat = pad_latents(latents, lat_pad, pieces[2:])
        stacked = collect([p[None] for p in pieces], ())
        chunks, steps, passed = gather_scene(stacked, [own_lat] + early)
        return unpack(where, chunks, steps, shard), own_lat, [stacked] + passed
    flat = jnp.concatenate(vectors)
    flat = jnp.pad(flat, (0, OWN - flat.shape[0])).reshape(1, OWN)
    lat, scene = lax.axis_index("lat"), lax.axis_index("scene")
    scenes = lax.axis_size("scene")
    trio = jnp.stack([w_query, w_key, w_value]).reshape(3, shard, LATS, OWN)
    trio = jnp.transpose(trio, (2, 0, 1, 3)).reshape(LATS, 3 * shard, OWN)
    message = jnp.concatenate([trio, jnp.broadcast_to(flat, (LATS, 1, OWN))], axis=1)
    pieces = [lax.dynamic_index_in_dim(message, lat ^ k, 0, keepdims=False) for k in range(LATS)]
    pieces = [pieces[0]] + [swap(pieces[k], "lat", k) for k in range(1, LATS)]
    pieces = in_order(jnp.stack(pieces), list(range(LATS)), lat)
    chunks, steps, passed = gather_scene(pieces[None])
    gathered = in_order(jnp.concatenate(chunks), steps, scene)
    trio = gathered[:, :, : 3 * shard].reshape(scenes, LATS, 3, shard, OWN)
    trio = jnp.transpose(trio, (2, 0, 1, 3, 4)).reshape(3, width, OWN)
    lines = gathered[:, :, 3 * shard, : 8 * shard].astype(F32).reshape(scenes * LATS, 8, shard)
    rows = jnp.transpose(lines, (1, 0, 2)).reshape(8, width)
    up = lines[:, 6:].reshape(1, 2 * width)
    own_lat = pad_latents(latents, lat_pad, [])
    return (trio, jnp.transpose(trio, (0, 2, 1)), rows, up), own_lat, []


def gate_kernel(*refs):
    pass


def gate(values, after):
    one = not isinstance(values, list)
    values = [values] if one else values
    out = pl.pallas_call(
        gate_kernel,
        out_shape=[shape(v.shape, v.dtype) for v in values],
        in_specs=[ANY] * (len(values) + len(after)),
        out_specs=[ANY] * len(values),
        input_output_aliases={i: i for i in range(len(values))},
        compiler_params=params(),
        cost_estimate=cost(0.2),
        name="gate",
    )(*values, *after)
    return out[0] if one else list(out)


def pad_kernel(latents, *refs):
    out = refs[-1]
    rows = latents.shape[0]
    out[:rows, :] = latents[...]
    out[rows:, :] = jnp.zeros((out.shape[0] - rows, out.shape[1]), out.dtype)


def pad_latents(latents, rows, after):
    return pl.pallas_call(
        pad_kernel,
        out_shape=shape((rows, latents.shape[1])),
        in_specs=vmem(1) + [ANY] * len(after),
        out_specs=pl.BlockSpec(memory_space=pltpu.VMEM),
        compiler_params=params(),
        cost_estimate=cost(0.5),
        name="pad_latents",
    )(latents, *after)


def pack_feed_kernel(w_out, w_up, w_down, *refs):
    out = refs[-1]
    shard, width = w_out.shape
    out[: 2 * shard, :] = w_down[...]
    out[2 * shard : 3 * shard, :] = w_out[...]
    out[3 * shard : 4 * shard, :] = w_up[:, :width]
    out[4 * shard :, :] = w_up[:, width:]


def pack_feed(w_out, w_up, w_down, after):
    shard, width = w_out.shape
    return pl.pallas_call(
        pack_feed_kernel,
        out_shape=shape((5 * shard, width)),
        in_specs=vmem(3) + [ANY] * len(after),
        out_specs=pl.BlockSpec(memory_space=pltpu.VMEM),
        compiler_params=params(),
        cost_estimate=cost(0.3),
        name="pack_feed",
    )(w_out, w_up, w_down, *after)


def feed_weights(w_out, w_up, w_down, after):
    if w_out.shape[0] % 8 == 0:
        packed = gate(pack_feed(w_out, w_up, w_down, after[:1]), after[1:])
        return lax.all_gather(packed, ("scene", "lat"), axis=0, tiled=False)
    width = w_out.shape[1]
    packed = jnp.concatenate([w_down, w_out, w_up[:, :width], w_up[:, width:]], axis=0)
    held = lax.all_gather(packed, ("scene", "lat"), axis=0, tiled=False)
    shard = w_out.shape[0]
    parts = [held[:, : 2 * shard].reshape(2 * width, width)]
    parts += [held[:, n * shard : (n + 1) * shard].reshape(width, width) for n in range(2, 5)]
    return jnp.concatenate(parts, axis=0)


def widen(weight):
    gap = jnp.zeros((weight.shape[0], 2 * LANES - OWN), weight.dtype)
    return jnp.concatenate([weight, gap], axis=1)


def own_lanes(head, axis):
    spot = lax.broadcasted_iota(jnp.int32, (1, LANES) if axis == 1 else (LANES, 1), axis)
    first = (head % 2) * HEAD_DIM
    return (spot >= first) & (spot < first + HEAD_DIM), spot, HEAD_DIM - first


def lane_block(values, head):
    return values[:, (head // 2) * LANES : (head // 2 + 1) * LANES]


def norms_kernel(where, rays, normed_low, centers, factors):
    values = rays[...].astype(F32)
    middle = jnp.mean(values, axis=-1, keepdims=True)
    center = values - middle
    factor = lax.rsqrt(jnp.mean(center * center, axis=-1, keepdims=True) + 1e-05)
    normed_low[...] = (center * factor).astype(BF)
    centers[...] = jnp.broadcast_to(middle, centers.shape)
    factors[...] = jnp.broadcast_to(factor, factors.shape)


def make_norms(where, rays):
    count, width = rays.shape
    block = count // 4
    rows = lambda cols: pl.BlockSpec((block, cols), lambda i, w: (i, 0))
    return pl.pallas_call(
        norms_kernel,
        grid_spec=pltpu.PrefetchScalarGridSpec(
            num_scalar_prefetch=1,
            grid=(4,),
            in_specs=[pl.BlockSpec((block, width), lambda i, w: (i ^ (2 * w[1]), 0))],
            out_specs=[rows(width), rows(LANES), rows(LANES)],
        ),
        out_shape=[shape((count, width)), shape((count, LANES), F32), shape((count, LANES), F32)],
        compiler_params=params(),
        cost_estimate=cost(1),
        name="norms",
    )(where, rays)


def query_kernel(where, rays, centers, factors, weight, rows_in, query, wide):
    @pl.when(pl.program_id(0) == 0)
    def _():
        wide[...] = widen(weight[0])

    copies = rays.shape[1] // LANES
    middle = jnp.concatenate([centers[...]] * copies, axis=1)
    factor = jnp.concatenate([factors[...]] * copies, axis=1)
    normed = (rays[...].astype(F32) - middle) * factor
    low = (normed * rows_in[0:1, :] + rows_in[1:2, :]).astype(BF)
    values = dot(low, wide[...]) * Q_SCALE
    for h in range(OWN_HEADS):
        own, lane, spare = own_lanes(h, 1)
        one = jnp.where(lane == spare, 1.0, 0.0)
        query[h] = jnp.where(own, lane_block(values, h), one).astype(BF)


def make_queries(where, rays, centers, factors, trio, rows_in):
    count, width = rays.shape
    block = count // 4
    whole = lambda a: pl.BlockSpec(a.shape, lambda i, w: (0,) * a.ndim)
    return pl.pallas_call(
        query_kernel,
        grid_spec=pltpu.PrefetchScalarGridSpec(
            num_scalar_prefetch=1,
            grid=(4,),
            in_specs=[
                pl.BlockSpec((block, width), lambda i, w: (i ^ (2 * w[1]), 0)),
                pl.BlockSpec((block, LANES), lambda i, w: (i, 0)),
                pl.BlockSpec((block, LANES), lambda i, w: (i, 0)),
                pl.BlockSpec((1,) + trio.shape[1:], lambda i, w: (0, 0, 0)),
                whole(rows_in),
            ],
            out_specs=pl.BlockSpec((OWN_HEADS, block, LANES), lambda i, w: (0, i, 0)),
            scratch_shapes=[pltpu.VMEM((width, 2 * LANES), BF)],
        ),
        out_shape=shape((OWN_HEADS, count, LANES)),
        compiler_params=params(),
        cost_estimate=cost(2),
        name="queries",
    )(where, rays, centers, factors, trio, rows_in)


def keyset_kernel(count, *refs):
    lats, trio, shut = refs[:count], refs[count], refs[count + 1]
    key, key_t, val, val_t, wide, here = refs[-6:]
    step = pl.program_id(0)

    @pl.when(step == 0)
    def _():
        wide[0] = widen(trio[1])
        wide[1] = widen(trio[2])

    for j, lat in enumerate(lats):

        @pl.when(step == j)
        def _():
            here[...] = lat[...]

    keys = dot(here[...], wide[0])
    vals = dot(here[...], wide[1])
    blocks = lambda v: [v[:, i * LANES : (i + 1) * LANES].T for i in range(2)]
    keys_t, vals_t = blocks(keys), blocks(vals)
    for h in range(OWN_HEADS):
        own, _, _ = own_lanes(h, 1)
        own_line, line, spare = own_lanes(h, 0)
        key[h] = jnp.where(own, lane_block(keys, h), 0.0).astype(BF)
        val[h] = jnp.where(own, lane_block(vals, h), 1.0).astype(BF)
        mask = jnp.where(line == spare, shut[0], 0.0)
        key_t[h] = jnp.where(own_line, keys_t[h // 2], mask).astype(BF)
        val_t[h] = jnp.where(own_line, vals_t[h // 2], 1.0).astype(BF)


def make_keyset(start, lats, trio, shut, held=None):
    count = len(lats)
    rows, width = lats[0].shape
    total = LATS * rows
    tall, long = shape((OWN_HEADS, total, LANES)), shape((OWN_HEADS, LANES, total))
    whole = lambda a: pl.BlockSpec(a.shape, lambda i: (0,) * a.ndim)
    down = pl.BlockSpec((OWN_HEADS, rows, LANES), lambda i: (0, start + i, 0))
    over = pl.BlockSpec((OWN_HEADS, LANES, rows), lambda i: (0, 0, start + i))
    extra = [] if held is None else list(held)
    return pl.pallas_call(
        partial(keyset_kernel, count),
        grid=(count,),
        out_shape=[tall, long, tall, long],
        in_specs=[whole(lat) for lat in lats]
        + [whole(trio), pl.BlockSpec((1, 1, rows), lambda i: (start + i, 0, 0))]
        + [ANY] * len(extra),
        out_specs=[down, over, down, over],
        scratch_shapes=[pltpu.VMEM((2, width, 2 * LANES), BF), pltpu.VMEM((rows, width), BF)],
        input_output_aliases={count + 2 + i: i for i in range(len(extra))},
        compiler_params=params(),
        cost_estimate=cost(5),
        name="keyset",
    )(*lats, trio, shut, *extra)


def attend_kernel(sub, query, key_t, val, *rest):
    context, native, weights, inverse, mixed = rest[-5:]
    head, part = pl.program_id(0), pl.program_id(1)
    rows = query.shape[1]
    own, _, _ = own_lanes(head, 1)
    spot = part * 2 + head // 2

    def score(i):
        return dot(query[0, i * sub : (i + 1) * sub, :], key_t[0])

    scores = score(0)
    for i in range(rows // sub):
        later = score(i + 1) if i + 1 < rows // sub else None
        at = slice(i * sub, (i + 1) * sub)
        low = jnp.exp2(scores - jnp.max(scores, axis=1, keepdims=True)).astype(BF)
        weights[0, at, :] = low
        summed = dot(low, val[0])
        scale = 1.0 / jnp.where(own, pltpu.roll(summed, HEAD_DIM, 1), summed)
        held = jnp.where(head == 1, mixed[spot, at, :], 0.0)
        mixed[spot, at, :] = jnp.where(own, summed * scale, held)
        inverse[0, at, :] = scale
        scores = later

    for p in range(2):

        @pl.when((head == OWN_HEADS - 1) & (part == p))
        def _():
            both = jnp.concatenate([mixed[2 * p], mixed[2 * p + 1]], axis=1).astype(BF)
            native[p * rows : (p + 1) * rows, :] = both
            context[:, p * OWN : (p + 1) * OWN] = both[:, :OWN]


def attend(half_index, query, key_t, val, held=None, after=()):
    _, count, _ = query.shape
    total = key_t.shape[2]
    half = count // 2
    block = half // 2
    sub = block // 3 if block % 48 == 0 else block
    rows = lambda cols: pl.BlockSpec((1, block, cols), lambda h, b: (h, 2 * half_index + b, 0))
    every = lambda rows, cols: pl.BlockSpec((1, rows, cols), lambda h, b: (h, 0, 0))
    extra = ([] if held is None else list(held)) + list(after)
    return pl.pallas_call(
        partial(attend_kernel, sub),
        grid=(OWN_HEADS, 2),
        in_specs=[rows(LANES), every(LANES, total), every(total, LANES)] + [ANY] * len(extra),
        out_specs=[
            pl.BlockSpec((block, 2 * OWN), lambda h, b: (0, 0)),
            pl.BlockSpec((half, 2 * LANES), lambda h, b: (0, 0)),
            rows(total),
            rows(LANES),
        ],
        out_shape=[
            shape((block, 2 * OWN)),
            shape((half, 2 * LANES)),
            shape((OWN_HEADS, count, total)),
            shape((OWN_HEADS, count, LANES), F32),
        ],
        scratch_shapes=[pltpu.VMEM((4, block, LANES), F32)],
        input_output_aliases={} if held is None else {3: 2, 4: 3},
        compiler_params=params(),
        cost_estimate=cost(16),
        name="attend",
    )(query, key_t, val, *extra)


def back_kernel(sub, lat_rows, head, fine, weights, inverse, *refs):
    d_here, d_there, ctx_here, ctx_there, query, key, val_t = refs[:7]
    refs = refs[7:]
    project = not fine or head > 0
    lats, normed_low, earlier, where = refs[:LATS], refs[LATS], refs[5:9], refs[9]
    count = LATS + (0 if not project else 2 if fine else 1)
    out, scratch = refs[-(count + (5 if project else 2)) :][:count], refs[-5 if project else -2 :]
    sums, d_query = scratch[:2]
    grads_out = out[LATS:]
    pair_out = query_out = out[:LATS]
    query_at = 2 * lat_rows
    step = pl.program_id(0)
    rows = weights.shape[1]
    half = 2 * rows
    start = pl.multiple_of((step % 2) * rows, rows)
    loads = []
    if project:
        lat_here, normed_here, sem = scratch[2:]
        for j, lat in enumerate(lats):
            at = pl.ds(j * lat_rows, lat_rows)
            loads.append(pltpu.make_async_copy(lat, lat_here.at[at], sem.at[j]))
        loads.append(pltpu.make_async_copy(normed_low, normed_here, sem.at[LATS]))

    @pl.when(step == 0)
    def _():
        for load in loads:
            load.start()

    own, lane, spare = own_lanes(head, 1)
    far = step >= 2
    upstream = jnp.where(far, d_there[...], d_here[...]).astype(F32)
    ctx = jnp.where(far, ctx_there[...], ctx_here[...]).astype(F32)
    scale = inverse[0]
    delta = jnp.sum(jnp.where(own, upstream * ctx, 0.0), axis=1, keepdims=True) * scale
    high = delta.astype(BF).astype(F32)
    rest = jnp.where(lane == spare + 1, high - delta, 0.0)
    rest = jnp.where(lane == spare, -high, rest)
    grad = jnp.where(own, upstream * scale, rest).astype(BF)
    val_part = dot_lt(grad, weights[0])
    found = []
    for i in range(rows // sub):
        at = slice(i * sub, (i + 1) * sub)
        d_weights = dot(grad[at], val_t[0])
        d_scores = (weights[0, at, :].astype(F32) * d_weights).astype(BF)
        d_query[pl.ds(start + i * sub, sub), :] = dot(d_scores, key[0]) * 0.125
        found.append(d_scores)
    d_scores = jnp.concatenate(found, axis=0) if len(found) > 1 else found[0]
    key_part = dot_lt(query[0], d_scores) * (1.0 / LOG2E)

    @pl.when(step == 0)
    def _():
        sums[0] = key_part
        sums[1] = val_part

    @pl.when(step > 0)
    def _():
        sums[0] += key_part
        sums[1] += val_part

    first = (head % 2) * HEAD_DIM

    @pl.when(step == 3)
    def _():
        for i in range(2):
            total = sums[i, first : first + HEAD_DIM].astype(BF)
            for j in range(LATS):
                pair_out[j][:, i * lat_rows : (i + 1) * lat_rows] = total[
                    :, j * lat_rows : (j + 1) * lat_rows
                ]

    for last in (1, 3):

        @pl.when(step == last)
        def _():
            turned = d_query[...].T[first : first + HEAD_DIM].astype(BF)
            for j in (last // 2, last // 2 + 2):
                query_out[j][:, query_at : query_at + half] = turned

    if not project:
        return

    @pl.when(step == 3)
    def _():
        for load in loads:
            load.wait()
        groups = [list(earlier), list(out[:LATS])] if head == 1 and fine else [list(out[:LATS])]
        at = slice(2 * lat_rows, 2 * lat_rows + half)
        turned = [jnp.concatenate([g[b][:, at] for g in groups], axis=0) for b in range(2)]
        part = dot(turned[0], normed_here[:half]) + dot(turned[1], normed_here[half:])
        both = []
        for i in range(2):
            at = slice(i * lat_rows, (i + 1) * lat_rows)
            for g in groups:
                both.append(jnp.concatenate([g[j][:, at] for j in range(LATS)], axis=1))
        both = dot(jnp.concatenate(both, axis=0), lat_here[...])
        rows = both.shape[0] // 2
        col = sum(jnp.sum(t.astype(F32), axis=1, keepdims=True) for t in turned)
        high = col.astype(BF).astype(F32)
        col = jnp.where(lane == 0, high, jnp.where(lane == 1, col - high, 0.0)).T[:16]
        parts = [p.T for p in (part, both[:rows], both[rows:])] + [col]
        if not fine:
            grads_out[0][...] = jnp.concatenate(parts, axis=0)
            return
        send, keep = grads_out
        scenes = 2 * send.shape[0]
        width = normed_here.shape[1]
        block = width // scenes
        for s in range(scenes):
            mine = [p[s * block : (s + 1) * block] for p in parts[:3]] + parts[3:]
            if head == 2:
                mine = fold(jnp.concatenate(mine + [jnp.zeros((16, HEAD_DIM), F32)], axis=0))
            else:
                mine = jnp.concatenate(mine, axis=0)
            mine = mine.astype(BF)
            kept = where[4] == s % 2

            @pl.when(kept)
            def _():
                keep[s // 2] = mine

            @pl.when(jnp.logical_not(kept))
            def _():
                send[s // 2] = mine


def attend_back(head, fine, weights, inverse, d_ctxs, ctxs, query, key, val_t, lats, normed_low, earlier, where, after):
    _, count, total = weights.shape
    rows = count // 4
    sub = rows // 2 if rows % 32 == 0 else rows
    lat_rows = total // LATS
    width = normed_low.shape[1]
    pad = lambda n: -(-n // LANES) * LANES
    outs = [shape((HEAD_DIM, pad(2 * lat_rows + 2 * rows)))] * LATS
    project = not fine or head > 0
    if not fine:
        outs.append(shape((3 * width + 16, HEAD_DIM), F32))
    elif project:
        block = 3 * (width // 8)
        dims = (4, block + 16, LANES) if head == 1 else (4, block // 2 + 16, LANES)
        outs += [shape(dims)] * 2
    of_head = lambda cols: pl.BlockSpec((1, rows, cols), lambda b: (head, b, 0))
    here = pl.BlockSpec((rows, LANES), lambda b: (jnp.minimum(b, 1), head // 2))
    there = pl.BlockSpec((rows, LANES), lambda b: (jnp.maximum(b, 2) - 2, head // 2))
    whole = lambda a: pl.BlockSpec(a.shape, lambda b: (0,) * len(a.shape))
    earlier = list(earlier) if head == 1 and fine else [where] * LATS
    early = [whole(a) for a in earlier] if head == 1 and fine else [ANY] * LATS
    return pl.pallas_call(
        partial(back_kernel, sub, lat_rows, head, fine),
        grid=(4,),
        in_specs=[
            of_head(total),
            of_head(LANES),
            here,
            there,
            here,
            there,
            of_head(LANES),
            pl.BlockSpec((1, total, LANES), lambda b: (head, 0, 0)),
            pl.BlockSpec((1, LANES, total), lambda b: (head, 0, 0)),
        ]
        + [ANY] * (LATS + 1)
        + early
        + [SMEM]
        + [ANY] * len(after),
        out_specs=[whole(o) for o in outs],
        out_shape=outs,
        scratch_shapes=[
            pltpu.VMEM((2, LANES, total), F32),
            pltpu.VMEM((2 * rows, LANES), F32),
        ]
        + [
            pltpu.VMEM((total, width), BF),
            pltpu.VMEM((count, width), BF),
            pltpu.SemaphoreType.DMA((LATS + 1,)),
        ]
        * project,
        compiler_params=params(),
        cost_estimate=cost(14),
        name=f"attend_back_{head}",
    )(weights, inverse, *d_ctxs, *ctxs, query, key, val_t, *lats, normed_low, *earlier, where, *after)


def quarter_halves(values, core):
    mid = values.shape[1] // 2
    low, high = values[:, :mid], values[:, mid:]
    return jnp.where(core == 0, low, high), jnp.where(core == 0, high, low)


def feed_kernel(fine, where, *refs):
    ins, rows_in, up_shift = refs[:7], refs[7], refs[8]
    layer_out, layer_half, d_middle, d_own, d_sibling = refs[9:14]
    grads_out = refs[14:-16]
    held, rays, ctxs, upstream, w_out, w_up, w_down, low_out, low_mid, own, sibling = refs[-16:-5]
    halves, active, lifted, sem_in, sem_out = refs[-5:]
    lat, core, side = where[0], where[1], where[2]
    half, width = rays.shape
    hidden = w_up.shape[1]
    block = half // 4
    mine = pl.ds(pl.multiple_of(core * half, half), half)
    sources = [ins[6], ins[0].at[mine]] + list(ins[1:5]) + [ins[5].at[mine]]
    targets = [held, rays] + [ctxs.at[j] for j in range(LATS)] + [upstream]
    loads = [
        pltpu.make_async_copy(a, b, sem_in.at[n]) for n, (a, b) in enumerate(zip(sources, targets))
    ]
    stores = []

    def store(source, target):
        stores.append(pltpu.make_async_copy(source, target, sem_out.at[len(stores)]))
        stores[-1].start()

    for load in loads:
        load.start()
    for load in loads[:6]:
        load.wait()
    if held.ndim == 3:
        shard = held.shape[1] // 5
        piece = lambda n, count=1: held[:, n * shard : (n + count) * shard, :]
    else:
        piece = lambda n, count=1: held[n * width : (n + count) * width, :]
    w_out[...] = piece(2).reshape(width, width)
    w_up[:, :width] = piece(3).reshape(width, width)
    w_up[:, width:] = piece(4).reshape(width, width)
    w_down[...] = piece(0, 2).reshape(hidden, width)
    gain, bias = rows_in[2:3, :], rows_in[3:4, :]
    spots = [pl.ds(pl.multiple_of((lat ^ j) * OWN, OWN), OWN) for j in range(LATS)]

    def ctx_rows(j, i):
        at = slice((i % 2) * block, (i % 2 + 1) * block)
        return ctxs[j, at, (i // 2) * OWN : (i // 2 + 1) * OWN]

    begun = []
    for i in range(4):
        at = slice(i * block, (i + 1) * block)
        middle = rays[at, :].astype(F32) + rows_in[4:5, :]
        for j in range(LATS):
            middle = middle + dot(ctx_rows(j, i), w_out[spots[j], :])
        normed, factor = norm_parts(middle)
        lifted[at, :] = (normed * gain + bias).astype(BF)
        begun.append((middle, normed, factor))
    for load in loads[6:]:
        load.wait()
    column = lambda v: jnp.sum(v, axis=0, keepdims=True)
    sums, up_sums = [0.0] * 4, 0.0
    for i in range(4):
        at = slice(i * block, (i + 1) * block)
        middle, normed, factor = begun[i]
        before = dot(lifted[at, :], w_up[...]) + up_shift[...]
        squared = before * before
        bent = jnp.tanh(before * (ROOT + (ROOT * 0.044715) * squared))
        scaled = 0.5 * before
        act = (scaled + scaled * bent).astype(BF)
        active[at, :] = act
        slope = 0.5 + 0.5 * bent + scaled * (1.0 - bent * bent) * (
            ROOT + (3 * 0.044715 * ROOT) * squared
        )
        d_pre = (dot_rt(upstream[at, :], w_down[...]) * slope).astype(BF)
        halves[at, :hidden] = d_pre
        low_out[at, :] = (middle + dot(act, w_down[...]) + rows_in[5:6, :]).astype(BF)
        d_lifted = dot_rt(d_pre, w_up[...])
        up_wide = upstream[at, :].astype(F32)
        d_mid = up_wide + norm_back(d_lifted, normed, factor, gain)
        branch = d_mid.astype(BF)
        low_mid[at, :] = branch
        halves[at, hidden:] = branch
        gap = jnp.zeros((block, 2 * LANES - OWN), F32)
        for target, spot in zip((own, sibling), spots):
            part = dot_rt(branch, w_out[spot, :])
            target[at, :] = jnp.concatenate([part, gap], axis=1).astype(BF)
        pieces = (d_lifted * normed, d_lifted, branch.astype(F32), up_wide)
        sums = [total + column(piece) for total, piece in zip(sums, pieces)]
        up_sums = up_sums + column(d_pre.astype(F32))
    store(sibling, d_sibling)
    store(own, d_own)
    store(low_out, layer_half)
    store(low_out, layer_out.at[mine])
    store(low_mid, d_middle)

    wide, narrow = hidden // 2, width // 2
    pre_half = halves[:, pl.ds(pl.multiple_of(side * wide, LANES), wide)]
    branch_half = halves[:, pl.ds(pl.multiple_of(hidden + side * narrow, LANES), narrow)]
    up_half = upstream[:, pl.ds(pl.multiple_of(side * narrow, LANES), narrow)]
    up_grad = dot_lt(lifted[...], pre_half)
    down_grad = dot_lt(active[...], up_half)
    if fine:
        messages = grads_out[2:]
        scenes = messages[0].shape[0]
        shard = width // (scenes * LATS)

        def parities(values, rows):
            parts = [values[n * rows : (n + 1) * rows] for n in range(LATS)]
            even = jnp.concatenate([parts[0], parts[2]], axis=0)
            odd = jnp.concatenate([parts[1], parts[3]], axis=0)
            first, second = jnp.where(core == 0, even, odd), jnp.where(core == 0, odd, even)
            return zip(messages, (first.astype(BF), second.astype(BF)))

        for s in range(scenes):
            rows = LATS * shard
            for message, part in parities(up_grad[s * rows : (s + 1) * rows], shard):
                message[s, 2 * shard : 4 * shard, :] = part[:, :narrow]
                message[s, 4 * shard : 6 * shard, :] = part[:, narrow:]
            rows = 2 * LATS * shard
            for message, part in parities(down_grad[s * rows : (s + 1) * rows], 2 * shard):
                message[s, 6 * shard : 10 * shard, :] = part
        for j in range(LATS):
            ctx = jnp.concatenate([ctxs[j, :, :OWN], ctxs[j, :, OWN:]], axis=0)
            values = dot_lt(ctx, branch_half)
            rows = LATS * shard
            for q in range(OWN // rows):
                place = (lat ^ j) * (OWN // rows) + q
                for message, part in parities(values[q * rows : (q + 1) * rows], shard):
                    message[place, : 2 * shard, :] = part
        lines = line_up(sums, up_sums, scenes * LATS)
        for s in range(scenes):
            line = lines[s * LATS : (s + 1) * LATS]
            even = jnp.concatenate([line[0:1], line[2:3]], axis=0)
            odd = jnp.concatenate([line[1:2], line[3:4]], axis=0)
            for n, message in enumerate(messages):
                rows = jnp.where(core == n, even, odd)
                rows = jnp.concatenate([rows, jnp.zeros((14, OWN), F32)], axis=0)
                rows = jnp.concatenate([rows, jnp.zeros_like(rows)], axis=1)
                message[s, 10 * shard :, :] = rows.astype(BF)
        for message, target in zip(messages, grads_out):
            store(message, target)
    else:
        for i, part in ((1, up_grad), (2, down_grad)):
            first, second = quarter_halves(part, core)
            grads_out[2 * i][...] = first.astype(BF)
            grads_out[2 * i + 1][...] = second.astype(BF)
        for j in range(LATS):
            ctx = jnp.concatenate([ctxs[j, :, :OWN], ctxs[j, :, OWN:]], axis=0)
            first, second = quarter_halves(dot_lt(ctx, branch_half), core)
            grads_out[0][spots[j], :] = first.astype(BF)
            grads_out[1][spots[j], :] = second.astype(BF)
        grads_out[6][...] = jnp.concatenate(sums + [jnp.zeros((4, width), F32)], axis=0)
        grads_out[7][...] = jnp.broadcast_to(up_sums, (8, hidden))
    for copy in stores:
        copy.wait()


def line_up(sums, up_sums, sources):
    total = None
    shard = sums[0].shape[1] // sources
    for rows, size, first in ((sums, shard, 2), ([up_sums], 2 * shard, 6)):
        wide = rows[0].shape[1]
        col = lax.broadcasted_iota(jnp.int32, (1, wide), 1).astype(F32)
        owner = jnp.floor((col + 0.5) * (1.0 / size))
        spot = (col - owner * size)
        row = lax.broadcasted_iota(jnp.int32, (OWN, 1), 0).astype(F32)
        line = lax.broadcasted_iota(jnp.int32, (sources, 1), 0).astype(F32)
        for v, values in enumerate(rows):
            hot = jnp.where(row == spot + (first + v) * shard, 1.0, 0.0).astype(BF)
            mine = jnp.where(line == owner, values, 0.0).astype(BF)
            part = dot_rt(mine, hot)
            total = part if total is None else total + part
    return total


def feed(where, rays, ctxs, upstream, weights, rows_in, up_shift, scenes, fine):
    count, width = rays.shape
    hidden = up_shift.shape[1]
    half = count // 2
    mats = [(width, width // 4), (width, hidden // 4), (hidden, width // 4)]
    if fine:
        message = (scenes, 10 * (width // (scenes * LATS)) + 16, width // 2)
        grads = [shape(message)] * 2
        spec, held = ANY, [pltpu.VMEM(message, BF)] * 2
    else:
        grads = [shape(d) for d in mats for _ in range(2)]
        grads += [shape((8, width), F32), shape((8, hidden), F32)]
        spec, held = pl.BlockSpec(memory_space=pltpu.VMEM), []
    return pl.pallas_call(
        partial(feed_kernel, fine),
        out_shape=[
            shape((count, width)),
            shape((half, width)),
            shape((half, width)),
            shape((half, 2 * LANES)),
            shape((half, 2 * LANES)),
        ]
        + grads,
        in_specs=[SMEM] + [ANY] * 7 + vmem(2),
        out_specs=[ANY] * 5 + [spec] * len(grads),
        scratch_shapes=held
        + [
            pltpu.VMEM(weights.shape, BF),
            pltpu.VMEM((half, width), BF),
            pltpu.VMEM((LATS, half // 2, 2 * OWN), BF),
            pltpu.VMEM((half, width), BF),
            pltpu.VMEM((width, width), BF),
            pltpu.VMEM((width, hidden), BF),
            pltpu.VMEM((hidden, width), BF),
            pltpu.VMEM((half, width), BF),
            pltpu.VMEM((half, width), BF),
            pltpu.VMEM((half, 2 * LANES), BF),
            pltpu.VMEM((half, 2 * LANES), BF),
            pltpu.VMEM((half, hidden + width), BF),
            pltpu.VMEM((half, hidden), BF),
            pltpu.VMEM((half, width), BF),
            pltpu.SemaphoreType.DMA((7,)),
            pltpu.SemaphoreType.DMA((8,)),
        ],
        compiler_params=params(),
        cost_estimate=cost(26),
        name="feed",
    )(where, rays, *ctxs, upstream, weights, rows_in, up_shift)


def halve_kernel(bit, where, own, got, send, keep):
    count = send.shape[0]
    mine = where[4] if count == 4 else where[6]
    low = (1 << bit) - 1
    for n in range(count):
        first = ((n & ~low) << 1) | (n & low)
        for target, side in ((send, 1 - mine), (keep, mine)):
            at = first + (side << bit)
            target[n] = (own[at].astype(F32) + got[at].astype(F32)).astype(BF)


def halve(where, bit, own, got):
    count, rows, cols = own.shape
    half = shape((count // 2, rows, cols))
    return pl.pallas_call(
        partial(halve_kernel, bit),
        out_shape=[half, half],
        in_specs=[SMEM] + vmem(2),
        out_specs=vmem(2),
        compiler_params=params(),
        cost_estimate=cost(3),
        name="halve",
    )(where, own, got)


def spread_kernel(count, where, *refs):
    pairs, (feed_keep, feed_got), out = refs[: 2 * count], refs[2 * count : 2 * count + 2], refs[-6:]
    for k in range(4):
        at = where[5] ^ k
        parts = [
            pairs[2 * n][at].astype(F32) + pairs[2 * n + 1][at].astype(F32) for n in range(count)
        ]
        out[k][...] = jnp.concatenate(parts, axis=0).astype(BF)
    mine = where[5] % 2
    for target, at in ((out[4], 1 - mine), (out[5], mine)):
        target[...] = (feed_keep[at].astype(F32) + feed_got[at].astype(F32)).astype(BF)


def add_spread(where, pairs, feed_keep, feed_got, after):
    rows = sum(keep.shape[1] for keep, _ in pairs)
    last = shape(feed_keep.shape[1:])
    return pl.pallas_call(
        partial(spread_kernel, len(pairs)),
        out_shape=[shape((rows, pairs[0][0].shape[2]))] * 4 + [last] * 2,
        in_specs=[SMEM] + vmem(2 * len(pairs) + 2) + [ANY] * len(after),
        out_specs=vmem(6),
        compiler_params=params(),
        cost_estimate=cost(2),
        name="add_spread",
    )(where, *[a for pair in pairs for a in pair], feed_keep, feed_got, *after)


def regroup_kernel(shard, where, *refs):
    trio, out, held = refs[:4], refs[6:10], refs[10]
    side = where[2]
    block = LATS * shard
    total = sum(r[...].astype(F32) for r in trio)
    pair, third = total[: 3 * block + 16], unfold(total[3 * block + 16 :])
    held[...] = jnp.concatenate([pair, third[: 3 * block + 16]], axis=1)
    feed_sum = refs[4][...].astype(F32) + refs[5][...].astype(F32)
    places = [[], []]
    for q in range(2):
        for first, rows in ((0, shard), (2 * shard, shard), (4 * shard, shard), (6 * shard, 2 * shard)):
            places[q].append(feed_sum[first + q * rows : first + (q + 1) * rows])
        line = feed_sum[10 * shard + q : 10 * shard + q + 1]
        places[q].append(jnp.broadcast_to(line, (8, line.shape[1])))
    places = [jnp.concatenate(p, axis=0) for p in places]
    for k in range(LATS):
        rows = []
        for n in range(3):
            at = n * block + (where[0] ^ k) * shard
            rows.append(held[pl.ds(pl.multiple_of(at, 8), shard), :])
        rows.append(held[3 * block : 3 * block + 8, :])
        rows.append(jnp.zeros((16, OWN), F32))
        value = fold(jnp.concatenate(rows, axis=0))
        if k % 2 == 0:
            mine = jnp.where(side == (k // 2), places[0], places[1])
            value = jnp.concatenate([value, mine], axis=0)
        out[k][...] = value.astype(BF)


def regroup(where, trio, feed_keep, feed_got, shard):
    small = (3 * shard + 24) // 2
    large = small + 5 * shard + 8
    return pl.pallas_call(
        partial(regroup_kernel, shard),
        out_shape=[shape((rows, 2 * OWN)) for rows in (large, small, large, small)],
        in_specs=[SMEM] + vmem(6),
        out_specs=vmem(LATS),
        scratch_shapes=[pltpu.VMEM((3 * LATS * shard + 16, OWN), F32)],
        compiler_params=params(),
        cost_estimate=cost(2),
        name="regroup",
    )(where, *trio, feed_keep, feed_got)


def settle_kernel(shard, where, got0, got1, got2, got3, w_query, gain, bias, *out):
    lat, side = where[0], where[2]
    mats, firsts, rest = out[-13:-7], out[-7:-5], out[-5:]
    got = [g[...].astype(F32) for g in (got0, got1, got2, got3)]
    small = got[1].shape[0]
    here, there = got[0][small:], got[2][small:]
    left, right = jnp.where(side == 0, here, there), jnp.where(side == 0, there, here)
    both = lambda a, b: jnp.concatenate([left[a:b], right[a:b]], axis=1)
    got = [unfold(g[:small]) for g in got]
    whole = jnp.concatenate([choose(lat ^ p, got) for p in range(LATS)], axis=1)
    part = lambda n: whole[n * shard : (n + 1) * shard]
    sums = whole[3 * shard : 3 * shard + 1] + whole[3 * shard + 1 : 3 * shard + 2]
    weight = w_query[...].astype(F32)
    mats[0][...] = part(0) * gain[...] + bias[...] * sums
    mats[1][...] = part(1)
    mats[2][...] = part(2)
    mats[3][...] = both(0, shard)
    cols = [half[n * shard : (n + 1) * shard] for half in (left, right) for n in (1, 2)]
    mats[4][...] = jnp.concatenate(cols, axis=1)
    mats[5][...] = both(3 * shard, 5 * shard)
    firsts[0][...] = jnp.sum((part(0) * weight).T, axis=0)
    firsts[1][...] = jnp.sum((weight * sums).T, axis=0)
    line = here[5 * shard : 5 * shard + 1]
    for target, (first, count) in zip(rest, ((2, 1), (3, 1), (4, 1), (6, 2), (5, 1))):
        target[...] = line[:, first * shard : (first + count) * shard].reshape(count * shard)


def settle(where, got, w_query, gain, bias, after):
    shard, width = w_query.shape
    flat = shape((shard, width), F32)
    tall = shape((2 * shard, width), F32)
    wide = shape((shard, 2 * width), F32)
    return pl.pallas_call(
        partial(settle_kernel, shard),
        out_shape=[flat] * 4
        + [wide, tall]
        + [shape((n * shard,), F32) for n in (1, 1, 1, 1, 1, 2, 1)],
        in_specs=[SMEM] + vmem(7) + [ANY] * len(after),
        out_specs=vmem(13),
        compiler_params=params(),
        cost_estimate=cost(2),
        name="settle",
    )(where, *got, w_query, gain, bias, *after)


def place_rows(where, h, j):
    first = (where[0] ^ j) * OWN + h * HEAD_DIM
    return pl.ds(pl.multiple_of(first, HEAD_DIM), HEAD_DIM)


def first_grads_kernel(parts, where, rows_in, rays_in, middle_in, turned, *refs):
    msgs, (ray_grad, ray_half) = refs[:12], refs[-9:-7]
    rays, middle, weight, d_query, low, sem_in, sem_out = refs[-7:]
    half, width = rays.shape
    tail = d_query.shape[1]
    first_row = pl.multiple_of(where[1] * half, half)
    loads = []

    def load(source, target):
        loads.append(pltpu.make_async_copy(source, target, sem_in.at[len(loads)]))
        loads[-1].start()

    load(turned.at[:, 0], weight)
    for h in range(OWN_HEADS):
        for j in range(LATS):
            source = msgs[h * LATS + j]
            load(source.at[:, source.shape[1] - tail :], d_query.at[place_rows(where, h, j)])
    for first, last in parts:
        at = pl.ds(first, last - first)
        load(rays_in.at[pl.ds(first_row + first, last - first)], rays.at[at])
        load(middle_in.at[at], middle.at[at])
    for copy in loads[:13]:
        copy.wait()
    matrix = weight[...].reshape(width, width)
    stores = []
    for n, (first, last) in enumerate(parts):
        for copy in loads[13 + 2 * n : 15 + 2 * n]:
            copy.wait()
        at = slice(first, last)
        d_lifted = dot_lt(d_query[:, at], matrix)
        normed, factor = norm_parts(rays[at, :].astype(F32))
        back = norm_back(d_lifted, normed, factor, rows_in[0:1, :])
        low[at, :] = (middle[at, :].astype(F32) + back).astype(BF)
        source = low.at[pl.ds(first, last - first)]
        for target in (
            ray_half.at[pl.ds(first, last - first)],
            ray_grad.at[pl.ds(first_row + first, last - first)],
        ):
            stores.append(pltpu.make_async_copy(source, target, sem_out.at[len(stores)]))
            stores[-1].start()
    for copy in stores:
        copy.wait()


def first_grads(where, rays, turned, rows_in, d_middle, msgs, lat_rows, after):
    count, width = rays.shape
    half = count // 2
    parts = [(a, min(a + 256, half)) for a in range(0, half, 256)]
    tail = msgs[0][0].shape[1] - 2 * lat_rows
    return pl.pallas_call(
        partial(first_grads_kernel, parts),
        in_specs=[SMEM] + vmem(1) + [ANY] * (15 + len(after)),
        out_specs=[ANY] * 2,
        out_shape=[shape((count, width)), shape((half, width))],
        scratch_shapes=[
            pltpu.VMEM((half, width), BF),
            pltpu.VMEM((half, width), BF),
            pltpu.VMEM((LATS, OWN, width), BF),
            pltpu.VMEM((width, tail), BF),
            pltpu.VMEM((half, width), BF),
            pltpu.SemaphoreType.DMA((13 + 2 * len(parts),)),
            pltpu.SemaphoreType.DMA((2 * len(parts),)),
        ],
        compiler_params=params(),
        cost_estimate=cost(6),
        name="first_grads",
    )(where, rows_in, rays, d_middle, turned, *[m for group in msgs for m in group], *after)


def latent_kernel(where, turned, *refs):
    msgs, (out, weight, held, sem) = refs[:12], refs[-4:]
    _, width, lat_rows = held.shape
    loads = [[], []]
    for i in range(2):
        copies = [(turned.at[:, 1 + i], weight.at[i])]
        for h in range(OWN_HEADS):
            for j in range(LATS):
                source = msgs[h * LATS + j].at[:, i * lat_rows : (i + 1) * lat_rows]
                copies.append((source, held.at[i, place_rows(where, h, j)]))
        for source, target in copies:
            at = sem.at[i, len(loads[i])]
            loads[i].append(pltpu.make_async_copy(source, target, at))
            loads[i][-1].start()
    for copy in loads[0]:
        copy.wait()
    total = dot_lt(held[0], weight[0].reshape(width, width))
    for copy in loads[1]:
        copy.wait()
    total = total + dot_lt(held[1], weight[1].reshape(width, width))
    out[...] = total[: out.shape[0]].astype(BF)


def latent_grads(where, turned, msgs, rows, lat_rows, after):
    width = turned.shape[3]
    return pl.pallas_call(
        latent_kernel,
        in_specs=[SMEM] + [ANY] * (13 + len(after)),
        out_specs=pl.BlockSpec(memory_space=pltpu.VMEM),
        out_shape=shape((rows, width)),
        scratch_shapes=[
            pltpu.VMEM((2, LATS, OWN, width), BF),
            pltpu.VMEM((2, width, lat_rows), BF),
            pltpu.SemaphoreType.DMA((2, 13)),
        ],
        compiler_params=params(),
        cost_estimate=cost(6),
        name="latent_grads",
    )(where, turned, *msgs, *after)


def join(where, full, there):
    first = (1 - where[1]) * there.shape[0]
    return lax.dynamic_update_slice(full, there, (first, jnp.int32(0)))


def body(
    rays,
    latents,
    view_count,
    view_mask,
    cotangent,
    w_query,
    w_key,
    w_value,
    w_out,
    w_up,
    w_down,
    first_gain,
    first_bias,
    second_gain,
    second_bias,
    out_bias,
    up_bias,
    down_bias,
):
    scenes = lax.axis_size("scene")
    lat, scene = lax.axis_index("lat"), lax.axis_index("scene")
    core, side = lat % 2, lat // 2
    where = jnp.stack([lat, core, side, scene, scene % 2, scene // 2, scene // 4])
    where = where.astype(jnp.int32)
    count, width = rays.shape
    hidden = w_up.shape[1]
    lat_rows = latents.shape[0]
    lat_pad = -(-lat_rows // LANES) * LANES
    shard = w_query.shape[0]
    fine = shard % 8 == 0 and scenes == 8

    normed_low, *stats = make_norms(where, rays)
    vectors = [first_gain, first_bias, second_gain, second_bias, out_bias, down_bias, up_bias]
    (trio, turned, rows_in, up_shift), own_lat, passed = attention_weights(
        where, w_query, w_key, w_value, vectors, latents, lat_pad, [normed_low]
    )

    near_lat, far_lat = swap(own_lat, "lat", 1), swap(own_lat, "lat", 2)

    weights_in = feed_weights(w_out, w_up, w_down, passed)

    spot = jnp.arange(lat_pad, dtype=jnp.int32)
    block_of = lat ^ jnp.arange(LATS, dtype=jnp.int32)
    view_of = (block_of[:, None] * lat_rows + spot[None, :]) // VIEW_TOK
    matches = view_of[..., None] == jnp.arange(VIEWS, dtype=jnp.int32)
    listed = jnp.sum(jnp.where(matches, view_mask[0], 0), axis=-1) > 0
    live = listed & (view_of < view_count[0]) & (spot < lat_rows)[None, :]
    shut = jnp.where(live, 0.0, DEAD).astype(F32).reshape(LATS, 1, lat_pad)


    keyset = make_keyset(0, [own_lat, near_lat], trio, shut)
    query = make_queries(where, rays, *stats, trio, rows_in)
    far_lat = gate(far_lat, [query, keyset[0]])
    last_lat = swap(far_lat, "lat", 1)
    lats = [own_lat, near_lat, far_lat, last_lat]
    keyset = make_keyset(2, [far_lat], trio, shut, keyset)
    key, key_t, val, val_t = make_keyset(3, [last_lat], trio, shut, keyset)
    there_ctx, there_wide, weights, inverse = attend(1, query, key_t, val)
    near, far = swap(there_ctx, "lat", 1), swap(there_ctx, "lat", 3)
    here_ctx, here_wide, weights, inverse = attend(0, query, key_t, val, (weights, inverse))
    here_ctx = gate(here_ctx, [near, far])
    ctxs = [here_ctx, near, swap(here_ctx, "lat", 2), far]

    turned = lax.all_gather(gate(turned, ctxs[2:]), "lat", axis=0, tiled=False)
    layer_out, out_half, d_middle, d_own, d_sibling, *feed_out = feed(
        where, rays, ctxs, cotangent, weights_in, rows_in, up_shift, scenes, fine
    )
    d_there = swap(d_sibling, "lat", 1)
    out_there = swap(out_half, "lat", 1)
    layer_out = join(where, layer_out, out_there)
    if fine:
        own_msg, sib_msg = feed_out
        feed_send, feed_keep = halve(where, 0, own_msg, swap(sib_msg, "lat", 1))
        feed_got = swap(feed_send, "scene", 1)

    got, grads, after, got_own = [], [], [], ()
    for h in range(OWN_HEADS):
        if h == 1:
            after = after + [out_there] + ([feed_send] if fine else [])
        elif h == 2:
            after = after + got[0][1:]
            if fine:
                feed_keep = gate(feed_keep, after)
                feed_send, feed_keep = halve(where, 1, feed_keep, feed_got)
                feed_got = swap(feed_send, "scene", 4)
                after = after + [feed_send]
        out = attend_back(
            h,
            fine,
            weights,
            inverse,
            (d_own, d_there),
            (here_wide, there_wide),
            query,
            key,
            val_t,
            lats,
            normed_low,
            got_own,
            where,
            after,
        )
        if h == 2:
            out = gate(list(out), got[1][1:] + ([pair_got, feed_got] if fine else []))
        after = [out[0]]
        got_own = out[:LATS]
        grads += out[LATS:]
        if h == 1 and fine:
            pair_got = swap(grads[0], "scene", 1)
        got.append([out[0]] + [swap(out[k], "lat", k) for k in range(1, LATS)])
    after = []
    if fine:
        pairs = [(grads[1], pair_got), (grads[3], swap(grads[2], "scene", 1))]
        *late, feed_send, feed_keep = add_spread(where, pairs, feed_keep, feed_got, [layer_out])
        after = [late[0]]
        feed_got = swap(feed_send, "scene", 2)
        late = [late[0]] + [swap(late[k], "scene", 2 * k) for k in range(1, 4)]
    ray_grad, ray_half = first_grads(where, rays, turned, rows_in, d_middle, got, lat_pad, after)
    if fine:
        ray_half = gate(ray_half, late[1:] + [feed_got])
    ray_grad = join(where, ray_grad, swap(ray_half, "lat", 1))
    if fine:
        final = regroup(where, late, feed_keep, feed_got, shard)
        after = [final[0]]
    latent_grad = latent_grads(
        where, turned, [m for g in got for m in g], lat_rows, lat_pad, after
    )
    first = [v.reshape(shard, 1).astype(F32) for v in (first_gain, first_bias)]
    if fine:
        final = [final[0]] + [swap(final[k], "lat", k) for k in range(1, LATS)]
        small = settle(where, final, w_query, *first, [latent_grad])
    else:
        joined = jnp.concatenate(grads, axis=1)
        grads = joined[: 3 * width].reshape(3, width, OWN), joined[3 * width :]
        small = plain_final(feed_out, grads, scenes, shard, w_query, *first)
    return (layer_out, ray_grad, latent_grad, *small)


def plain_final(feed_out, grads, scenes, shard, w_query, gain, bias):
    lat = lax.axis_index("lat")
    out_own, out_sib, up_own, up_sib, down_own, down_sib, sums, up_sums = feed_out
    trio, query_sums = grads

    def by_scene(out_part, up_part, down_part):
        parts = [
            out_part.reshape(scenes, -1, OWN),
            up_part.reshape(scenes, -1, 2, OWN).swapaxes(1, 2).reshape(scenes, -1, OWN),
            down_part.reshape(scenes, -1, OWN),
        ]
        return jnp.concatenate(parts, axis=1).astype(F32)

    feed_part = by_scene(out_own, up_own, down_own)
    feed_part = feed_part + swap(by_scene(out_sib, up_sib, down_sib), "lat", 1)
    feed_part = scatter_scene(feed_part)
    block = LATS * shard
    trio = trio.reshape(3, scenes, block, OWN).swapaxes(0, 1).reshape(scenes, 3 * block, OWN)
    lines = [v.reshape(scenes, LATS, shard) for v in sums[:4]]
    lines = [jnp.zeros_like(lines[0])] * 2 + lines + [up_sums[0].reshape(scenes, LATS, 2 * shard)]
    lines = jnp.concatenate(lines, axis=2)
    lines = jnp.pad(lines, ((0, 0), (0, 0), (0, OWN - 8 * shard)))
    cols = jnp.broadcast_to(query_sums[:2], (scenes, 2, OWN))
    late = scatter_scene(jnp.concatenate([trio.astype(F32), cols, lines], axis=1))
    mats = [late[i * block : (i + 1) * block].reshape(LATS, shard, OWN) for i in range(3)]
    mats += [feed_part[i * block : (i + 1) * block].reshape(LATS, shard, OWN) for i in range(3)]
    mats.append(feed_part[3 * block :].reshape(LATS, 2 * shard, OWN))
    mats.append(jnp.broadcast_to(late[3 * block : 3 * block + 2], (LATS, 2, OWN)))
    mats.append(late[3 * block + 2 :].reshape(LATS, 1, OWN))
    final = jnp.concatenate(mats, axis=1).astype(BF)
    sent = [lax.dynamic_index_in_dim(final, lat ^ k, 0, keepdims=False) for k in range(LATS)]
    got = [sent[0]] + [swap(sent[k], "lat", k) for k in range(1, LATS)]
    got = [g.astype(F32) for g in got]
    line = got[0][-1] + got[1][-1]
    cols = in_order(jnp.stack(got), list(range(LATS)), lat)
    joined = jnp.transpose(cols, (1, 0, 2)).reshape(cols.shape[1], -1)
    part = lambda n, count=1: joined[n * shard : (n + count) * shard]
    up = cols[:, 4 * shard : 6 * shard].reshape(LATS, 2, shard, OWN)
    up = jnp.transpose(up, (2, 0, 1, 3)).reshape(shard, -1)
    sums = joined[8 * shard : 8 * shard + 1] + joined[8 * shard + 1 : 8 * shard + 2]
    weight = w_query.astype(F32)
    piece = lambda i, n=1: line[i * shard : (i + n) * shard]
    return (
        part(0) * gain + bias * sums,
        part(1),
        part(2),
        part(3),
        up,
        part(6, 2),
        jnp.sum(part(0) * weight, axis=1),
        jnp.sum(weight * sums, axis=1),
        piece(2),
        piece(3),
        piece(4),
        piece(6, 2),
        piece(5),
    )


def solution(mesh):
    rows = P(("scene", "lat"), None)
    line = P(("scene", "lat"))
    scene = P("scene", None)
    in_specs = (scene, rows, P("scene"), scene, scene) + (rows,) * 6 + (line,) * 7
    out_specs = (scene, scene, rows) + (rows,) * 6 + (line,) * 7
    return jax.shard_map(body, mesh=mesh, in_specs=in_specs, out_specs=out_specs, check_vma=False)
```

```python
import math
from functools import partial

import jax
import jax.numpy as jnp
from jax import lax
from jax.experimental import pallas as pl
from jax.experimental.pallas import tpu as pltpu
from jax.sharding import PartitionSpec as P

HEADS = 12
HEAD_DIM = 64
VIEWS = 10
VIEW_TOK = 300
LANES = 128
LATS = 4
OWN_HEADS = HEADS // LATS
OWN = OWN_HEADS * HEAD_DIM
DEAD = -1e30
LOG2E = math.log2(math.e)
Q_SCALE = 0.125 * LOG2E
ROOT = math.sqrt(2.0 / math.pi)
SCALE = 1.0
VMEM_BYTES = 64 * 2**20 - 2**16
BF = jnp.bfloat16
F32 = jnp.float32


def dot(left, right):
    return jnp.dot(left, right, preferred_element_type=F32)


def dot_rt(left, right):
    return lax.dot_general(left, right, (((1,), (1,)), ((), ())), preferred_element_type=F32)


def dot_lt(left, right):
    return lax.dot_general(left, right, (((0,), (0,)), ((), ())), preferred_element_type=F32)


def params():
    return pltpu.CompilerParams(vmem_limit_bytes=VMEM_BYTES)


def cost(micros):
    return pl.CostEstimate(
        flops=int(micros * SCALE * 1e9), bytes_accessed=int(micros * SCALE * 3.3e6), transcendentals=0
    )


def vmem(count):
    return [pl.BlockSpec(memory_space=pltpu.VMEM)] * count


ANY = pl.BlockSpec(memory_space=pl.ANY)
SMEM = pl.BlockSpec(memory_space=pltpu.SMEM)


def shape(dims, dtype=BF):
    return jax.ShapeDtypeStruct(tuple(dims), dtype)


def norm_parts(values):
    center = values - jnp.mean(values, axis=-1, keepdims=True)
    spread = jnp.mean(center * center, axis=-1, keepdims=True)
    factor = lax.rsqrt(spread + 1e-05)
    return center * factor, factor


def norm_back(grad_out, normed, factor, gain_row):
    scaled = grad_out * gain_row
    return factor * (
        scaled
        - jnp.mean(scaled, axis=-1, keepdims=True)
        - normed * jnp.mean(scaled * normed, axis=-1, keepdims=True)
    )


def swap(values, axis, step):
    count = lax.axis_size(axis)
    return lax.ppermute(values, axis, [(i, i ^ step) for i in range(count)])


def stages(count):
    found, stride = [], count
    while stride > 1:
        group = 4 if stride % 4 == 0 else 2
        stride //= group
        found.append((stride, group))
    return found


def collect_kernel(count, *refs):
    out, rows = refs[-1], 0
    for ref in refs[:count]:
        out[rows : rows + ref.shape[0]] = ref[...]
        rows += ref.shape[0]


def collect(values, after):
    rows = sum(v.shape[0] for v in values)
    return pl.pallas_call(
        partial(collect_kernel, len(values)),
        out_shape=shape((rows,) + values[0].shape[1:]),
        in_specs=vmem(len(values)) + [ANY] * len(after),
        out_specs=pl.BlockSpec(memory_space=pltpu.VMEM),
        compiler_params=params(),
        cost_estimate=cost(0.3),
        name="collect",
    )(*values, *after)


def gather_scene(parts, after=()):
    steps = [0]
    got = [parts]
    passed = []
    for stride, group in stages(lax.axis_size("scene")):
        if len(got) == 1:
            parts = got[0]
        else:
            parts = collect(got, after) if after else jnp.concatenate(got)
        got = [parts] + [swap(parts, "scene", k * stride) for k in range(1, group)]
        steps = [step ^ (k * stride) for k in range(group) for step in steps]
        passed = [parts]
    return got, steps, passed


def in_order(stacked, steps, me):
    places = [steps.index(i) for i in range(len(steps))]
    order = jnp.take(jnp.array(places, jnp.int32), jnp.arange(len(steps)) ^ me)
    return jnp.take(stacked, order, axis=0)


def scatter_scene(blocks):
    count = lax.axis_size("scene")
    me = lax.axis_index("scene")
    held = blocks
    for stride, group in reversed(stages(count)):
        digit = (me // stride) % group
        view = held.reshape((-1, group) + blocks.shape[1:])
        total = lax.dynamic_index_in_dim(view, digit, 1, keepdims=False).astype(F32)
        for k in range(1, group):
            mine = lax.dynamic_index_in_dim(view, digit ^ k, 1, keepdims=False)
            total = total + swap(mine.astype(BF), "scene", k * stride).astype(F32)
        held = total.astype(BF)
    return total.reshape(blocks.shape[1:])


def fold(rows):
    half = rows.shape[0] // 2
    return jnp.concatenate([rows[:half], rows[half:]], axis=1)


def unfold(rows):
    half = rows.shape[1] // 2
    return jnp.concatenate([rows[:, :half], rows[:, half:]], axis=0)


def choose(index, options):
    picked = options[0]
    for i in range(1, len(options)):
        picked = jnp.where(index == i, options[i], picked)
    return picked


def pack_kernel(where, w_query, w_key, w_value, *refs):
    vectors, out = refs[:-LATS], refs[-LATS:]
    values = [w[...].astype(F32) for w in (w_query, w_key, w_value)]
    line = [v[...].astype(F32).reshape(1, v.shape[0]) for v in vectors]
    line = jnp.concatenate(line, axis=1)
    line = jnp.concatenate([line, jnp.zeros((1, OWN - line.shape[1]), F32)], axis=1) if (
        line.shape[1] < OWN
    ) else line
    tail = jnp.broadcast_to(line, (8, OWN))
    for k in range(LATS):
        target = where[0] ^ k
        rows = []
        for value in values:
            cols = [value[:, p * OWN : (p + 1) * OWN] for p in range(LATS)]
            rows.append(choose(target, cols))
        out[k][...] = fold(jnp.concatenate(rows + [tail], axis=0)).astype(BF)


def pack(where, w_query, w_key, w_value, vectors):
    rows = 3 * w_query.shape[0] + 8
    return pl.pallas_call(
        pack_kernel,
        out_shape=[shape((rows // 2, 2 * OWN))] * LATS,
        in_specs=[SMEM] + vmem(3 + len(vectors)),
        out_specs=vmem(LATS),
        compiler_params=params(),
        cost_estimate=cost(0.5),
        name="pack",
    )(where, w_query, w_key, w_value, *vectors)


def unpack_kernel(steps, where, *refs):
    *chunks, trio, turned, rows_out, up_out, held, lines = refs
    lat, scene = where[0], where[3]
    shard = held.shape[1] // (len(steps) * LATS)
    entry = 0
    for chunk in chunks:
        for p in range(chunk.shape[0]):
            values = unfold(chunk[p].astype(F32))
            source = (scene ^ steps[entry // LATS]) * LATS + (lat ^ (entry % LATS))
            at = pl.ds(pl.multiple_of(source * shard, 8), shard)
            for m in range(3):
                held[m, at, :] = values[m * shard : (m + 1) * shard]
            lines[pl.ds(source, 1), :] = values[3 * shard : 3 * shard + 1]
            entry += 1
    for m in range(3):
        low = held[m].astype(BF)
        trio[m] = low
        turned[m] = held[m].T.astype(BF)
    sources = lines.shape[0]
    low = lines[...].astype(BF)
    for target, size, first in ((rows_out, shard, 0), (up_out, 2 * shard, 6)):
        wide = target.shape[1]
        col = lax.broadcasted_iota(jnp.int32, (1, wide), 1).astype(F32)
        owner = jnp.floor((col + 0.5) * (1.0 / size))
        spot = col - owner * size
        row = lax.broadcasted_iota(jnp.int32, (OWN, 1), 0).astype(F32)
        line = lax.broadcasted_iota(jnp.int32, (sources, 1), 0).astype(F32)
        for v in range(6 if first == 0 else 1):
            hot = jnp.where(row == spot + (first + v) * shard, 1.0, 0.0).astype(BF)
            spread = jnp.where(line == owner, dot(low, hot), 0.0)
            target[v : v + 1, :] = jnp.sum(spread, axis=0, keepdims=True)


def unpack(where, chunks, steps, shard):
    sources = len(steps) * LATS
    width = sources * shard
    return pl.pallas_call(
        partial(unpack_kernel, steps),
        out_shape=[
            shape((3, width, OWN)),
            shape((3, OWN, width)),
            shape((8, width), F32),
            shape((1, 2 * width), F32),
        ],
        in_specs=[SMEM] + vmem(len(chunks)),
        out_specs=vmem(4),
        scratch_shapes=[pltpu.VMEM((3, width, OWN), F32), pltpu.VMEM((sources, OWN), F32)],
        compiler_params=params(),
        cost_estimate=cost(0.5),
        name="unpack",
    )(where, *chunks)


def attention_weights(where, w_query, w_key, w_value, vectors, latents, lat_pad, early):
    shard, width = w_query.shape
    if shard % 8 == 0:
        pieces = pack(where, w_query, w_key, w_value, vectors)
        pieces = [pieces[0]] + [swap(pieces[k], "lat", k) for k in range(1, LATS)]
        own_lat = pad_latents(latents, lat_pad, pieces[2:])
        stacked = collect([p[None] for p in pieces], ())
        chunks, steps, passed = gather_scene(stacked, [own_lat] + early)
        return unpack(where, chunks, steps, shard), own_lat, [stacked] + passed
    flat = jnp.concatenate(vectors)
    flat = jnp.pad(flat, (0, OWN - flat.shape[0])).reshape(1, OWN)
    lat, scene = lax.axis_index("lat"), lax.axis_index("scene")
    scenes = lax.axis_size("scene")
    trio = jnp.stack([w_query, w_key, w_value]).reshape(3, shard, LATS, OWN)
    trio = jnp.transpose(trio, (2, 0, 1, 3)).reshape(LATS, 3 * shard, OWN)
    message = jnp.concatenate([trio, jnp.broadcast_to(flat, (LATS, 1, OWN))], axis=1)
    pieces = [lax.dynamic_index_in_dim(message, lat ^ k, 0, keepdims=False) for k in range(LATS)]
    pieces = [pieces[0]] + [swap(pieces[k], "lat", k) for k in range(1, LATS)]
    pieces = in_order(jnp.stack(pieces), list(range(LATS)), lat)
    chunks, steps, passed = gather_scene(pieces[None])
    gathered = in_order(jnp.concatenate(chunks), steps, scene)
    trio = gathered[:, :, : 3 * shard].reshape(scenes, LATS, 3, shard, OWN)
    trio = jnp.transpose(trio, (2, 0, 1, 3, 4)).reshape(3, width, OWN)
    lines = gathered[:, :, 3 * shard, : 8 * shard].astype(F32).reshape(scenes * LATS, 8, shard)
    rows = jnp.transpose(lines, (1, 0, 2)).reshape(8, width)
    up = lines[:, 6:].reshape(1, 2 * width)
    own_lat = pad_latents(latents, lat_pad, [])
    return (trio, jnp.transpose(trio, (0, 2, 1)), rows, up), own_lat, []


def gate_kernel(*refs):
    pass


def gate(values, after):
    one = not isinstance(values, list)
    values = [values] if one else values
    out = pl.pallas_call(
        gate_kernel,
        out_shape=[shape(v.shape, v.dtype) for v in values],
        in_specs=[ANY] * (len(values) + len(after)),
        out_specs=[ANY] * len(values),
        input_output_aliases={i: i for i in range(len(values))},
        compiler_params=params(),
        cost_estimate=cost(0.2),
        name="gate",
    )(*values, *after)
    return out[0] if one else list(out)


def pad_kernel(latents, *refs):
    out = refs[-1]
    rows = latents.shape[0]
    out[:rows, :] = latents[...]
    out[rows:, :] = jnp.zeros((out.shape[0] - rows, out.shape[1]), out.dtype)


def pad_latents(latents, rows, after):
    return pl.pallas_call(
        pad_kernel,
        out_shape=shape((rows, latents.shape[1])),
        in_specs=vmem(1) + [ANY] * len(after),
        out_specs=pl.BlockSpec(memory_space=pltpu.VMEM),
        compiler_params=params(),
        cost_estimate=cost(0.5),
        name="pad_latents",
    )(latents, *after)


def pack_feed_kernel(w_out, w_up, w_down, *refs):
    out = refs[-1]
    shard, width = w_out.shape
    out[: 2 * shard, :] = w_down[...]
    out[2 * shard : 3 * shard, :] = w_out[...]
    out[3 * shard : 4 * shard, :] = w_up[:, :width]
    out[4 * shard :, :] = w_up[:, width:]


def pack_feed(w_out, w_up, w_down, after):
    shard, width = w_out.shape
    return pl.pallas_call(
        pack_feed_kernel,
        out_shape=shape((5 * shard, width)),
        in_specs=vmem(3) + [ANY] * len(after),
        out_specs=pl.BlockSpec(memory_space=pltpu.VMEM),
        compiler_params=params(),
        cost_estimate=cost(0.3),
        name="pack_feed",
    )(w_out, w_up, w_down, *after)


def assemble_kernel(gathered, *refs):
    w_out, w_up, w_down = refs[-3:]
    shard = gathered.shape[1] // 5
    width = w_out.shape[1]
    w_down[...] = gathered[:, : 2 * shard, :].reshape(w_down.shape)
    w_out[...] = gathered[:, 2 * shard : 3 * shard, :].reshape(w_out.shape)
    w_up[:, :width] = gathered[:, 3 * shard : 4 * shard, :].reshape(width, width)
    w_up[:, width:] = gathered[:, 4 * shard :, :].reshape(width, width)


def assemble(gathered, after):
    width = gathered.shape[2]
    return pl.pallas_call(
        assemble_kernel,
        out_shape=[shape((width, width)), shape((width, 2 * width)), shape((2 * width, width))],
        in_specs=vmem(1) + [ANY] * len(after),
        out_specs=vmem(3),
        compiler_params=params(),
        cost_estimate=cost(6),
        name="assemble",
    )(gathered, *after)


def feed_weights(w_out, w_up, w_down, after):
    if w_out.shape[0] % 8 == 0:
        packed = gate(pack_feed(w_out, w_up, w_down, after[:1]), after[1:])
        return lax.all_gather(packed, ("scene", "lat"), axis=0, tiled=False)
    width = w_out.shape[1]
    packed = jnp.concatenate([w_down, w_out, w_up[:, :width], w_up[:, width:]], axis=0)
    held = lax.all_gather(packed, ("scene", "lat"), axis=0, tiled=False)
    shard = w_out.shape[0]
    parts = [held[:, n * shard : (n + 1) * shard].reshape(width, width) for n in range(2, 5)]
    up = jnp.concatenate(parts[1:], axis=1)
    return parts[0], up, held[:, : 2 * shard].reshape(2 * width, width)


def widen(weight):
    gap = jnp.zeros((weight.shape[0], 2 * LANES - OWN), weight.dtype)
    return jnp.concatenate([weight, gap], axis=1)


def own_lanes(head, axis):
    spot = lax.broadcasted_iota(jnp.int32, (1, LANES) if axis == 1 else (LANES, 1), axis)
    first = (head % 2) * HEAD_DIM
    return (spot >= first) & (spot < first + HEAD_DIM), spot, HEAD_DIM - first


def lane_block(values, head):
    return values[:, (head // 2) * LANES : (head // 2 + 1) * LANES]


def norms_kernel(where, rays, normed_low, centers, factors):
    values = rays[...].astype(F32)
    middle = jnp.mean(values, axis=-1, keepdims=True)
    center = values - middle
    factor = lax.rsqrt(jnp.mean(center * center, axis=-1, keepdims=True) + 1e-05)
    normed_low[...] = (center * factor).astype(BF)
    centers[...] = jnp.broadcast_to(middle, centers.shape)
    factors[...] = jnp.broadcast_to(factor, factors.shape)


def make_norms(where, rays):
    count, width = rays.shape
    block = count // 4
    rows = lambda cols: pl.BlockSpec((block, cols), lambda i, w: (i, 0))
    return pl.pallas_call(
        norms_kernel,
        grid_spec=pltpu.PrefetchScalarGridSpec(
            num_scalar_prefetch=1,
            grid=(4,),
            in_specs=[pl.BlockSpec((block, width), lambda i, w: (i ^ (2 * w[1]), 0))],
            out_specs=[rows(width), rows(LANES), rows(LANES)],
        ),
        out_shape=[shape((count, width)), shape((count, LANES), F32), shape((count, LANES), F32)],
        compiler_params=params(),
        cost_estimate=cost(1),
        name="norms",
    )(where, rays)


def query_kernel(where, rays, centers, factors, weight, rows_in, query, wide):
    @pl.when(pl.program_id(0) == 0)
    def _():
        wide[...] = widen(weight[0])

    copies = rays.shape[1] // LANES
    middle = jnp.concatenate([centers[...]] * copies, axis=1)
    factor = jnp.concatenate([factors[...]] * copies, axis=1)
    normed = (rays[...].astype(F32) - middle) * factor
    low = (normed * rows_in[0:1, :] + rows_in[1:2, :]).astype(BF)
    values = dot(low, wide[...]) * Q_SCALE
    for h in range(OWN_HEADS):
        own, lane, spare = own_lanes(h, 1)
        one = jnp.where(lane == spare, 1.0, 0.0)
        query[h] = jnp.where(own, lane_block(values, h), one).astype(BF)


def make_queries(where, rays, centers, factors, trio, rows_in):
    count, width = rays.shape
    block = count // 4
    whole = lambda a: pl.BlockSpec(a.shape, lambda i, w: (0,) * a.ndim)
    return pl.pallas_call(
        query_kernel,
        grid_spec=pltpu.PrefetchScalarGridSpec(
            num_scalar_prefetch=1,
            grid=(4,),
            in_specs=[
                pl.BlockSpec((block, width), lambda i, w: (i ^ (2 * w[1]), 0)),
                pl.BlockSpec((block, LANES), lambda i, w: (i, 0)),
                pl.BlockSpec((block, LANES), lambda i, w: (i, 0)),
                pl.BlockSpec((1,) + trio.shape[1:], lambda i, w: (0, 0, 0)),
                whole(rows_in),
            ],
            out_specs=pl.BlockSpec((OWN_HEADS, block, LANES), lambda i, w: (0, i, 0)),
            scratch_shapes=[pltpu.VMEM((width, 2 * LANES), BF)],
        ),
        out_shape=shape((OWN_HEADS, count, LANES)),
        compiler_params=params(),
        cost_estimate=cost(2),
        name="queries",
    )(where, rays, centers, factors, trio, rows_in)


def keyset_kernel(count, *refs):
    lats, trio, shut = refs[:count], refs[count], refs[count + 1]
    key, key_t, val, val_t, wide, here = refs[-6:]
    step = pl.program_id(0)

    @pl.when(step == 0)
    def _():
        wide[0] = widen(trio[1])
        wide[1] = widen(trio[2])

    for j, lat in enumerate(lats):

        @pl.when(step == j)
        def _():
            here[...] = lat[...]

    keys = dot(here[...], wide[0])
    vals = dot(here[...], wide[1])
    blocks = lambda v: [v[:, i * LANES : (i + 1) * LANES].T for i in range(2)]
    keys_t, vals_t = blocks(keys), blocks(vals)
    for h in range(OWN_HEADS):
        own, _, _ = own_lanes(h, 1)
        own_line, line, spare = own_lanes(h, 0)
        key[h] = jnp.where(own, lane_block(keys, h), 0.0).astype(BF)
        val[h] = jnp.where(own, lane_block(vals, h), 1.0).astype(BF)
        mask = jnp.where(line == spare, shut[0], 0.0)
        key_t[h] = jnp.where(own_line, keys_t[h // 2], mask).astype(BF)
        val_t[h] = jnp.where(own_line, vals_t[h // 2], 1.0).astype(BF)


def make_keyset(start, lats, trio, shut, held=None):
    count = len(lats)
    rows, width = lats[0].shape
    total = LATS * rows
    tall, long = shape((OWN_HEADS, total, LANES)), shape((OWN_HEADS, LANES, total))
    whole = lambda a: pl.BlockSpec(a.shape, lambda i: (0,) * a.ndim)
    down = pl.BlockSpec((OWN_HEADS, rows, LANES), lambda i: (0, start + i, 0))
    over = pl.BlockSpec((OWN_HEADS, LANES, rows), lambda i: (0, 0, start + i))
    extra = [] if held is None else list(held)
    return pl.pallas_call(
        partial(keyset_kernel, count),
        grid=(count,),
        out_shape=[tall, long, tall, long],
        in_specs=[whole(lat) for lat in lats]
        + [whole(trio), pl.BlockSpec((1, 1, rows), lambda i: (start + i, 0, 0))]
        + [ANY] * len(extra),
        out_specs=[down, over, down, over],
        scratch_shapes=[pltpu.VMEM((2, width, 2 * LANES), BF), pltpu.VMEM((rows, width), BF)],
        input_output_aliases={count + 2 + i: i for i in range(len(extra))},
        compiler_params=params(),
        cost_estimate=cost(5),
        name="keyset",
    )(*lats, trio, shut, *extra)


def attend_kernel(sub, query, key_t, val, *rest):
    context, native, weights, inverse, mixed = rest[-5:]
    head, part = pl.program_id(0), pl.program_id(1)
    rows = query.shape[1]
    own, _, _ = own_lanes(head, 1)
    spot = part * 2 + head // 2

    def score(i):
        return dot(query[0, i * sub : (i + 1) * sub, :], key_t[0])

    scores = score(0)
    for i in range(rows // sub):
        later = score(i + 1) if i + 1 < rows // sub else None
        at = slice(i * sub, (i + 1) * sub)
        low = jnp.exp2(scores - jnp.max(scores, axis=1, keepdims=True)).astype(BF)
        weights[0, at, :] = low
        summed = dot(low, val[0])
        scale = 1.0 / jnp.where(own, pltpu.roll(summed, HEAD_DIM, 1), summed)
        held = jnp.where(head == 1, mixed[spot, at, :], 0.0)
        mixed[spot, at, :] = jnp.where(own, summed * scale, held)
        inverse[0, at, :] = scale
        scores = later

    for p in range(2):

        @pl.when((head == OWN_HEADS - 1) & (part == p))
        def _():
            both = jnp.concatenate([mixed[2 * p], mixed[2 * p + 1]], axis=1).astype(BF)
            native[p * rows : (p + 1) * rows, :] = both
            context[:, p * OWN : (p + 1) * OWN] = both[:, :OWN]


def attend(half_index, query, key_t, val, held=None, after=()):
    _, count, _ = query.shape
    total = key_t.shape[2]
    half = count // 2
    block = half // 2
    sub = block // 3 if block % 48 == 0 else block
    rows = lambda cols: pl.BlockSpec((1, block, cols), lambda h, b: (h, 2 * half_index + b, 0))
    every = lambda rows, cols: pl.BlockSpec((1, rows, cols), lambda h, b: (h, 0, 0))
    extra = ([] if held is None else list(held)) + list(after)
    return pl.pallas_call(
        partial(attend_kernel, sub),
        grid=(OWN_HEADS, 2),
        in_specs=[rows(LANES), every(LANES, total), every(total, LANES)] + [ANY] * len(extra),
        out_specs=[
            pl.BlockSpec((block, 2 * OWN), lambda h, b: (0, 0)),
            pl.BlockSpec((half, 2 * LANES), lambda h, b: (0, 0)),
            rows(total),
            rows(LANES),
        ],
        out_shape=[
            shape((block, 2 * OWN)),
            shape((half, 2 * LANES)),
            shape((OWN_HEADS, count, total)),
            shape((OWN_HEADS, count, LANES), F32),
        ],
        scratch_shapes=[pltpu.VMEM((4, block, LANES), F32)],
        input_output_aliases={} if held is None else {3: 2, 4: 3},
        compiler_params=params(),
        cost_estimate=cost(16),
        name="attend",
    )(query, key_t, val, *extra)


def back_kernel(sub, lat_rows, head, fine, weights, inverse, *refs):
    d_here, d_there, ctx_here, ctx_there, query, key, val_t = refs[:7]
    refs = refs[7:]
    project = not fine or head > 0
    lats, normed_low, earlier, where = refs[:LATS], refs[LATS], refs[5:9], refs[9]
    count = LATS + (0 if not project else 2 if fine else 1)
    out, scratch = refs[-(count + (5 if project else 2)) :][:count], refs[-5 if project else -2 :]
    sums, d_query = scratch[:2]
    grads_out = out[LATS:]
    pair_out = query_out = out[:LATS]
    query_at = 2 * lat_rows
    step = pl.program_id(0)
    rows = weights.shape[1]
    half = 2 * rows
    start = pl.multiple_of((step % 2) * rows, rows)
    loads = []
    if project:
        lat_here, normed_here, sem = scratch[2:]
        for j, lat in enumerate(lats):
            at = pl.ds(j * lat_rows, lat_rows)
            loads.append(pltpu.make_async_copy(lat, lat_here.at[at], sem.at[j]))
        loads.append(pltpu.make_async_copy(normed_low, normed_here, sem.at[LATS]))

    @pl.when(step == 0)
    def _():
        for load in loads:
            load.start()

    own, lane, spare = own_lanes(head, 1)
    far = step >= 2
    upstream = jnp.where(far, d_there[...], d_here[...]).astype(F32)
    ctx = jnp.where(far, ctx_there[...], ctx_here[...]).astype(F32)
    scale = inverse[0]
    delta = jnp.sum(jnp.where(own, upstream * ctx, 0.0), axis=1, keepdims=True) * scale
    high = delta.astype(BF).astype(F32)
    rest = jnp.where(lane == spare + 1, high - delta, 0.0)
    rest = jnp.where(lane == spare, -high, rest)
    grad = jnp.where(own, upstream * scale, rest).astype(BF)
    val_part = dot_lt(grad, weights[0])
    found = []
    for i in range(rows // sub):
        at = slice(i * sub, (i + 1) * sub)
        d_weights = dot(grad[at], val_t[0])
        d_scores = (weights[0, at, :].astype(F32) * d_weights).astype(BF)
        d_query[pl.ds(start + i * sub, sub), :] = dot(d_scores, key[0]) * 0.125
        found.append(d_scores)
    d_scores = jnp.concatenate(found, axis=0) if len(found) > 1 else found[0]
    key_part = dot_lt(query[0], d_scores) * (1.0 / LOG2E)

    @pl.when(step == 0)
    def _():
        sums[0] = key_part
        sums[1] = val_part

    @pl.when(step > 0)
    def _():
        sums[0] += key_part
        sums[1] += val_part

    first = (head % 2) * HEAD_DIM

    @pl.when(step == 3)
    def _():
        for i in range(2):
            total = sums[i, first : first + HEAD_DIM].astype(BF)
            for j in range(LATS):
                pair_out[j][:, i * lat_rows : (i + 1) * lat_rows] = total[
                    :, j * lat_rows : (j + 1) * lat_rows
                ]

    for last in (1, 3):

        @pl.when(step == last)
        def _():
            turned = d_query[...].T[first : first + HEAD_DIM].astype(BF)
            for j in (last // 2, last // 2 + 2):
                query_out[j][:, query_at : query_at + half] = turned

    if not project:
        return

    @pl.when(step == 3)
    def _():
        for load in loads:
            load.wait()
        groups = [list(earlier), list(out[:LATS])] if head == 1 and fine else [list(out[:LATS])]
        at = slice(2 * lat_rows, 2 * lat_rows + half)
        turned = [jnp.concatenate([g[b][:, at] for g in groups], axis=0) for b in range(2)]
        part = dot(turned[0], normed_here[:half]) + dot(turned[1], normed_here[half:])
        both = []
        for i in range(2):
            at = slice(i * lat_rows, (i + 1) * lat_rows)
            for g in groups:
                both.append(jnp.concatenate([g[j][:, at] for j in range(LATS)], axis=1))
        both = dot(jnp.concatenate(both, axis=0), lat_here[...])
        rows = both.shape[0] // 2
        col = sum(jnp.sum(t.astype(F32), axis=1, keepdims=True) for t in turned)
        high = col.astype(BF).astype(F32)
        col = jnp.where(lane == 0, high, jnp.where(lane == 1, col - high, 0.0)).T[:16]
        parts = [p.T for p in (part, both[:rows], both[rows:])] + [col]
        if not fine:
            grads_out[0][...] = jnp.concatenate(parts, axis=0)
            return
        send, keep = grads_out
        scenes = 2 * send.shape[0]
        width = normed_here.shape[1]
        block = width // scenes
        for s in range(scenes):
            mine = [p[s * block : (s + 1) * block] for p in parts[:3]] + parts[3:]
            if head == 2:
                mine = fold(jnp.concatenate(mine + [jnp.zeros((16, HEAD_DIM), F32)], axis=0))
            else:
                mine = jnp.concatenate(mine, axis=0)
            mine = mine.astype(BF)
            kept = where[4] == s % 2

            @pl.when(kept)
            def _():
                keep[s // 2] = mine

            @pl.when(jnp.logical_not(kept))
            def _():
                send[s // 2] = mine


def attend_back(head, fine, weights, inverse, d_ctxs, ctxs, query, key, val_t, lats, normed_low, earlier, where, after):
    _, count, total = weights.shape
    rows = count // 4
    sub = rows // 2 if rows % 32 == 0 else rows
    lat_rows = total // LATS
    width = normed_low.shape[1]
    pad = lambda n: -(-n // LANES) * LANES
    outs = [shape((HEAD_DIM, pad(2 * lat_rows + 2 * rows)))] * LATS
    project = not fine or head > 0
    if not fine:
        outs.append(shape((3 * width + 16, HEAD_DIM), F32))
    elif project:
        block = 3 * (width // 8)
        dims = (4, block + 16, LANES) if head == 1 else (4, block // 2 + 16, LANES)
        outs += [shape(dims)] * 2
    of_head = lambda cols: pl.BlockSpec((1, rows, cols), lambda b: (head, b, 0))
    here = pl.BlockSpec((rows, LANES), lambda b: (jnp.minimum(b, 1), head // 2))
    there = pl.BlockSpec((rows, LANES), lambda b: (jnp.maximum(b, 2) - 2, head // 2))
    whole = lambda a: pl.BlockSpec(a.shape, lambda b: (0,) * len(a.shape))
    earlier = list(earlier) if head == 1 and fine else [where] * LATS
    early = [whole(a) for a in earlier] if head == 1 and fine else [ANY] * LATS
    return pl.pallas_call(
        partial(back_kernel, sub, lat_rows, head, fine),
        grid=(4,),
        in_specs=[
            of_head(total),
            of_head(LANES),
            here,
            there,
            here,
            there,
            of_head(LANES),
            pl.BlockSpec((1, total, LANES), lambda b: (head, 0, 0)),
            pl.BlockSpec((1, LANES, total), lambda b: (head, 0, 0)),
        ]
        + [ANY] * (LATS + 1)
        + early
        + [SMEM]
        + [ANY] * len(after),
        out_specs=[whole(o) for o in outs],
        out_shape=outs,
        scratch_shapes=[
            pltpu.VMEM((2, LANES, total), F32),
            pltpu.VMEM((2 * rows, LANES), F32),
        ]
        + [
            pltpu.VMEM((total, width), BF),
            pltpu.VMEM((count, width), BF),
            pltpu.SemaphoreType.DMA((LATS + 1,)),
        ]
        * project,
        compiler_params=params(),
        cost_estimate=cost(14),
        name=f"attend_back_{head}",
    )(weights, inverse, *d_ctxs, *ctxs, query, key, val_t, *lats, normed_low, *earlier, where, *after)


def quarter_halves(values, core):
    mid = values.shape[1] // 2
    low, high = values[:, :mid], values[:, mid:]
    return jnp.where(core == 0, low, high), jnp.where(core == 0, high, low)


def feed_kernel(fine, where, *refs):
    ins, rows_in, up_shift = refs[:9], refs[9], refs[10]
    layer_out, layer_half, d_middle, d_own, d_sibling = refs[11:16]
    grads_out = refs[16:-15]
    rays, ctxs, upstream, w_out, w_up, w_down, low_out, low_mid, own, sibling = refs[-15:-5]
    halves, active, lifted, sem_in, sem_out = refs[-5:]
    lat, core, side = where[0], where[1], where[2]
    half, width = rays.shape
    hidden = w_up.shape[1]
    block = half // 4
    mine = pl.ds(pl.multiple_of(core * half, half), half)
    sources = [ins[0].at[mine]] + list(ins[1:5]) + [ins[6], ins[7], ins[5].at[mine], ins[8]]
    targets = [rays] + [ctxs.at[j] for j in range(LATS)] + [w_out, w_up, upstream, w_down]
    loads = [
        pltpu.make_async_copy(a, b, sem_in.at[n]) for n, (a, b) in enumerate(zip(sources, targets))
    ]
    stores = []

    def store(source, target):
        stores.append(pltpu.make_async_copy(source, target, sem_out.at[len(stores)]))
        stores[-1].start()

    for load in loads:
        load.start()
    for load in loads[:6]:
        load.wait()
    gain, bias = rows_in[2:3, :], rows_in[3:4, :]
    spots = [pl.ds(pl.multiple_of((lat ^ j) * OWN, OWN), OWN) for j in range(LATS)]

    def ctx_rows(j, i):
        at = slice((i % 2) * block, (i % 2 + 1) * block)
        return ctxs[j, at, (i // 2) * OWN : (i // 2 + 1) * OWN]

    begun = []
    for i in range(4):
        at = slice(i * block, (i + 1) * block)
        middle = rays[at, :].astype(F32) + rows_in[4:5, :]
        for j in range(LATS):
            middle = middle + dot(ctx_rows(j, i), w_out[spots[j], :])
        normed, factor = norm_parts(middle)
        lifted[at, :] = (normed * gain + bias).astype(BF)
        begun.append((middle, normed, factor))
    for load in loads[6:]:
        load.wait()
    column = lambda v: jnp.sum(v, axis=0, keepdims=True)
    sums, up_sums = [0.0] * 4, 0.0
    for i in range(4):
        at = slice(i * block, (i + 1) * block)
        middle, normed, factor = begun[i]
        before = dot(lifted[at, :], w_up[...]) + up_shift[...]
        squared = before * before
        bent = jnp.tanh(before * (ROOT + (ROOT * 0.044715) * squared))
        scaled = 0.5 * before
        act = (scaled + scaled * bent).astype(BF)
        active[at, :] = act
        slope = 0.5 + 0.5 * bent + scaled * (1.0 - bent * bent) * (
            ROOT + (3 * 0.044715 * ROOT) * squared
        )
        d_pre = (dot_rt(upstream[at, :], w_down[...]) * slope).astype(BF)
        halves[at, :hidden] = d_pre
        low_out[at, :] = (middle + dot(act, w_down[...]) + rows_in[5:6, :]).astype(BF)
        d_lifted = dot_rt(d_pre, w_up[...])
        up_wide = upstream[at, :].astype(F32)
        d_mid = up_wide + norm_back(d_lifted, normed, factor, gain)
        branch = d_mid.astype(BF)
        low_mid[at, :] = branch
        halves[at, hidden:] = branch
        gap = jnp.zeros((block, 2 * LANES - OWN), F32)
        for target, spot in zip((own, sibling), spots):
            part = dot_rt(branch, w_out[spot, :])
            target[at, :] = jnp.concatenate([part, gap], axis=1).astype(BF)
        pieces = (d_lifted * normed, d_lifted, branch.astype(F32), up_wide)
        sums = [total + column(piece) for total, piece in zip(sums, pieces)]
        up_sums = up_sums + column(d_pre.astype(F32))
    store(sibling, d_sibling)
    store(own, d_own)
    store(low_out, layer_half)
    store(low_out, layer_out.at[mine])
    store(low_mid, d_middle)

    wide, narrow = hidden // 2, width // 2
    pre_half = halves[:, pl.ds(pl.multiple_of(side * wide, LANES), wide)]
    branch_half = halves[:, pl.ds(pl.multiple_of(hidden + side * narrow, LANES), narrow)]
    up_half = upstream[:, pl.ds(pl.multiple_of(side * narrow, LANES), narrow)]
    up_grad = dot_lt(lifted[...], pre_half)
    down_grad = dot_lt(active[...], up_half)
    if fine:
        messages = grads_out[2:]
        scenes = messages[0].shape[0]
        shard = width // (scenes * LATS)

        def parities(values, rows):
            parts = [values[n * rows : (n + 1) * rows] for n in range(LATS)]
            even = jnp.concatenate([parts[0], parts[2]], axis=0)
            odd = jnp.concatenate([parts[1], parts[3]], axis=0)
            first, second = jnp.where(core == 0, even, odd), jnp.where(core == 0, odd, even)
            return zip(messages, (first.astype(BF), second.astype(BF)))

        for s in range(scenes):
            rows = LATS * shard
            for message, part in parities(up_grad[s * rows : (s + 1) * rows], shard):
                message[s, 2 * shard : 4 * shard, :] = part[:, :narrow]
                message[s, 4 * shard : 6 * shard, :] = part[:, narrow:]
            rows = 2 * LATS * shard
            for message, part in parities(down_grad[s * rows : (s + 1) * rows], 2 * shard):
                message[s, 6 * shard : 10 * shard, :] = part
        for j in range(LATS):
            ctx = jnp.concatenate([ctxs[j, :, :OWN], ctxs[j, :, OWN:]], axis=0)
            values = dot_lt(ctx, branch_half)
            rows = LATS * shard
            for q in range(OWN // rows):
                place = (lat ^ j) * (OWN // rows) + q
                for message, part in parities(values[q * rows : (q + 1) * rows], shard):
                    message[place, : 2 * shard, :] = part
        lines = line_up(sums, up_sums, scenes * LATS)
        for s in range(scenes):
            line = lines[s * LATS : (s + 1) * LATS]
            even = jnp.concatenate([line[0:1], line[2:3]], axis=0)
            odd = jnp.concatenate([line[1:2], line[3:4]], axis=0)
            for n, message in enumerate(messages):
                rows = jnp.where(core == n, even, odd)
                rows = jnp.concatenate([rows, jnp.zeros((14, OWN), F32)], axis=0)
                rows = jnp.concatenate([rows, jnp.zeros_like(rows)], axis=1)
                message[s, 10 * shard :, :] = rows.astype(BF)
        for message, target in zip(messages, grads_out):
            store(message, target)
    else:
        for i, part in ((1, up_grad), (2, down_grad)):
            first, second = quarter_halves(part, core)
            grads_out[2 * i][...] = first.astype(BF)
            grads_out[2 * i + 1][...] = second.astype(BF)
        for j in range(LATS):
            ctx = jnp.concatenate([ctxs[j, :, :OWN], ctxs[j, :, OWN:]], axis=0)
            first, second = quarter_halves(dot_lt(ctx, branch_half), core)
            grads_out[0][spots[j], :] = first.astype(BF)
            grads_out[1][spots[j], :] = second.astype(BF)
        grads_out[6][...] = jnp.concatenate(sums + [jnp.zeros((4, width), F32)], axis=0)
        grads_out[7][...] = jnp.broadcast_to(up_sums, (8, hidden))
    for copy in stores:
        copy.wait()


def line_up(sums, up_sums, sources):
    total = None
    shard = sums[0].shape[1] // sources
    for rows, size, first in ((sums, shard, 2), ([up_sums], 2 * shard, 6)):
        wide = rows[0].shape[1]
        col = lax.broadcasted_iota(jnp.int32, (1, wide), 1).astype(F32)
        owner = jnp.floor((col + 0.5) * (1.0 / size))
        spot = (col - owner * size)
        row = lax.broadcasted_iota(jnp.int32, (OWN, 1), 0).astype(F32)
        line = lax.broadcasted_iota(jnp.int32, (sources, 1), 0).astype(F32)
        for v, values in enumerate(rows):
            hot = jnp.where(row == spot + (first + v) * shard, 1.0, 0.0).astype(BF)
            mine = jnp.where(line == owner, values, 0.0).astype(BF)
            part = dot_rt(mine, hot)
            total = part if total is None else total + part
    return total


def feed(where, rays, ctxs, upstream, weights, rows_in, up_shift, scenes, fine):
    count, width = rays.shape
    hidden = up_shift.shape[1]
    half = count // 2
    mats = [(width, width // 4), (width, hidden // 4), (hidden, width // 4)]
    if fine:
        message = (scenes, 10 * (width // (scenes * LATS)) + 16, width // 2)
        grads = [shape(message)] * 2
        spec, held = ANY, [pltpu.VMEM(message, BF)] * 2
    else:
        grads = [shape(d) for d in mats for _ in range(2)]
        grads += [shape((8, width), F32), shape((8, hidden), F32)]
        spec, held = pl.BlockSpec(memory_space=pltpu.VMEM), []
    return pl.pallas_call(
        partial(feed_kernel, fine),
        out_shape=[
            shape((count, width)),
            shape((half, width)),
            shape((half, width)),
            shape((half, 2 * LANES)),
            shape((half, 2 * LANES)),
        ]
        + grads,
        in_specs=[SMEM] + [ANY] * 9 + vmem(2),
        out_specs=[ANY] * 5 + [spec] * len(grads),
        scratch_shapes=held
        + [
            pltpu.VMEM((half, width), BF),
            pltpu.VMEM((LATS, half // 2, 2 * OWN), BF),
            pltpu.VMEM((half, width), BF),
            pltpu.VMEM((width, width), BF),
            pltpu.VMEM((width, hidden), BF),
            pltpu.VMEM((hidden, width), BF),
            pltpu.VMEM((half, width), BF),
            pltpu.VMEM((half, width), BF),
            pltpu.VMEM((half, 2 * LANES), BF),
            pltpu.VMEM((half, 2 * LANES), BF),
            pltpu.VMEM((half, hidden + width), BF),
            pltpu.VMEM((half, hidden), BF),
            pltpu.VMEM((half, width), BF),
            pltpu.SemaphoreType.DMA((9,)),
            pltpu.SemaphoreType.DMA((8,)),
        ],
        compiler_params=params(),
        cost_estimate=cost(26),
        name="feed",
    )(where, rays, *ctxs, upstream, *weights, rows_in, up_shift)


def halve_kernel(bit, where, own, got, send, keep):
    count = send.shape[0]
    mine = where[4] if count == 4 else where[6]
    low = (1 << bit) - 1
    for n in range(count):
        first = ((n & ~low) << 1) | (n & low)
        for target, side in ((send, 1 - mine), (keep, mine)):
            at = first + (side << bit)
            target[n] = (own[at].astype(F32) + got[at].astype(F32)).astype(BF)


def halve(where, bit, own, got):
    count, rows, cols = own.shape
    half = shape((count // 2, rows, cols))
    return pl.pallas_call(
        partial(halve_kernel, bit),
        out_shape=[half, half],
        in_specs=[SMEM] + vmem(2),
        out_specs=vmem(2),
        compiler_params=params(),
        cost_estimate=cost(3),
        name="halve",
    )(where, own, got)


def spread_kernel(count, where, *refs):
    pairs, (feed_keep, feed_got), out = refs[: 2 * count], refs[2 * count : 2 * count + 2], refs[-6:]
    for k in range(4):
        at = where[5] ^ k
        parts = [
            pairs[2 * n][at].astype(F32) + pairs[2 * n + 1][at].astype(F32) for n in range(count)
        ]
        out[k][...] = jnp.concatenate(parts, axis=0).astype(BF)
    mine = where[5] % 2
    for target, at in ((out[4], 1 - mine), (out[5], mine)):
        target[...] = (feed_keep[at].astype(F32) + feed_got[at].astype(F32)).astype(BF)


def add_spread(where, pairs, feed_keep, feed_got, after):
    rows = sum(keep.shape[1] for keep, _ in pairs)
    last = shape(feed_keep.shape[1:])
    return pl.pallas_call(
        partial(spread_kernel, len(pairs)),
        out_shape=[shape((rows, pairs[0][0].shape[2]))] * 4 + [last] * 2,
        in_specs=[SMEM] + vmem(2 * len(pairs) + 2) + [ANY] * len(after),
        out_specs=vmem(6),
        compiler_params=params(),
        cost_estimate=cost(2),
        name="add_spread",
    )(where, *[a for pair in pairs for a in pair], feed_keep, feed_got, *after)


def regroup_kernel(shard, where, *refs):
    trio, out, held = refs[:4], refs[6:10], refs[10]
    side = where[2]
    block = LATS * shard
    total = sum(r[...].astype(F32) for r in trio)
    pair, third = total[: 3 * block + 16], unfold(total[3 * block + 16 :])
    held[...] = jnp.concatenate([pair, third[: 3 * block + 16]], axis=1)
    feed_sum = refs[4][...].astype(F32) + refs[5][...].astype(F32)
    places = [[], []]
    for q in range(2):
        for first, rows in ((0, shard), (2 * shard, shard), (4 * shard, shard), (6 * shard, 2 * shard)):
            places[q].append(feed_sum[first + q * rows : first + (q + 1) * rows])
        line = feed_sum[10 * shard + q : 10 * shard + q + 1]
        places[q].append(jnp.broadcast_to(line, (8, line.shape[1])))
    places = [jnp.concatenate(p, axis=0) for p in places]
    for k in range(LATS):
        rows = []
        for n in range(3):
            at = n * block + (where[0] ^ k) * shard
            rows.append(held[pl.ds(pl.multiple_of(at, 8), shard), :])
        rows.append(held[3 * block : 3 * block + 8, :])
        rows.append(jnp.zeros((16, OWN), F32))
        value = fold(jnp.concatenate(rows, axis=0))
        if k % 2 == 0:
            mine = jnp.where(side == (k // 2), places[0], places[1])
            value = jnp.concatenate([value, mine], axis=0)
        out[k][...] = value.astype(BF)


def regroup(where, trio, feed_keep, feed_got, shard):
    small = (3 * shard + 24) // 2
    large = small + 5 * shard + 8
    return pl.pallas_call(
        partial(regroup_kernel, shard),
        out_shape=[shape((rows, 2 * OWN)) for rows in (large, small, large, small)],
        in_specs=[SMEM] + vmem(6),
        out_specs=vmem(LATS),
        scratch_shapes=[pltpu.VMEM((3 * LATS * shard + 16, OWN), F32)],
        compiler_params=params(),
        cost_estimate=cost(2),
        name="regroup",
    )(where, *trio, feed_keep, feed_got)


def settle_kernel(shard, where, got0, got1, got2, got3, w_query, gain, bias, *out):
    lat, side = where[0], where[2]
    mats, firsts, rest = out[-13:-7], out[-7:-5], out[-5:]
    got = [g[...].astype(F32) for g in (got0, got1, got2, got3)]
    small = got[1].shape[0]
    here, there = got[0][small:], got[2][small:]
    left, right = jnp.where(side == 0, here, there), jnp.where(side == 0, there, here)
    both = lambda a, b: jnp.concatenate([left[a:b], right[a:b]], axis=1)
    got = [unfold(g[:small]) for g in got]
    whole = jnp.concatenate([choose(lat ^ p, got) for p in range(LATS)], axis=1)
    part = lambda n: whole[n * shard : (n + 1) * shard]
    sums = whole[3 * shard : 3 * shard + 1] + whole[3 * shard + 1 : 3 * shard + 2]
    weight = w_query[...].astype(F32)
    lane = lax.broadcasted_iota(jnp.int32, (shard, shard), 1)
    line = lax.broadcasted_iota(jnp.int32, (shard, shard), 0)

    def column(ref):
        row = ref[...].astype(F32).reshape(1, shard)
        return jnp.sum(jnp.where(lane == line, row, 0.0), axis=1, keepdims=True)

    mats[0][...] = part(0) * column(gain) + column(bias) * sums
    mats[1][...] = part(1)
    mats[2][...] = part(2)
    mats[3][...] = both(0, shard)
    cols = [half[n * shard : (n + 1) * shard] for half in (left, right) for n in (1, 2)]
    mats[4][...] = jnp.concatenate(cols, axis=1)
    mats[5][...] = both(3 * shard, 5 * shard)
    firsts[0][...] = jnp.sum((part(0) * weight).T, axis=0)
    firsts[1][...] = jnp.sum((weight * sums).T, axis=0)
    line = here[5 * shard : 5 * shard + 1]
    for target, (first, count) in zip(rest, ((2, 1), (3, 1), (4, 1), (6, 2), (5, 1))):
        target[...] = line[:, first * shard : (first + count) * shard].reshape(count * shard)


def settle(where, got, w_query, gain, bias, after):
    shard, width = w_query.shape
    flat = shape((shard, width), F32)
    tall = shape((2 * shard, width), F32)
    wide = shape((shard, 2 * width), F32)
    return pl.pallas_call(
        partial(settle_kernel, shard),
        out_shape=[flat] * 4
        + [wide, tall]
        + [shape((n * shard,), F32) for n in (1, 1, 1, 1, 1, 2, 1)],
        in_specs=[SMEM] + vmem(7) + [ANY] * len(after),
        out_specs=vmem(13),
        compiler_params=params(),
        cost_estimate=cost(2),
        name="settle",
    )(where, *got, w_query, gain, bias, *after)


def place_rows(where, h, j):
    first = (where[0] ^ j) * OWN + h * HEAD_DIM
    return pl.ds(pl.multiple_of(first, HEAD_DIM), HEAD_DIM)


def first_grads_kernel(parts, where, rows_in, rays_in, middle_in, turned, *refs):
    msgs, (ray_grad, ray_half) = refs[:12], refs[-9:-7]
    rays, middle, weight, d_query, low, sem_in, sem_out = refs[-7:]
    half, width = rays.shape
    tail = d_query.shape[1]
    first_row = pl.multiple_of(where[1] * half, half)
    loads = []

    def load(source, target):
        loads.append(pltpu.make_async_copy(source, target, sem_in.at[len(loads)]))
        loads[-1].start()

    load(turned.at[:, 0], weight)
    for h in range(OWN_HEADS):
        for j in range(LATS):
            source = msgs[h * LATS + j]
            load(source.at[:, source.shape[1] - tail :], d_query.at[place_rows(where, h, j)])
    for first, last in parts:
        at = pl.ds(first, last - first)
        load(rays_in.at[pl.ds(first_row + first, last - first)], rays.at[at])
        load(middle_in.at[at], middle.at[at])
    for copy in loads[:13]:
        copy.wait()
    matrix = weight[...].reshape(width, width)
    stores = []
    for n, (first, last) in enumerate(parts):
        for copy in loads[13 + 2 * n : 15 + 2 * n]:
            copy.wait()
        at = slice(first, last)
        d_lifted = dot_lt(d_query[:, at], matrix)
        normed, factor = norm_parts(rays[at, :].astype(F32))
        back = norm_back(d_lifted, normed, factor, rows_in[0:1, :])
        low[at, :] = (middle[at, :].astype(F32) + back).astype(BF)
        source = low.at[pl.ds(first, last - first)]
        for target in (
            ray_half.at[pl.ds(first, last - first)],
            ray_grad.at[pl.ds(first_row + first, last - first)],
        ):
            stores.append(pltpu.make_async_copy(source, target, sem_out.at[len(stores)]))
            stores[-1].start()
    for copy in stores:
        copy.wait()


def first_grads(where, rays, turned, rows_in, d_middle, msgs, lat_rows, after):
    count, width = rays.shape
    half = count // 2
    parts = [(a, min(a + 256, half)) for a in range(0, half, 256)]
    tail = msgs[0][0].shape[1] - 2 * lat_rows
    return pl.pallas_call(
        partial(first_grads_kernel, parts),
        in_specs=[SMEM] + vmem(1) + [ANY] * (15 + len(after)),
        out_specs=[ANY] * 2,
        out_shape=[shape((count, width)), shape((half, width))],
        scratch_shapes=[
            pltpu.VMEM((half, width), BF),
            pltpu.VMEM((half, width), BF),
            pltpu.VMEM((LATS, OWN, width), BF),
            pltpu.VMEM((width, tail), BF),
            pltpu.VMEM((half, width), BF),
            pltpu.SemaphoreType.DMA((13 + 2 * len(parts),)),
            pltpu.SemaphoreType.DMA((2 * len(parts),)),
        ],
        compiler_params=params(),
        cost_estimate=cost(6),
        name="first_grads",
    )(where, rows_in, rays, d_middle, turned, *[m for group in msgs for m in group], *after)


def latent_kernel(where, turned, *refs):
    msgs, (out, weight, held, sem) = refs[:12], refs[-4:]
    _, width, lat_rows = held.shape
    loads = [[], []]
    for i in range(2):
        copies = [(turned.at[:, 1 + i], weight.at[i])]
        for h in range(OWN_HEADS):
            for j in range(LATS):
                source = msgs[h * LATS + j].at[:, i * lat_rows : (i + 1) * lat_rows]
                copies.append((source, held.at[i, place_rows(where, h, j)]))
        for source, target in copies:
            at = sem.at[i, len(loads[i])]
            loads[i].append(pltpu.make_async_copy(source, target, at))
            loads[i][-1].start()
    for copy in loads[0]:
        copy.wait()
    total = dot_lt(held[0], weight[0].reshape(width, width))
    for copy in loads[1]:
        copy.wait()
    total = total + dot_lt(held[1], weight[1].reshape(width, width))
    out[...] = total[: out.shape[0]].astype(BF)


def latent_grads(where, turned, msgs, rows, lat_rows, after):
    width = turned.shape[3]
    return pl.pallas_call(
        latent_kernel,
        in_specs=[SMEM] + [ANY] * (13 + len(after)),
        out_specs=pl.BlockSpec(memory_space=pltpu.VMEM),
        out_shape=shape((rows, width)),
        scratch_shapes=[
            pltpu.VMEM((2, LATS, OWN, width), BF),
            pltpu.VMEM((2, width, lat_rows), BF),
            pltpu.SemaphoreType.DMA((2, 13)),
        ],
        compiler_params=params(),
        cost_estimate=cost(6),
        name="latent_grads",
    )(where, turned, *msgs, *after)


def join(where, full, there):
    first = (1 - where[1]) * there.shape[0]
    return lax.dynamic_update_slice(full, there, (first, jnp.int32(0)))


def body(
    rays,
    latents,
    view_count,
    view_mask,
    cotangent,
    w_query,
    w_key,
    w_value,
    w_out,
    w_up,
    w_down,
    first_gain,
    first_bias,
    second_gain,
    second_bias,
    out_bias,
    up_bias,
    down_bias,
):
    scenes = lax.axis_size("scene")
    lat, scene = lax.axis_index("lat"), lax.axis_index("scene")
    core, side = lat % 2, lat // 2
    where = jnp.stack([lat, core, side, scene, scene % 2, scene // 2, scene // 4])
    where = where.astype(jnp.int32)
    count, width = rays.shape
    hidden = w_up.shape[1]
    lat_rows = latents.shape[0]
    lat_pad = -(-lat_rows // LANES) * LANES
    shard = w_query.shape[0]
    fine = shard % 8 == 0 and scenes == 8

    normed_low, *stats = make_norms(where, rays)
    vectors = [first_gain, first_bias, second_gain, second_bias, out_bias, down_bias, up_bias]
    (trio, turned, rows_in, up_shift), own_lat, passed = attention_weights(
        where, w_query, w_key, w_value, vectors, latents, lat_pad, [normed_low]
    )

    near_lat, far_lat = swap(own_lat, "lat", 1), swap(own_lat, "lat", 2)

    weights_in = feed_weights(w_out, w_up, w_down, passed)

    spot = jnp.arange(lat_pad, dtype=jnp.int32)
    block_of = lat ^ jnp.arange(LATS, dtype=jnp.int32)
    view_of = (block_of[:, None] * lat_rows + spot[None, :]) // VIEW_TOK
    matches = view_of[..., None] == jnp.arange(VIEWS, dtype=jnp.int32)
    listed = jnp.sum(jnp.where(matches, view_mask[0], 0), axis=-1) > 0
    live = listed & (view_of < view_count[0]) & (spot < lat_rows)[None, :]
    shut = jnp.where(live, 0.0, DEAD).astype(F32).reshape(LATS, 1, lat_pad)


    keyset = make_keyset(0, [own_lat, near_lat], trio, shut)
    query = make_queries(where, rays, *stats, trio, rows_in)
    far_lat = gate(far_lat, [query, keyset[0]])
    last_lat = swap(far_lat, "lat", 1)
    lats = [own_lat, near_lat, far_lat, last_lat]
    keyset = make_keyset(2, [far_lat], trio, shut, keyset)
    key, key_t, val, val_t = make_keyset(3, [last_lat], trio, shut, keyset)
    there_ctx, there_wide, weights, inverse = attend(1, query, key_t, val)
    near, far = swap(there_ctx, "lat", 1), swap(there_ctx, "lat", 3)
    here_ctx, here_wide, weights, inverse = attend(0, query, key_t, val, (weights, inverse))
    here_ctx = gate(here_ctx, [near, far])
    beside = swap(here_ctx, "lat", 2)
    if shard % 8 == 0:
        weights_in = assemble(weights_in, [here_ctx])
        beside = gate(beside, [weights_in[2]])
    ctxs = [here_ctx, near, beside, far]

    turned = lax.all_gather(gate(turned, ctxs[2:]), "lat", axis=0, tiled=False)
    layer_out, out_half, d_middle, d_own, d_sibling, *feed_out = feed(
        where, rays, ctxs, cotangent, weights_in, rows_in, up_shift, scenes, fine
    )
    d_there = swap(d_sibling, "lat", 1)
    out_there = swap(out_half, "lat", 1)
    layer_out = join(where, layer_out, out_there)
    if fine:
        own_msg, sib_msg = feed_out
        feed_send, feed_keep = halve(where, 0, own_msg, swap(sib_msg, "lat", 1))
        feed_got = swap(feed_send, "scene", 1)

    got, grads, after, got_own = [], [], [], ()
    for h in range(OWN_HEADS):
        if h == 1:
            after = after + [out_there] + ([feed_send] if fine else [])
        elif h == 2:
            after = after + got[0][1:]
            if fine:
                feed_keep = gate(feed_keep, after)
                feed_send, feed_keep = halve(where, 1, feed_keep, feed_got)
                feed_got = swap(feed_send, "scene", 4)
                after = after + [feed_send]
        out = attend_back(
            h,
            fine,
            weights,
            inverse,
            (d_own, d_there),
            (here_wide, there_wide),
            query,
            key,
            val_t,
            lats,
            normed_low,
            got_own,
            where,
            after,
        )
        if h == 2:
            out = gate(list(out), got[1][1:] + ([pair_got, feed_got] if fine else []))
        after = [out[0]]
        got_own = out[:LATS]
        grads += out[LATS:]
        if h == 1 and fine:
            pair_got = swap(grads[0], "scene", 1)
        got.append([out[0]] + [swap(out[k], "lat", k) for k in range(1, LATS)])
    after = []
    if fine:
        pairs = [(grads[1], pair_got), (grads[3], swap(grads[2], "scene", 1))]
        *late, feed_send, feed_keep = add_spread(where, pairs, feed_keep, feed_got, [layer_out])
        after = [late[0]]
        feed_got = swap(feed_send, "scene", 2)
        late = [late[0]] + [swap(late[k], "scene", 2 * k) for k in range(1, 4)]
    ray_grad, ray_half = first_grads(where, rays, turned, rows_in, d_middle, got, lat_pad, after)
    if fine:
        ray_half = gate(ray_half, late[1:] + [feed_got])
    ray_grad = join(where, ray_grad, swap(ray_half, "lat", 1))
    if fine:
        final = regroup(where, late, feed_keep, feed_got, shard)
        after = [final[0]]
    latent_grad = latent_grads(
        where, turned, [m for g in got for m in g], lat_rows, lat_pad, after
    )
    first = [first_gain, first_bias]
    if fine:
        final = [final[0]] + [swap(final[k], "lat", k) for k in range(1, LATS)]
        small = settle(where, final, w_query, *first, [latent_grad])
    else:
        joined = jnp.concatenate(grads, axis=1)
        grads = joined[: 3 * width].reshape(3, width, OWN), joined[3 * width :]
        first = [v.reshape(shard, 1).astype(F32) for v in first]
        small = plain_final(feed_out, grads, scenes, shard, w_query, *first)
    return (layer_out, ray_grad, latent_grad, *small)


def plain_final(feed_out, grads, scenes, shard, w_query, gain, bias):
    lat = lax.axis_index("lat")
    out_own, out_sib, up_own, up_sib, down_own, down_sib, sums, up_sums = feed_out
    trio, query_sums = grads

    def by_scene(out_part, up_part, down_part):
        parts = [
            out_part.reshape(scenes, -1, OWN),
            up_part.reshape(scenes, -1, 2, OWN).swapaxes(1, 2).reshape(scenes, -1, OWN),
            down_part.reshape(scenes, -1, OWN),
        ]
        return jnp.concatenate(parts, axis=1).astype(F32)

    feed_part = by_scene(out_own, up_own, down_own)
    feed_part = feed_part + swap(by_scene(out_sib, up_sib, down_sib), "lat", 1)
    feed_part = scatter_scene(feed_part)
    block = LATS * shard
    trio = trio.reshape(3, scenes, block, OWN).swapaxes(0, 1).reshape(scenes, 3 * block, OWN)
    lines = [v.reshape(scenes, LATS, shard) for v in sums[:4]]
    lines = [jnp.zeros_like(lines[0])] * 2 + lines + [up_sums[0].reshape(scenes, LATS, 2 * shard)]
    lines = jnp.concatenate(lines, axis=2)
    lines = jnp.pad(lines, ((0, 0), (0, 0), (0, OWN - 8 * shard)))
    cols = jnp.broadcast_to(query_sums[:2], (scenes, 2, OWN))
    late = scatter_scene(jnp.concatenate([trio.astype(F32), cols, lines], axis=1))
    mats = [late[i * block : (i + 1) * block].reshape(LATS, shard, OWN) for i in range(3)]
    mats += [feed_part[i * block : (i + 1) * block].reshape(LATS, shard, OWN) for i in range(3)]
    mats.append(feed_part[3 * block :].reshape(LATS, 2 * shard, OWN))
    mats.append(jnp.broadcast_to(late[3 * block : 3 * block + 2], (LATS, 2, OWN)))
    mats.append(late[3 * block + 2 :].reshape(LATS, 1, OWN))
    final = jnp.concatenate(mats, axis=1).astype(BF)
    sent = [lax.dynamic_index_in_dim(final, lat ^ k, 0, keepdims=False) for k in range(LATS)]
    got = [sent[0]] + [swap(sent[k], "lat", k) for k in range(1, LATS)]
    got = [g.astype(F32) for g in got]
    line = got[0][-1] + got[1][-1]
    cols = in_order(jnp.stack(got), list(range(LATS)), lat)
    joined = jnp.transpose(cols, (1, 0, 2)).reshape(cols.shape[1], -1)
    part = lambda n, count=1: joined[n * shard : (n + count) * shard]
    up = cols[:, 4 * shard : 6 * shard].reshape(LATS, 2, shard, OWN)
    up = jnp.transpose(up, (2, 0, 1, 3)).reshape(shard, -1)
    sums = joined[8 * shard : 8 * shard + 1] + joined[8 * shard + 1 : 8 * shard + 2]
    weight = w_query.astype(F32)
    piece = lambda i, n=1: line[i * shard : (i + n) * shard]
    return (
        part(0) * gain + bias * sums,
        part(1),
        part(2),
        part(3),
        up,
        part(6, 2),
        jnp.sum(part(0) * weight, axis=1),
        jnp.sum(weight * sums, axis=1),
        piece(2),
        piece(3),
        piece(4),
        piece(6, 2),
        piece(5),
    )


def solution(mesh):
    rows = P(("scene", "lat"), None)
    line = P(("scene", "lat"))
    scene = P("scene", None)
    in_specs = (scene, rows, P("scene"), scene, scene) + (rows,) * 6 + (line,) * 7
    out_specs = (scene, scene, rows) + (rows,) * 6 + (line,) * 7
    return jax.shard_map(body, mesh=mesh, in_specs=in_specs, out_specs=out_specs, check_vma=False)
```

```python
import math
from functools import partial

import jax
import jax.numpy as jnp
from jax import lax
from jax.experimental import pallas as pl
from jax.experimental.pallas import tpu as pltpu
from jax.sharding import PartitionSpec as P

HEADS = 12
HEAD_DIM = 64
VIEWS = 10
VIEW_TOK = 300
LANES = 128
LATS = 4
OWN_HEADS = HEADS // LATS
OWN = OWN_HEADS * HEAD_DIM
DEAD = -1e30
LOG2E = math.log2(math.e)
Q_SCALE = 0.125 * LOG2E
ROOT = math.sqrt(2.0 / math.pi)
SCALE = 1.0
VMEM_BYTES = 64 * 2**20 - 2**16
BF = jnp.bfloat16
F32 = jnp.float32


def dot(left, right):
    return jnp.dot(left, right, preferred_element_type=F32)


def dot_rt(left, right):
    return lax.dot_general(left, right, (((1,), (1,)), ((), ())), preferred_element_type=F32)


def dot_lt(left, right):
    return lax.dot_general(left, right, (((0,), (0,)), ((), ())), preferred_element_type=F32)


def params():
    return pltpu.CompilerParams(vmem_limit_bytes=VMEM_BYTES)


def cost(micros):
    return pl.CostEstimate(
        flops=int(micros * SCALE * 1e9), bytes_accessed=int(micros * SCALE * 3.3e6), transcendentals=0
    )


def vmem(count):
    return [pl.BlockSpec(memory_space=pltpu.VMEM)] * count


ANY = pl.BlockSpec(memory_space=pl.ANY)
SMEM = pl.BlockSpec(memory_space=pltpu.SMEM)


def shape(dims, dtype=BF):
    return jax.ShapeDtypeStruct(tuple(dims), dtype)


def norm_parts(values):
    center = values - jnp.mean(values, axis=-1, keepdims=True)
    spread = jnp.mean(center * center, axis=-1, keepdims=True)
    factor = lax.rsqrt(spread + 1e-05)
    return center * factor, factor


def norm_back(grad_out, normed, factor, gain_row):
    scaled = grad_out * gain_row
    return factor * (
        scaled
        - jnp.mean(scaled, axis=-1, keepdims=True)
        - normed * jnp.mean(scaled * normed, axis=-1, keepdims=True)
    )


def swap(values, axis, step):
    count = lax.axis_size(axis)
    return lax.ppermute(values, axis, [(i, i ^ step) for i in range(count)])


def stages(count):
    found, stride = [], count
    while stride > 1:
        group = 4 if stride % 4 == 0 else 2
        stride //= group
        found.append((stride, group))
    return found


def collect_kernel(count, *refs):
    out, rows = refs[-1], 0
    for ref in refs[:count]:
        out[rows : rows + ref.shape[0]] = ref[...]
        rows += ref.shape[0]


def collect(values, after):
    rows = sum(v.shape[0] for v in values)
    return pl.pallas_call(
        partial(collect_kernel, len(values)),
        out_shape=shape((rows,) + values[0].shape[1:]),
        in_specs=vmem(len(values)) + [ANY] * len(after),
        out_specs=pl.BlockSpec(memory_space=pltpu.VMEM),
        compiler_params=params(),
        cost_estimate=cost(0.3),
        name="collect",
    )(*values, *after)


def gather_scene(parts, after=()):
    steps = [0]
    got = [parts]
    passed = []
    for stride, group in stages(lax.axis_size("scene")):
        if len(got) == 1:
            parts = got[0]
        else:
            parts = collect(got, after) if after else jnp.concatenate(got)
        got = [parts] + [swap(parts, "scene", k * stride) for k in range(1, group)]
        steps = [step ^ (k * stride) for k in range(group) for step in steps]
        passed = [parts]
    return got, steps, passed


def in_order(stacked, steps, me):
    places = [steps.index(i) for i in range(len(steps))]
    order = jnp.take(jnp.array(places, jnp.int32), jnp.arange(len(steps)) ^ me)
    return jnp.take(stacked, order, axis=0)


def scatter_scene(blocks):
    count = lax.axis_size("scene")
    me = lax.axis_index("scene")
    held = blocks
    for stride, group in reversed(stages(count)):
        digit = (me // stride) % group
        view = held.reshape((-1, group) + blocks.shape[1:])
        total = lax.dynamic_index_in_dim(view, digit, 1, keepdims=False).astype(F32)
        for k in range(1, group):
            mine = lax.dynamic_index_in_dim(view, digit ^ k, 1, keepdims=False)
            total = total + swap(mine.astype(BF), "scene", k * stride).astype(F32)
        held = total.astype(BF)
    return total.reshape(blocks.shape[1:])


def fold(rows):
    half = rows.shape[0] // 2
    return jnp.concatenate([rows[:half], rows[half:]], axis=1)


def unfold(rows):
    half = rows.shape[1] // 2
    return jnp.concatenate([rows[:, :half], rows[:, half:]], axis=0)


def choose(index, options):
    picked = options[0]
    for i in range(1, len(options)):
        picked = jnp.where(index == i, options[i], picked)
    return picked


def pack_kernel(where, w_query, w_key, w_value, *refs):
    vectors, out = refs[:-LATS], refs[-LATS:]
    values = [w[...].astype(F32) for w in (w_query, w_key, w_value)]
    line = [v[...].astype(F32).reshape(1, v.shape[0]) for v in vectors]
    line = jnp.concatenate(line, axis=1)
    line = jnp.concatenate([line, jnp.zeros((1, OWN - line.shape[1]), F32)], axis=1) if (
        line.shape[1] < OWN
    ) else line
    tail = jnp.broadcast_to(line, (8, OWN))
    for k in range(LATS):
        target = where[0] ^ k
        rows = []
        for value in values:
            cols = [value[:, p * OWN : (p + 1) * OWN] for p in range(LATS)]
            rows.append(choose(target, cols))
        out[k][...] = fold(jnp.concatenate(rows + [tail], axis=0)).astype(BF)


def pack(where, w_query, w_key, w_value, vectors):
    rows = 3 * w_query.shape[0] + 8
    return pl.pallas_call(
        pack_kernel,
        out_shape=[shape((rows // 2, 2 * OWN))] * LATS,
        in_specs=[SMEM] + vmem(3 + len(vectors)),
        out_specs=vmem(LATS),
        compiler_params=params(),
        cost_estimate=cost(0.5),
        name="pack",
    )(where, w_query, w_key, w_value, *vectors)


def unpack_kernel(steps, where, *refs):
    *chunks, trio, turned, rows_out, up_out, held, lines = refs
    lat, scene = where[0], where[3]
    shard = held.shape[1] // (len(steps) * LATS)
    entry = 0
    for chunk in chunks:
        for p in range(chunk.shape[0]):
            values = unfold(chunk[p].astype(F32))
            source = (scene ^ steps[entry // LATS]) * LATS + (lat ^ (entry % LATS))
            at = pl.ds(pl.multiple_of(source * shard, 8), shard)
            for m in range(3):
                held[m, at, :] = values[m * shard : (m + 1) * shard]
            lines[pl.ds(source, 1), :] = values[3 * shard : 3 * shard + 1]
            entry += 1
    for m in range(3):
        low = held[m].astype(BF)
        trio[m] = low
        turned[m] = held[m].T.astype(BF)
    sources = lines.shape[0]
    low = lines[...].astype(BF)
    for target, size, first in ((rows_out, shard, 0), (up_out, 2 * shard, 6)):
        wide = target.shape[1]
        col = lax.broadcasted_iota(jnp.int32, (1, wide), 1).astype(F32)
        owner = jnp.floor((col + 0.5) * (1.0 / size))
        spot = col - owner * size
        row = lax.broadcasted_iota(jnp.int32, (OWN, 1), 0).astype(F32)
        line = lax.broadcasted_iota(jnp.int32, (sources, 1), 0).astype(F32)
        for v in range(6 if first == 0 else 1):
            hot = jnp.where(row == spot + (first + v) * shard, 1.0, 0.0).astype(BF)
            spread = jnp.where(line == owner, dot(low, hot), 0.0)
            target[v : v + 1, :] = jnp.sum(spread, axis=0, keepdims=True)


def unpack(where, chunks, steps, shard):
    sources = len(steps) * LATS
    width = sources * shard
    return pl.pallas_call(
        partial(unpack_kernel, steps),
        out_shape=[
            shape((3, width, OWN)),
            shape((3, OWN, width)),
            shape((8, width), F32),
            shape((1, 2 * width), F32),
        ],
        in_specs=[SMEM] + vmem(len(chunks)),
        out_specs=vmem(4),
        scratch_shapes=[pltpu.VMEM((3, width, OWN), F32), pltpu.VMEM((sources, OWN), F32)],
        compiler_params=params(),
        cost_estimate=cost(0.5),
        name="unpack",
    )(where, *chunks)


def attention_weights(where, w_query, w_key, w_value, vectors, latents, lat_pad, early, first):
    shard, width = w_query.shape
    if shard % 8 == 0:
        pieces = pack(where, w_query, w_key, w_value, vectors)
        pieces = [pieces[0]] + [swap(pieces[k], "lat", k) for k in range(1, LATS)]
        own_lat = pad_latents(latents, lat_pad, pieces[2:])
        stacked = collect([p[None] for p in pieces], first)
        chunks, steps, passed = gather_scene(stacked, [own_lat] + early)
        return unpack(where, chunks, steps, shard), own_lat, [stacked] + passed
    flat = jnp.concatenate(vectors)
    flat = jnp.pad(flat, (0, OWN - flat.shape[0])).reshape(1, OWN)
    lat, scene = lax.axis_index("lat"), lax.axis_index("scene")
    scenes = lax.axis_size("scene")
    trio = jnp.stack([w_query, w_key, w_value]).reshape(3, shard, LATS, OWN)
    trio = jnp.transpose(trio, (2, 0, 1, 3)).reshape(LATS, 3 * shard, OWN)
    message = jnp.concatenate([trio, jnp.broadcast_to(flat, (LATS, 1, OWN))], axis=1)
    pieces = [lax.dynamic_index_in_dim(message, lat ^ k, 0, keepdims=False) for k in range(LATS)]
    pieces = [pieces[0]] + [swap(pieces[k], "lat", k) for k in range(1, LATS)]
    pieces = in_order(jnp.stack(pieces), list(range(LATS)), lat)
    chunks, steps, passed = gather_scene(pieces[None])
    gathered = in_order(jnp.concatenate(chunks), steps, scene)
    trio = gathered[:, :, : 3 * shard].reshape(scenes, LATS, 3, shard, OWN)
    trio = jnp.transpose(trio, (2, 0, 1, 3, 4)).reshape(3, width, OWN)
    lines = gathered[:, :, 3 * shard, : 8 * shard].astype(F32).reshape(scenes * LATS, 8, shard)
    rows = jnp.transpose(lines, (1, 0, 2)).reshape(8, width)
    up = lines[:, 6:].reshape(1, 2 * width)
    own_lat = pad_latents(latents, lat_pad, [])
    return (trio, jnp.transpose(trio, (0, 2, 1)), rows, up), own_lat, []


def gate_kernel(*refs):
    pass


def gate(values, after):
    one = not isinstance(values, list)
    values = [values] if one else values
    out = pl.pallas_call(
        gate_kernel,
        out_shape=[shape(v.shape, v.dtype) for v in values],
        in_specs=[ANY] * (len(values) + len(after)),
        out_specs=[ANY] * len(values),
        input_output_aliases={i: i for i in range(len(values))},
        compiler_params=params(),
        cost_estimate=cost(0.2),
        name="gate",
    )(*values, *after)
    return out[0] if one else list(out)


def pad_kernel(latents, *refs):
    out = refs[-1]
    rows = latents.shape[0]
    out[:rows, :] = latents[...]
    out[rows:, :] = jnp.zeros((out.shape[0] - rows, out.shape[1]), out.dtype)


def pad_latents(latents, rows, after):
    return pl.pallas_call(
        pad_kernel,
        out_shape=shape((rows, latents.shape[1])),
        in_specs=vmem(1) + [ANY] * len(after),
        out_specs=pl.BlockSpec(memory_space=pltpu.VMEM),
        compiler_params=params(),
        cost_estimate=cost(0.5),
        name="pad_latents",
    )(latents, *after)


def pack_feed_kernel(w_out, w_up, w_down, *refs):
    out = refs[-1]
    shard, width = w_out.shape
    out[: 2 * shard, :] = w_down[...]
    out[2 * shard : 3 * shard, :] = w_out[...]
    out[3 * shard : 4 * shard, :] = w_up[:, :width]
    out[4 * shard :, :] = w_up[:, width:]


def pack_feed(w_out, w_up, w_down, after):
    shard, width = w_out.shape
    return pl.pallas_call(
        pack_feed_kernel,
        out_shape=shape((5 * shard, width)),
        in_specs=vmem(3) + [ANY] * len(after),
        out_specs=pl.BlockSpec(memory_space=pltpu.VMEM),
        compiler_params=params(),
        cost_estimate=cost(0.3),
        name="pack_feed",
    )(w_out, w_up, w_down, *after)


def assemble_kernel(gathered, *refs):
    w_out, w_up, w_down = refs[-3:]
    shard = gathered.shape[1] // 5
    width = w_out.shape[1]
    w_down[...] = gathered[:, : 2 * shard, :].reshape(w_down.shape)
    w_out[...] = gathered[:, 2 * shard : 3 * shard, :].reshape(w_out.shape)
    w_up[:, :width] = gathered[:, 3 * shard : 4 * shard, :].reshape(width, width)
    w_up[:, width:] = gathered[:, 4 * shard :, :].reshape(width, width)


def assemble(gathered, after):
    width = gathered.shape[2]
    return pl.pallas_call(
        assemble_kernel,
        out_shape=[shape((width, width)), shape((width, 2 * width)), shape((2 * width, width))],
        in_specs=vmem(1) + [ANY] * len(after),
        out_specs=vmem(3),
        compiler_params=params(),
        cost_estimate=cost(6),
        name="assemble",
    )(gathered, *after)


def feed_weights(w_out, w_up, w_down, after):
    if w_out.shape[0] % 8 == 0:
        packed = gate(pack_feed(w_out, w_up, w_down, after[:1]), after[1:])
        return lax.all_gather(packed, ("scene", "lat"), axis=0, tiled=False)
    width = w_out.shape[1]
    packed = jnp.concatenate([w_down, w_out, w_up[:, :width], w_up[:, width:]], axis=0)
    held = lax.all_gather(packed, ("scene", "lat"), axis=0, tiled=False)
    shard = w_out.shape[0]
    parts = [held[:, n * shard : (n + 1) * shard].reshape(width, width) for n in range(2, 5)]
    up = jnp.concatenate(parts[1:], axis=1)
    return parts[0], up, held[:, : 2 * shard].reshape(2 * width, width)


def widen(weight):
    gap = jnp.zeros((weight.shape[0], 2 * LANES - OWN), weight.dtype)
    return jnp.concatenate([weight, gap], axis=1)


def own_lanes(head, axis):
    spot = lax.broadcasted_iota(jnp.int32, (1, LANES) if axis == 1 else (LANES, 1), axis)
    first = (head % 2) * HEAD_DIM
    return (spot >= first) & (spot < first + HEAD_DIM), spot, HEAD_DIM - first


def lane_block(values, head):
    return values[:, (head // 2) * LANES : (head // 2 + 1) * LANES]


def norms_kernel(where, rays, normed_low, centers, factors):
    values = rays[...].astype(F32)
    middle = jnp.mean(values, axis=-1, keepdims=True)
    center = values - middle
    factor = lax.rsqrt(jnp.mean(center * center, axis=-1, keepdims=True) + 1e-05)
    normed_low[...] = (center * factor).astype(BF)
    centers[...] = jnp.broadcast_to(middle, centers.shape)
    factors[...] = jnp.broadcast_to(factor, factors.shape)


def make_norms(where, rays):
    count, width = rays.shape
    block = count // 4
    rows = lambda cols: pl.BlockSpec((block, cols), lambda i, w: (i, 0))
    return pl.pallas_call(
        norms_kernel,
        grid_spec=pltpu.PrefetchScalarGridSpec(
            num_scalar_prefetch=1,
            grid=(4,),
            in_specs=[pl.BlockSpec((block, width), lambda i, w: (i ^ (2 * w[1]), 0))],
            out_specs=[rows(width), rows(LANES), rows(LANES)],
        ),
        out_shape=[shape((count, width)), shape((count, LANES), F32), shape((count, LANES), F32)],
        compiler_params=params(),
        cost_estimate=cost(1),
        name="norms",
    )(where, rays)


def query_kernel(where, rays, centers, factors, weight, rows_in, query, wide):
    @pl.when(pl.program_id(0) == 0)
    def _():
        wide[...] = widen(weight[0])

    copies = rays.shape[1] // LANES
    middle = jnp.concatenate([centers[...]] * copies, axis=1)
    factor = jnp.concatenate([factors[...]] * copies, axis=1)
    normed = (rays[...].astype(F32) - middle) * factor
    low = (normed * rows_in[0:1, :] + rows_in[1:2, :]).astype(BF)
    values = dot(low, wide[...]) * Q_SCALE
    for h in range(OWN_HEADS):
        own, lane, spare = own_lanes(h, 1)
        one = jnp.where(lane == spare, 1.0, 0.0)
        query[h] = jnp.where(own, lane_block(values, h), one).astype(BF)


def make_queries(where, rays, centers, factors, trio, rows_in):
    count, width = rays.shape
    block = count // 4
    whole = lambda a: pl.BlockSpec(a.shape, lambda i, w: (0,) * a.ndim)
    return pl.pallas_call(
        query_kernel,
        grid_spec=pltpu.PrefetchScalarGridSpec(
            num_scalar_prefetch=1,
            grid=(4,),
            in_specs=[
                pl.BlockSpec((block, width), lambda i, w: (i ^ (2 * w[1]), 0)),
                pl.BlockSpec((block, LANES), lambda i, w: (i, 0)),
                pl.BlockSpec((block, LANES), lambda i, w: (i, 0)),
                pl.BlockSpec((1,) + trio.shape[1:], lambda i, w: (0, 0, 0)),
                whole(rows_in),
            ],
            out_specs=pl.BlockSpec((OWN_HEADS, block, LANES), lambda i, w: (0, i, 0)),
            scratch_shapes=[pltpu.VMEM((width, 2 * LANES), BF)],
        ),
        out_shape=shape((OWN_HEADS, count, LANES)),
        compiler_params=params(),
        cost_estimate=cost(2),
        name="queries",
    )(where, rays, centers, factors, trio, rows_in)


def keyset_kernel(count, *refs):
    lats, trio, shut = refs[:count], refs[count], refs[count + 1]
    key, key_t, val, val_t, wide, here = refs[-6:]
    step = pl.program_id(0)

    @pl.when(step == 0)
    def _():
        wide[0] = widen(trio[1])
        wide[1] = widen(trio[2])

    for j, lat in enumerate(lats):

        @pl.when(step == j)
        def _():
            here[...] = lat[...]

    keys = dot(here[...], wide[0])
    vals = dot(here[...], wide[1])
    blocks = lambda v: [v[:, i * LANES : (i + 1) * LANES].T for i in range(2)]
    keys_t, vals_t = blocks(keys), blocks(vals)
    for h in range(OWN_HEADS):
        own, _, _ = own_lanes(h, 1)
        own_line, line, spare = own_lanes(h, 0)
        key[h] = jnp.where(own, lane_block(keys, h), 0.0).astype(BF)
        val[h] = jnp.where(own, lane_block(vals, h), 1.0).astype(BF)
        mask = jnp.where(line == spare, shut[0], 0.0)
        key_t[h] = jnp.where(own_line, keys_t[h // 2], mask).astype(BF)
        val_t[h] = jnp.where(own_line, vals_t[h // 2], 1.0).astype(BF)


def make_keyset(start, lats, trio, shut, held=None):
    count = len(lats)
    rows, width = lats[0].shape
    total = LATS * rows
    tall, long = shape((OWN_HEADS, total, LANES)), shape((OWN_HEADS, LANES, total))
    whole = lambda a: pl.BlockSpec(a.shape, lambda i: (0,) * a.ndim)
    down = pl.BlockSpec((OWN_HEADS, rows, LANES), lambda i: (0, start + i, 0))
    over = pl.BlockSpec((OWN_HEADS, LANES, rows), lambda i: (0, 0, start + i))
    extra = [] if held is None else list(held)
    return pl.pallas_call(
        partial(keyset_kernel, count),
        grid=(count,),
        out_shape=[tall, long, tall, long],
        in_specs=[whole(lat) for lat in lats]
        + [whole(trio), pl.BlockSpec((1, 1, rows), lambda i: (start + i, 0, 0))]
        + [ANY] * len(extra),
        out_specs=[down, over, down, over],
        scratch_shapes=[pltpu.VMEM((2, width, 2 * LANES), BF), pltpu.VMEM((rows, width), BF)],
        input_output_aliases={count + 2 + i: i for i in range(len(extra))},
        compiler_params=params(),
        cost_estimate=cost(5),
        name="keyset",
    )(*lats, trio, shut, *extra)


def attend_kernel(sub, query, key_t, val, *rest):
    context, native, weights, inverse, mixed = rest[-5:]
    head, part = pl.program_id(0), pl.program_id(1)
    rows = query.shape[1]
    own, _, _ = own_lanes(head, 1)
    spot = part * 2 + head // 2

    def score(i):
        return dot(query[0, i * sub : (i + 1) * sub, :], key_t[0])

    scores = score(0)
    for i in range(rows // sub):
        later = score(i + 1) if i + 1 < rows // sub else None
        at = slice(i * sub, (i + 1) * sub)
        low = jnp.exp2(scores - jnp.max(scores, axis=1, keepdims=True)).astype(BF)
        weights[0, at, :] = low
        summed = dot(low, val[0])
        scale = 1.0 / jnp.where(own, pltpu.roll(summed, HEAD_DIM, 1), summed)
        held = jnp.where(head == 1, mixed[spot, at, :], 0.0)
        mixed[spot, at, :] = jnp.where(own, summed * scale, held)
        inverse[0, at, :] = scale
        scores = later

    for p in range(2):

        @pl.when((head == OWN_HEADS - 1) & (part == p))
        def _():
            both = jnp.concatenate([mixed[2 * p], mixed[2 * p + 1]], axis=1).astype(BF)
            native[p * rows : (p + 1) * rows, :] = both
            context[:, p * OWN : (p + 1) * OWN] = both[:, :OWN]


def attend(half_index, query, key_t, val, held=None, after=()):
    _, count, _ = query.shape
    total = key_t.shape[2]
    half = count // 2
    block = half // 2
    sub = block // 3 if block % 48 == 0 else block
    rows = lambda cols: pl.BlockSpec((1, block, cols), lambda h, b: (h, 2 * half_index + b, 0))
    every = lambda rows, cols: pl.BlockSpec((1, rows, cols), lambda h, b: (h, 0, 0))
    extra = ([] if held is None else list(held)) + list(after)
    return pl.pallas_call(
        partial(attend_kernel, sub),
        grid=(OWN_HEADS, 2),
        in_specs=[rows(LANES), every(LANES, total), every(total, LANES)] + [ANY] * len(extra),
        out_specs=[
            pl.BlockSpec((block, 2 * OWN), lambda h, b: (0, 0)),
            pl.BlockSpec((half, 2 * LANES), lambda h, b: (0, 0)),
            rows(total),
            rows(LANES),
        ],
        out_shape=[
            shape((block, 2 * OWN)),
            shape((half, 2 * LANES)),
            shape((OWN_HEADS, count, total)),
            shape((OWN_HEADS, count, LANES), F32),
        ],
        scratch_shapes=[pltpu.VMEM((4, block, LANES), F32)],
        input_output_aliases={} if held is None else {3: 2, 4: 3},
        compiler_params=params(),
        cost_estimate=cost(16),
        name="attend",
    )(query, key_t, val, *extra)


def back_kernel(sub, lat_rows, head, fine, weights, inverse, *refs):
    d_here, d_there, ctx_here, ctx_there, query, key, val_t = refs[:7]
    refs = refs[7:]
    project = not fine or head > 0
    lats, normed_low, earlier, where = refs[:LATS], refs[LATS], refs[5:9], refs[9]
    count = LATS + (0 if not project else 2 if fine else 1)
    out, scratch = refs[-(count + (5 if project else 2)) :][:count], refs[-5 if project else -2 :]
    sums, d_query = scratch[:2]
    grads_out = out[LATS:]
    pair_out = query_out = out[:LATS]
    query_at = 2 * lat_rows
    step = pl.program_id(0)
    rows = weights.shape[1]
    half = 2 * rows
    start = pl.multiple_of((step % 2) * rows, rows)
    loads = []
    if project:
        lat_here, normed_here, sem = scratch[2:]
        for j, lat in enumerate(lats):
            at = pl.ds(j * lat_rows, lat_rows)
            loads.append(pltpu.make_async_copy(lat, lat_here.at[at], sem.at[j]))
        loads.append(pltpu.make_async_copy(normed_low, normed_here, sem.at[LATS]))

    @pl.when(step == 0)
    def _():
        for load in loads:
            load.start()

    own, lane, spare = own_lanes(head, 1)
    far = step >= 2
    upstream = jnp.where(far, d_there[...], d_here[...]).astype(F32)
    ctx = jnp.where(far, ctx_there[...], ctx_here[...]).astype(F32)
    scale = inverse[0]
    delta = jnp.sum(jnp.where(own, upstream * ctx, 0.0), axis=1, keepdims=True) * scale
    high = delta.astype(BF).astype(F32)
    rest = jnp.where(lane == spare + 1, high - delta, 0.0)
    rest = jnp.where(lane == spare, -high, rest)
    grad = jnp.where(own, upstream * scale, rest).astype(BF)
    val_part = dot_lt(grad, weights[0])
    found = []
    for i in range(rows // sub):
        at = slice(i * sub, (i + 1) * sub)
        d_weights = dot(grad[at], val_t[0])
        d_scores = (weights[0, at, :].astype(F32) * d_weights).astype(BF)
        d_query[pl.ds(start + i * sub, sub), :] = dot(d_scores, key[0]) * 0.125
        found.append(d_scores)
    d_scores = jnp.concatenate(found, axis=0) if len(found) > 1 else found[0]
    key_part = dot_lt(query[0], d_scores) * (1.0 / LOG2E)

    @pl.when(step == 0)
    def _():
        sums[0] = key_part
        sums[1] = val_part

    @pl.when(step > 0)
    def _():
        sums[0] += key_part
        sums[1] += val_part

    first = (head % 2) * HEAD_DIM

    @pl.when(step == 3)
    def _():
        for i in range(2):
            total = sums[i, first : first + HEAD_DIM].astype(BF)
            for j in range(LATS):
                pair_out[j][:, i * lat_rows : (i + 1) * lat_rows] = total[
                    :, j * lat_rows : (j + 1) * lat_rows
                ]

    for last in (1, 3):

        @pl.when(step == last)
        def _():
            turned = d_query[...].T[first : first + HEAD_DIM].astype(BF)
            for j in (last // 2, last // 2 + 2):
                query_out[j][:, query_at : query_at + half] = turned

    if not project:
        return

    @pl.when(step == 3)
    def _():
        for load in loads:
            load.wait()
        groups = [list(earlier), list(out[:LATS])] if head == 1 and fine else [list(out[:LATS])]
        at = slice(2 * lat_rows, 2 * lat_rows + half)
        turned = [jnp.concatenate([g[b][:, at] for g in groups], axis=0) for b in range(2)]
        part = dot(turned[0], normed_here[:half]) + dot(turned[1], normed_here[half:])
        both = []
        for i in range(2):
            at = slice(i * lat_rows, (i + 1) * lat_rows)
            for g in groups:
                both.append(jnp.concatenate([g[j][:, at] for j in range(LATS)], axis=1))
        both = dot(jnp.concatenate(both, axis=0), lat_here[...])
        rows = both.shape[0] // 2
        col = sum(jnp.sum(t.astype(F32), axis=1, keepdims=True) for t in turned)
        high = col.astype(BF).astype(F32)
        col = jnp.where(lane == 0, high, jnp.where(lane == 1, col - high, 0.0)).T[:16]
        parts = [p.T for p in (part, both[:rows], both[rows:])] + [col]
        if not fine:
            grads_out[0][...] = jnp.concatenate(parts, axis=0)
            return
        send, keep = grads_out
        scenes = 2 * send.shape[0]
        width = normed_here.shape[1]
        block = width // scenes
        for s in range(scenes):
            mine = [p[s * block : (s + 1) * block] for p in parts[:3]] + parts[3:]
            if head == 2:
                mine = fold(jnp.concatenate(mine + [jnp.zeros((16, HEAD_DIM), F32)], axis=0))
            else:
                mine = jnp.concatenate(mine, axis=0)
            mine = mine.astype(BF)
            kept = where[4] == s % 2

            @pl.when(kept)
            def _():
                keep[s // 2] = mine

            @pl.when(jnp.logical_not(kept))
            def _():
                send[s // 2] = mine


def attend_back(head, fine, weights, inverse, d_ctxs, ctxs, query, key, val_t, lats, normed_low, earlier, where, after):
    _, count, total = weights.shape
    rows = count // 4
    sub = rows // 2 if rows % 32 == 0 else rows
    lat_rows = total // LATS
    width = normed_low.shape[1]
    pad = lambda n: -(-n // LANES) * LANES
    outs = [shape((HEAD_DIM, pad(2 * lat_rows + 2 * rows)))] * LATS
    project = not fine or head > 0
    if not fine:
        outs.append(shape((3 * width + 16, HEAD_DIM), F32))
    elif project:
        block = 3 * (width // 8)
        dims = (4, block + 16, LANES) if head == 1 else (4, block // 2 + 16, LANES)
        outs += [shape(dims)] * 2
    of_head = lambda cols: pl.BlockSpec((1, rows, cols), lambda b: (head, b, 0))
    here = pl.BlockSpec((rows, LANES), lambda b: (jnp.minimum(b, 1), head // 2))
    there = pl.BlockSpec((rows, LANES), lambda b: (jnp.maximum(b, 2) - 2, head // 2))
    whole = lambda a: pl.BlockSpec(a.shape, lambda b: (0,) * len(a.shape))
    earlier = list(earlier) if head == 1 and fine else [where] * LATS
    early = [whole(a) for a in earlier] if head == 1 and fine else [ANY] * LATS
    return pl.pallas_call(
        partial(back_kernel, sub, lat_rows, head, fine),
        grid=(4,),
        in_specs=[
            of_head(total),
            of_head(LANES),
            here,
            there,
            here,
            there,
            of_head(LANES),
            pl.BlockSpec((1, total, LANES), lambda b: (head, 0, 0)),
            pl.BlockSpec((1, LANES, total), lambda b: (head, 0, 0)),
        ]
        + [ANY] * (LATS + 1)
        + early
        + [SMEM]
        + [ANY] * len(after),
        out_specs=[whole(o) for o in outs],
        out_shape=outs,
        scratch_shapes=[
            pltpu.VMEM((2, LANES, total), F32),
            pltpu.VMEM((2 * rows, LANES), F32),
        ]
        + [
            pltpu.VMEM((total, width), BF),
            pltpu.VMEM((count, width), BF),
            pltpu.SemaphoreType.DMA((LATS + 1,)),
        ]
        * project,
        compiler_params=params(),
        cost_estimate=cost(14),
        name=f"attend_back_{head}",
    )(weights, inverse, *d_ctxs, *ctxs, query, key, val_t, *lats, normed_low, *earlier, where, *after)


def quarter_halves(values, core):
    mid = values.shape[1] // 2
    low, high = values[:, :mid], values[:, mid:]
    return jnp.where(core == 0, low, high), jnp.where(core == 0, high, low)


def feed_kernel(fine, where, *refs):
    ins, rows_in, up_shift = refs[:9], refs[9], refs[10]
    layer_out, layer_half, d_middle, d_own, d_sibling = refs[11:16]
    grads_out = refs[16:-15]
    rays, ctxs, upstream, w_out, w_up, w_down, low_out, low_mid, own, sibling = refs[-15:-5]
    halves, active, lifted, sem_in, sem_out = refs[-5:]
    lat, core, side = where[0], where[1], where[2]
    half, width = rays.shape
    hidden = w_up.shape[1]
    block = half // 4
    mine = pl.ds(pl.multiple_of(core * half, half), half)
    sources = [ins[0].at[mine]] + list(ins[1:5]) + [ins[6], ins[7], ins[5].at[mine], ins[8]]
    targets = [rays] + [ctxs.at[j] for j in range(LATS)] + [w_out, w_up, upstream, w_down]
    loads = [
        pltpu.make_async_copy(a, b, sem_in.at[n]) for n, (a, b) in enumerate(zip(sources, targets))
    ]
    stores = []

    def store(source, target):
        stores.append(pltpu.make_async_copy(source, target, sem_out.at[len(stores)]))
        stores[-1].start()

    for load in loads:
        load.start()
    for load in loads[:6]:
        load.wait()
    gain, bias = rows_in[2:3, :], rows_in[3:4, :]
    spots = [pl.ds(pl.multiple_of((lat ^ j) * OWN, OWN), OWN) for j in range(LATS)]

    def ctx_rows(j, i):
        at = slice((i % 2) * block, (i % 2 + 1) * block)
        return ctxs[j, at, (i // 2) * OWN : (i // 2 + 1) * OWN]

    begun = []
    for i in range(4):
        at = slice(i * block, (i + 1) * block)
        middle = rays[at, :].astype(F32) + rows_in[4:5, :]
        for j in range(LATS):
            middle = middle + dot(ctx_rows(j, i), w_out[spots[j], :])
        normed, factor = norm_parts(middle)
        lifted[at, :] = (normed * gain + bias).astype(BF)
        begun.append((middle, normed, factor))
    for load in loads[6:]:
        load.wait()
    column = lambda v: jnp.sum(v, axis=0, keepdims=True)
    sums, up_sums = [0.0] * 4, 0.0
    for i in range(4):
        at = slice(i * block, (i + 1) * block)
        middle, normed, factor = begun[i]
        before = dot(lifted[at, :], w_up[...]) + up_shift[...]
        squared = before * before
        bent = jnp.tanh(before * (ROOT + (ROOT * 0.044715) * squared))
        scaled = 0.5 * before
        act = (scaled + scaled * bent).astype(BF)
        active[at, :] = act
        slope = 0.5 + 0.5 * bent + scaled * (1.0 - bent * bent) * (
            ROOT + (3 * 0.044715 * ROOT) * squared
        )
        d_pre = (dot_rt(upstream[at, :], w_down[...]) * slope).astype(BF)
        halves[at, :hidden] = d_pre
        low_out[at, :] = (middle + dot(act, w_down[...]) + rows_in[5:6, :]).astype(BF)
        d_lifted = dot_rt(d_pre, w_up[...])
        up_wide = upstream[at, :].astype(F32)
        d_mid = up_wide + norm_back(d_lifted, normed, factor, gain)
        branch = d_mid.astype(BF)
        low_mid[at, :] = branch
        halves[at, hidden:] = branch
        gap = jnp.zeros((block, 2 * LANES - OWN), F32)
        for target, spot in zip((own, sibling), spots):
            part = dot_rt(branch, w_out[spot, :])
            target[at, :] = jnp.concatenate([part, gap], axis=1).astype(BF)
        pieces = (d_lifted * normed, d_lifted, branch.astype(F32), up_wide)
        sums = [total + column(piece) for total, piece in zip(sums, pieces)]
        up_sums = up_sums + column(d_pre.astype(F32))
    store(sibling, d_sibling)
    store(own, d_own)
    store(low_out, layer_half)
    store(low_out, layer_out.at[mine])
    store(low_mid, d_middle)

    wide, narrow = hidden // 2, width // 2
    pre_half = halves[:, pl.ds(pl.multiple_of(side * wide, LANES), wide)]
    branch_half = halves[:, pl.ds(pl.multiple_of(hidden + side * narrow, LANES), narrow)]
    up_half = upstream[:, pl.ds(pl.multiple_of(side * narrow, LANES), narrow)]
    up_grad = dot_lt(lifted[...], pre_half)
    down_grad = dot_lt(active[...], up_half)
    if fine:
        messages = grads_out[2:]
        scenes = messages[0].shape[0]
        shard = width // (scenes * LATS)

        def parities(values, rows):
            parts = [values[n * rows : (n + 1) * rows] for n in range(LATS)]
            even = jnp.concatenate([parts[0], parts[2]], axis=0)
            odd = jnp.concatenate([parts[1], parts[3]], axis=0)
            first, second = jnp.where(core == 0, even, odd), jnp.where(core == 0, odd, even)
            return zip(messages, (first.astype(BF), second.astype(BF)))

        for s in range(scenes):
            rows = LATS * shard
            for message, part in parities(up_grad[s * rows : (s + 1) * rows], shard):
                message[s, 2 * shard : 4 * shard, :] = part[:, :narrow]
                message[s, 4 * shard : 6 * shard, :] = part[:, narrow:]
            rows = 2 * LATS * shard
            for message, part in parities(down_grad[s * rows : (s + 1) * rows], 2 * shard):
                message[s, 6 * shard : 10 * shard, :] = part
        for j in range(LATS):
            ctx = jnp.concatenate([ctxs[j, :, :OWN], ctxs[j, :, OWN:]], axis=0)
            values = dot_lt(ctx, branch_half)
            rows = LATS * shard
            for q in range(OWN // rows):
                place = (lat ^ j) * (OWN // rows) + q
                for message, part in parities(values[q * rows : (q + 1) * rows], shard):
                    message[place, : 2 * shard, :] = part
        lines = line_up(sums, up_sums, scenes * LATS)
        for s in range(scenes):
            line = lines[s * LATS : (s + 1) * LATS]
            even = jnp.concatenate([line[0:1], line[2:3]], axis=0)
            odd = jnp.concatenate([line[1:2], line[3:4]], axis=0)
            for n, message in enumerate(messages):
                rows = jnp.where(core == n, even, odd)
                rows = jnp.concatenate([rows, jnp.zeros((14, OWN), F32)], axis=0)
                rows = jnp.concatenate([rows, jnp.zeros_like(rows)], axis=1)
                message[s, 10 * shard :, :] = rows.astype(BF)
        for message, target in zip(messages, grads_out):
            store(message, target)
    else:
        for i, part in ((1, up_grad), (2, down_grad)):
            first, second = quarter_halves(part, core)
            grads_out[2 * i][...] = first.astype(BF)
            grads_out[2 * i + 1][...] = second.astype(BF)
        for j in range(LATS):
            ctx = jnp.concatenate([ctxs[j, :, :OWN], ctxs[j, :, OWN:]], axis=0)
            first, second = quarter_halves(dot_lt(ctx, branch_half), core)
            grads_out[0][spots[j], :] = first.astype(BF)
            grads_out[1][spots[j], :] = second.astype(BF)
        grads_out[6][...] = jnp.concatenate(sums + [jnp.zeros((4, width), F32)], axis=0)
        grads_out[7][...] = jnp.broadcast_to(up_sums, (8, hidden))
    for copy in stores:
        copy.wait()


def line_up(sums, up_sums, sources):
    total = None
    shard = sums[0].shape[1] // sources
    for rows, size, first in ((sums, shard, 2), ([up_sums], 2 * shard, 6)):
        wide = rows[0].shape[1]
        col = lax.broadcasted_iota(jnp.int32, (1, wide), 1).astype(F32)
        owner = jnp.floor((col + 0.5) * (1.0 / size))
        spot = (col - owner * size)
        row = lax.broadcasted_iota(jnp.int32, (OWN, 1), 0).astype(F32)
        line = lax.broadcasted_iota(jnp.int32, (sources, 1), 0).astype(F32)
        for v, values in enumerate(rows):
            hot = jnp.where(row == spot + (first + v) * shard, 1.0, 0.0).astype(BF)
            mine = jnp.where(line == owner, values, 0.0).astype(BF)
            part = dot_rt(mine, hot)
            total = part if total is None else total + part
    return total


def feed(where, rays, ctxs, upstream, weights, rows_in, up_shift, scenes, fine):
    count, width = rays.shape
    hidden = up_shift.shape[1]
    half = count // 2
    mats = [(width, width // 4), (width, hidden // 4), (hidden, width // 4)]
    if fine:
        message = (scenes, 10 * (width // (scenes * LATS)) + 16, width // 2)
        grads = [shape(message)] * 2
        spec, held = ANY, [pltpu.VMEM(message, BF)] * 2
    else:
        grads = [shape(d) for d in mats for _ in range(2)]
        grads += [shape((8, width), F32), shape((8, hidden), F32)]
        spec, held = pl.BlockSpec(memory_space=pltpu.VMEM), []
    return pl.pallas_call(
        partial(feed_kernel, fine),
        out_shape=[
            shape((count, width)),
            shape((half, width)),
            shape((half, width)),
            shape((half, 2 * LANES)),
            shape((half, 2 * LANES)),
        ]
        + grads,
        in_specs=[SMEM] + [ANY] * 9 + vmem(2),
        out_specs=[ANY] * 5 + [spec] * len(grads),
        scratch_shapes=held
        + [
            pltpu.VMEM((half, width), BF),
            pltpu.VMEM((LATS, half // 2, 2 * OWN), BF),
            pltpu.VMEM((half, width), BF),
            pltpu.VMEM((width, width), BF),
            pltpu.VMEM((width, hidden), BF),
            pltpu.VMEM((hidden, width), BF),
            pltpu.VMEM((half, width), BF),
            pltpu.VMEM((half, width), BF),
            pltpu.VMEM((half, 2 * LANES), BF),
            pltpu.VMEM((half, 2 * LANES), BF),
            pltpu.VMEM((half, hidden + width), BF),
            pltpu.VMEM((half, hidden), BF),
            pltpu.VMEM((half, width), BF),
            pltpu.SemaphoreType.DMA((9,)),
            pltpu.SemaphoreType.DMA((8,)),
        ],
        compiler_params=params(),
        cost_estimate=cost(26),
        name="feed",
    )(where, rays, *ctxs, upstream, *weights, rows_in, up_shift)


def halve_kernel(bit, where, own, got, send, keep):
    count = send.shape[0]
    mine = where[4] if count == 4 else where[6]
    low = (1 << bit) - 1
    for n in range(count):
        first = ((n & ~low) << 1) | (n & low)
        for target, side in ((send, 1 - mine), (keep, mine)):
            at = first + (side << bit)
            target[n] = (own[at].astype(F32) + got[at].astype(F32)).astype(BF)


def halve(where, bit, own, got):
    count, rows, cols = own.shape
    half = shape((count // 2, rows, cols))
    return pl.pallas_call(
        partial(halve_kernel, bit),
        out_shape=[half, half],
        in_specs=[SMEM] + vmem(2),
        out_specs=vmem(2),
        compiler_params=params(),
        cost_estimate=cost(3),
        name="halve",
    )(where, own, got)


def spread_kernel(count, where, *refs):
    pairs, (feed_keep, feed_got), out = refs[: 2 * count], refs[2 * count : 2 * count + 2], refs[-6:]
    for k in range(4):
        at = where[5] ^ k
        parts = [
            pairs[2 * n][at].astype(F32) + pairs[2 * n + 1][at].astype(F32) for n in range(count)
        ]
        out[k][...] = jnp.concatenate(parts, axis=0).astype(BF)
    mine = where[5] % 2
    for target, at in ((out[4], 1 - mine), (out[5], mine)):
        target[...] = (feed_keep[at].astype(F32) + feed_got[at].astype(F32)).astype(BF)


def add_spread(where, pairs, feed_keep, feed_got, after):
    rows = sum(keep.shape[1] for keep, _ in pairs)
    last = shape(feed_keep.shape[1:])
    return pl.pallas_call(
        partial(spread_kernel, len(pairs)),
        out_shape=[shape((rows, pairs[0][0].shape[2]))] * 4 + [last] * 2,
        in_specs=[SMEM] + vmem(2 * len(pairs) + 2) + [ANY] * len(after),
        out_specs=vmem(6),
        compiler_params=params(),
        cost_estimate=cost(2),
        name="add_spread",
    )(where, *[a for pair in pairs for a in pair], feed_keep, feed_got, *after)


def regroup_kernel(shard, where, *refs):
    trio, out, held = refs[:4], refs[6:10], refs[10]
    side = where[2]
    block = LATS * shard
    total = sum(r[...].astype(F32) for r in trio)
    pair, third = total[: 3 * block + 16], unfold(total[3 * block + 16 :])
    held[...] = jnp.concatenate([pair, third[: 3 * block + 16]], axis=1)
    feed_sum = refs[4][...].astype(F32) + refs[5][...].astype(F32)
    places = [[], []]
    for q in range(2):
        for first, rows in ((0, shard), (2 * shard, shard), (4 * shard, shard), (6 * shard, 2 * shard)):
            places[q].append(feed_sum[first + q * rows : first + (q + 1) * rows])
        line = feed_sum[10 * shard + q : 10 * shard + q + 1]
        places[q].append(jnp.broadcast_to(line, (8, line.shape[1])))
    places = [jnp.concatenate(p, axis=0) for p in places]
    for k in range(LATS):
        rows = []
        for n in range(3):
            at = n * block + (where[0] ^ k) * shard
            rows.append(held[pl.ds(pl.multiple_of(at, 8), shard), :])
        rows.append(held[3 * block : 3 * block + 8, :])
        rows.append(jnp.zeros((16, OWN), F32))
        value = fold(jnp.concatenate(rows, axis=0))
        if k % 2 == 0:
            mine = jnp.where(side == (k // 2), places[0], places[1])
            value = jnp.concatenate([value, mine], axis=0)
        out[k][...] = value.astype(BF)


def regroup(where, trio, feed_keep, feed_got, shard):
    small = (3 * shard + 24) // 2
    large = small + 5 * shard + 8
    return pl.pallas_call(
        partial(regroup_kernel, shard),
        out_shape=[shape((rows, 2 * OWN)) for rows in (large, small, large, small)],
        in_specs=[SMEM] + vmem(6),
        out_specs=vmem(LATS),
        scratch_shapes=[pltpu.VMEM((3 * LATS * shard + 16, OWN), F32)],
        compiler_params=params(),
        cost_estimate=cost(2),
        name="regroup",
    )(where, *trio, feed_keep, feed_got)


def settle_kernel(shard, where, got0, got1, got2, got3, w_query, gain, bias, *out):
    lat, side = where[0], where[2]
    mats, firsts, rest = out[-13:-7], out[-7:-5], out[-5:]
    got = [g[...].astype(F32) for g in (got0, got1, got2, got3)]
    small = got[1].shape[0]
    here, there = got[0][small:], got[2][small:]
    left, right = jnp.where(side == 0, here, there), jnp.where(side == 0, there, here)
    both = lambda a, b: jnp.concatenate([left[a:b], right[a:b]], axis=1)
    got = [unfold(g[:small]) for g in got]
    whole = jnp.concatenate([choose(lat ^ p, got) for p in range(LATS)], axis=1)
    part = lambda n: whole[n * shard : (n + 1) * shard]
    sums = whole[3 * shard : 3 * shard + 1] + whole[3 * shard + 1 : 3 * shard + 2]
    weight = w_query[...].astype(F32)
    lane = lax.broadcasted_iota(jnp.int32, (shard, shard), 1)
    line = lax.broadcasted_iota(jnp.int32, (shard, shard), 0)

    def column(ref):
        row = ref[...].astype(F32).reshape(1, shard)
        return jnp.sum(jnp.where(lane == line, row, 0.0), axis=1, keepdims=True)

    mats[0][...] = part(0) * column(gain) + column(bias) * sums
    mats[1][...] = part(1)
    mats[2][...] = part(2)
    mats[3][...] = both(0, shard)
    cols = [half[n * shard : (n + 1) * shard] for half in (left, right) for n in (1, 2)]
    mats[4][...] = jnp.concatenate(cols, axis=1)
    mats[5][...] = both(3 * shard, 5 * shard)
    firsts[0][...] = jnp.sum((part(0) * weight).T, axis=0)
    firsts[1][...] = jnp.sum((weight * sums).T, axis=0)
    line = here[5 * shard : 5 * shard + 1]
    for target, (first, count) in zip(rest, ((2, 1), (3, 1), (4, 1), (6, 2), (5, 1))):
        target[...] = line[:, first * shard : (first + count) * shard].reshape(count * shard)


def settle(where, got, w_query, gain, bias, after):
    shard, width = w_query.shape
    flat = shape((shard, width), F32)
    tall = shape((2 * shard, width), F32)
    wide = shape((shard, 2 * width), F32)
    return pl.pallas_call(
        partial(settle_kernel, shard),
        out_shape=[flat] * 4
        + [wide, tall]
        + [shape((n * shard,), F32) for n in (1, 1, 1, 1, 1, 2, 1)],
        in_specs=[SMEM] + vmem(7) + [ANY] * len(after),
        out_specs=vmem(13),
        compiler_params=params(),
        cost_estimate=cost(2),
        name="settle",
    )(where, *got, w_query, gain, bias, *after)


def place_rows(where, h, j):
    first = (where[0] ^ j) * OWN + h * HEAD_DIM
    return pl.ds(pl.multiple_of(first, HEAD_DIM), HEAD_DIM)


def first_grads_kernel(parts, where, rows_in, rays_in, middle_in, turned, *refs):
    msgs, (ray_grad, ray_half) = refs[:12], refs[-9:-7]
    rays, middle, weight, d_query, low, sem_in, sem_out = refs[-7:]
    half, width = rays.shape
    tail = d_query.shape[1]
    first_row = pl.multiple_of(where[1] * half, half)
    loads = []

    def load(source, target):
        loads.append(pltpu.make_async_copy(source, target, sem_in.at[len(loads)]))
        loads[-1].start()

    load(turned.at[:, 0], weight)
    for h in range(OWN_HEADS):
        for j in range(LATS):
            source = msgs[h * LATS + j]
            load(source.at[:, source.shape[1] - tail :], d_query.at[place_rows(where, h, j)])
    for first, last in parts:
        at = pl.ds(first, last - first)
        load(rays_in.at[pl.ds(first_row + first, last - first)], rays.at[at])
        load(middle_in.at[at], middle.at[at])
    for copy in loads[:13]:
        copy.wait()
    matrix = weight[...].reshape(width, width)
    stores = []
    for n, (first, last) in enumerate(parts):
        for copy in loads[13 + 2 * n : 15 + 2 * n]:
            copy.wait()
        at = slice(first, last)
        d_lifted = dot_lt(d_query[:, at], matrix)
        normed, factor = norm_parts(rays[at, :].astype(F32))
        back = norm_back(d_lifted, normed, factor, rows_in[0:1, :])
        low[at, :] = (middle[at, :].astype(F32) + back).astype(BF)
        source = low.at[pl.ds(first, last - first)]
        for target in (
            ray_half.at[pl.ds(first, last - first)],
            ray_grad.at[pl.ds(first_row + first, last - first)],
        ):
            stores.append(pltpu.make_async_copy(source, target, sem_out.at[len(stores)]))
            stores[-1].start()
    for copy in stores:
        copy.wait()


def first_grads(where, rays, turned, rows_in, d_middle, msgs, lat_rows, after):
    count, width = rays.shape
    half = count // 2
    parts = [(a, min(a + 256, half)) for a in range(0, half, 256)]
    tail = msgs[0][0].shape[1] - 2 * lat_rows
    return pl.pallas_call(
        partial(first_grads_kernel, parts),
        in_specs=[SMEM] + vmem(1) + [ANY] * (15 + len(after)),
        out_specs=[ANY] * 2,
        out_shape=[shape((count, width)), shape((half, width))],
        scratch_shapes=[
            pltpu.VMEM((half, width), BF),
            pltpu.VMEM((half, width), BF),
            pltpu.VMEM((LATS, OWN, width), BF),
            pltpu.VMEM((width, tail), BF),
            pltpu.VMEM((half, width), BF),
            pltpu.SemaphoreType.DMA((13 + 2 * len(parts),)),
            pltpu.SemaphoreType.DMA((2 * len(parts),)),
        ],
        compiler_params=params(),
        cost_estimate=cost(6),
        name="first_grads",
    )(where, rows_in, rays, d_middle, turned, *[m for group in msgs for m in group], *after)


def latent_kernel(where, turned, *refs):
    msgs, (out, weight, held, sem) = refs[:12], refs[-4:]
    _, width, lat_rows = held.shape
    loads = [[], []]
    for i in range(2):
        copies = [(turned.at[:, 1 + i], weight.at[i])]
        for h in range(OWN_HEADS):
            for j in range(LATS):
                source = msgs[h * LATS + j].at[:, i * lat_rows : (i + 1) * lat_rows]
                copies.append((source, held.at[i, place_rows(where, h, j)]))
        for source, target in copies:
            at = sem.at[i, len(loads[i])]
            loads[i].append(pltpu.make_async_copy(source, target, at))
            loads[i][-1].start()
    for copy in loads[0]:
        copy.wait()
    total = dot_lt(held[0], weight[0].reshape(width, width))
    for copy in loads[1]:
        copy.wait()
    total = total + dot_lt(held[1], weight[1].reshape(width, width))
    out[...] = total[: out.shape[0]].astype(BF)


def latent_grads(where, turned, msgs, rows, lat_rows, after):
    width = turned.shape[3]
    return pl.pallas_call(
        latent_kernel,
        in_specs=[SMEM] + [ANY] * (13 + len(after)),
        out_specs=pl.BlockSpec(memory_space=pltpu.VMEM),
        out_shape=shape((rows, width)),
        scratch_shapes=[
            pltpu.VMEM((2, LATS, OWN, width), BF),
            pltpu.VMEM((2, width, lat_rows), BF),
            pltpu.SemaphoreType.DMA((2, 13)),
        ],
        compiler_params=params(),
        cost_estimate=cost(6),
        name="latent_grads",
    )(where, turned, *msgs, *after)


def join(where, full, there):
    first = (1 - where[1]) * there.shape[0]
    return lax.dynamic_update_slice(full, there, (first, jnp.int32(0)))


def body(
    rays,
    latents,
    view_count,
    view_mask,
    cotangent,
    w_query,
    w_key,
    w_value,
    w_out,
    w_up,
    w_down,
    first_gain,
    first_bias,
    second_gain,
    second_bias,
    out_bias,
    up_bias,
    down_bias,
):
    scenes = lax.axis_size("scene")
    lat, scene = lax.axis_index("lat"), lax.axis_index("scene")
    core, side = lat % 2, lat // 2
    where = jnp.stack([lat, core, side, scene, scene % 2, scene // 2, scene // 4])
    where = where.astype(jnp.int32)
    count, width = rays.shape
    hidden = w_up.shape[1]
    lat_rows = latents.shape[0]
    lat_pad = -(-lat_rows // LANES) * LANES
    shard = w_query.shape[0]
    fine = shard % 8 == 0 and scenes == 8

    spot = jnp.arange(lat_pad, dtype=jnp.int32)
    block_of = lat ^ jnp.arange(LATS, dtype=jnp.int32)
    view_of = (block_of[:, None] * lat_rows + spot[None, :]) // VIEW_TOK
    matches = view_of[..., None] == jnp.arange(VIEWS, dtype=jnp.int32)
    listed = jnp.sum(jnp.where(matches, view_mask[0], 0), axis=-1) > 0
    live = listed & (view_of < view_count[0]) & (spot < lat_rows)[None, :]
    shut = jnp.where(live, 0.0, DEAD).astype(F32).reshape(LATS, 1, lat_pad)

    normed_low, *stats = make_norms(where, rays)
    vectors = [first_gain, first_bias, second_gain, second_bias, out_bias, down_bias, up_bias]
    (trio, turned, rows_in, up_shift), own_lat, passed = attention_weights(
        where, w_query, w_key, w_value, vectors, latents, lat_pad, [normed_low], [shut]
    )

    near_lat, far_lat = swap(own_lat, "lat", 1), swap(own_lat, "lat", 2)

    weights_in = feed_weights(w_out, w_up, w_down, passed)

    keyset = make_keyset(0, [own_lat, near_lat], trio, shut)
    query = make_queries(where, rays, *stats, trio, rows_in)
    far_lat = gate(far_lat, [query, keyset[0]])
    last_lat = swap(far_lat, "lat", 1)
    lats = [own_lat, near_lat, far_lat, last_lat]
    keyset = make_keyset(2, [far_lat], trio, shut, keyset)
    key, key_t, val, val_t = make_keyset(3, [last_lat], trio, shut, keyset)
    there_ctx, there_wide, weights, inverse = attend(1, query, key_t, val)
    near, far = swap(there_ctx, "lat", 1), swap(there_ctx, "lat", 3)
    here_ctx, here_wide, weights, inverse = attend(0, query, key_t, val, (weights, inverse))
    here_ctx = gate(here_ctx, [near, far])
    beside = swap(here_ctx, "lat", 2)
    if shard % 8 == 0:
        weights_in = assemble(weights_in, [here_ctx])
        beside = gate(beside, [weights_in[2]])
    ctxs = [here_ctx, near, beside, far]

    turned = lax.all_gather(gate(turned, ctxs[2:]), "lat", axis=0, tiled=False)
    layer_out, out_half, d_middle, d_own, d_sibling, *feed_out = feed(
        where, rays, ctxs, cotangent, weights_in, rows_in, up_shift, scenes, fine
    )
    d_there = swap(d_sibling, "lat", 1)
    out_there = swap(out_half, "lat", 1)
    layer_out = join(where, layer_out, out_there)
    if fine:
        own_msg, sib_msg = feed_out
        feed_send, feed_keep = halve(where, 0, own_msg, swap(sib_msg, "lat", 1))
        feed_got = swap(feed_send, "scene", 1)

    got, grads, after, got_own = [], [], [], ()
    for h in range(OWN_HEADS):
        if h == 1:
            after = after + [out_there] + ([feed_send] if fine else [])
        elif h == 2:
            after = after + got[0][1:]
            if fine:
                feed_keep = gate(feed_keep, after)
                feed_send, feed_keep = halve(where, 1, feed_keep, feed_got)
                feed_got = swap(feed_send, "scene", 4)
                after = after + [feed_send]
        out = attend_back(
            h,
            fine,
            weights,
            inverse,
            (d_own, d_there),
            (here_wide, there_wide),
            query,
            key,
            val_t,
            lats,
            normed_low,
            got_own,
            where,
            after,
        )
        if h == 2:
            out = gate(list(out), got[1][1:] + ([pair_got, feed_got] if fine else []))
        after = [out[0]]
        got_own = out[:LATS]
        grads += out[LATS:]
        if h == 1 and fine:
            pair_got = swap(grads[0], "scene", 1)
        got.append([out[0]] + [swap(out[k], "lat", k) for k in range(1, LATS)])
    after = []
    if fine:
        pairs = [(grads[1], pair_got), (grads[3], swap(grads[2], "scene", 1))]
        *late, feed_send, feed_keep = add_spread(where, pairs, feed_keep, feed_got, [layer_out])
        after = [late[0]]
        feed_got = swap(feed_send, "scene", 2)
        late = [late[0]] + [swap(late[k], "scene", 2 * k) for k in range(1, 4)]
    ray_grad, ray_half = first_grads(where, rays, turned, rows_in, d_middle, got, lat_pad, after)
    if fine:
        ray_half = gate(ray_half, late[1:] + [feed_got])
    ray_grad = join(where, ray_grad, swap(ray_half, "lat", 1))
    if fine:
        final = regroup(where, late, feed_keep, feed_got, shard)
        after = [final[0]]
    latent_grad = latent_grads(
        where, turned, [m for g in got for m in g], lat_rows, lat_pad, after
    )
    first = [first_gain, first_bias]
    if fine:
        final = [final[0]] + [swap(final[k], "lat", k) for k in range(1, LATS)]
        small = settle(where, final, w_query, *first, [latent_grad])
    else:
        joined = jnp.concatenate(grads, axis=1)
        grads = joined[: 3 * width].reshape(3, width, OWN), joined[3 * width :]
        first = [v.reshape(shard, 1).astype(F32) for v in first]
        small = plain_final(feed_out, grads, scenes, shard, w_query, *first)
    return (layer_out, ray_grad, latent_grad, *small)


def plain_final(feed_out, grads, scenes, shard, w_query, gain, bias):
    lat = lax.axis_index("lat")
    out_own, out_sib, up_own, up_sib, down_own, down_sib, sums, up_sums = feed_out
    trio, query_sums = grads

    def by_scene(out_part, up_part, down_part):
        parts = [
            out_part.reshape(scenes, -1, OWN),
            up_part.reshape(scenes, -1, 2, OWN).swapaxes(1, 2).reshape(scenes, -1, OWN),
            down_part.reshape(scenes, -1, OWN),
        ]
        return jnp.concatenate(parts, axis=1).astype(F32)

    feed_part = by_scene(out_own, up_own, down_own)
    feed_part = feed_part + swap(by_scene(out_sib, up_sib, down_sib), "lat", 1)
    feed_part = scatter_scene(feed_part)
    block = LATS * shard
    trio = trio.reshape(3, scenes, block, OWN).swapaxes(0, 1).reshape(scenes, 3 * block, OWN)
    lines = [v.reshape(scenes, LATS, shard) for v in sums[:4]]
    lines = [jnp.zeros_like(lines[0])] * 2 + lines + [up_sums[0].reshape(scenes, LATS, 2 * shard)]
    lines = jnp.concatenate(lines, axis=2)
    lines = jnp.pad(lines, ((0, 0), (0, 0), (0, OWN - 8 * shard)))
    cols = jnp.broadcast_to(query_sums[:2], (scenes, 2, OWN))
    late = scatter_scene(jnp.concatenate([trio.astype(F32), cols, lines], axis=1))
    mats = [late[i * block : (i + 1) * block].reshape(LATS, shard, OWN) for i in range(3)]
    mats += [feed_part[i * block : (i + 1) * block].reshape(LATS, shard, OWN) for i in range(3)]
    mats.append(feed_part[3 * block :].reshape(LATS, 2 * shard, OWN))
    mats.append(jnp.broadcast_to(late[3 * block : 3 * block + 2], (LATS, 2, OWN)))
    mats.append(late[3 * block + 2 :].reshape(LATS, 1, OWN))
    final = jnp.concatenate(mats, axis=1).astype(BF)
    sent = [lax.dynamic_index_in_dim(final, lat ^ k, 0, keepdims=False) for k in range(LATS)]
    got = [sent[0]] + [swap(sent[k], "lat", k) for k in range(1, LATS)]
    got = [g.astype(F32) for g in got]
    line = got[0][-1] + got[1][-1]
    cols = in_order(jnp.stack(got), list(range(LATS)), lat)
    joined = jnp.transpose(cols, (1, 0, 2)).reshape(cols.shape[1], -1)
    part = lambda n, count=1: joined[n * shard : (n + count) * shard]
    up = cols[:, 4 * shard : 6 * shard].reshape(LATS, 2, shard, OWN)
    up = jnp.transpose(up, (2, 0, 1, 3)).reshape(shard, -1)
    sums = joined[8 * shard : 8 * shard + 1] + joined[8 * shard + 1 : 8 * shard + 2]
    weight = w_query.astype(F32)
    piece = lambda i, n=1: line[i * shard : (i + n) * shard]
    return (
        part(0) * gain + bias * sums,
        part(1),
        part(2),
        part(3),
        up,
        part(6, 2),
        jnp.sum(part(0) * weight, axis=1),
        jnp.sum(weight * sums, axis=1),
        piece(2),
        piece(3),
        piece(4),
        piece(6, 2),
        piece(5),
    )


def solution(mesh):
    rows = P(("scene", "lat"), None)
    line = P(("scene", "lat"))
    scene = P("scene", None)
    in_specs = (scene, rows, P("scene"), scene, scene) + (rows,) * 6 + (line,) * 7
    out_specs = (scene, scene, rows) + (rows,) * 6 + (line,) * 7
    return jax.shard_map(body, mesh=mesh, in_specs=in_specs, out_specs=out_specs, check_vma=False)
```
